32 devices in a mesh: blk: 16 (over z, y, core), rep: 2 (over x).
Axes of the slice: x: 2, y: 2, z: 4, core: 2. Of those that a mesh axis runs over, the one named last changes fastest.
Arguments:
- features: bfloat16 [8192, 100], P(('blk', 'rep')), may hold values from -6 to 6
- node_order: int32 [16, 512], P('blk'), may hold values from 0 to 511, each once within a row
- tile_values: bfloat16 [32, 16, 256, 256], P(('blk', 'rep')), may hold values from 0 to 2, as said below
- tile_rows: int32 [32, 16], P(('blk', 'rep')), may hold values from 0 to 31, as said below
- tile_columns: int32 [32, 16], P(('blk', 'rep')), may hold values from 0 to 31, as said below
- tile_live: int32 [32], P(('blk', 'rep')), may hold values from 4 to 16, as said below
- first_weight: bfloat16 [100, 128], replicated, may hold values from -0.625 to 0.625
- first_bias: float32 [128], replicated, may hold values from -3 to 3
- second_weight: bfloat16 [128, 47], replicated, may hold values from -0.5 to 0.5
- second_bias: float32 [47], replicated, may hold values from -3 to 3
Outputs:
- logits: float32 [8192, 47], P(('blk', 'rep'))
The draws below stay inside these ranges and needn't reach their ends.
Inputs may be any that keep to these rules, and one draw needn't show every extreme that they name: `node_order`: each row is a permutation of 0 to 511. `tile_rows`: the slots of the device at blk index b name row blocks b * 2 to b * 2 + 1. `tile_columns`: the slots of the device at rep index r name column blocks p * 2 + r. `tile_live`: 16 on some devices in every draw. `tile_values`: nonnegative.
All inputs are finite; a program needn't handle non-finite values.
Results may differ from the reference program's by a relative error of at most 0.0015.
Values may be sent and summed in bfloat16 or wider, within the bound.
No kernel may reach another device: no remote copies, remote signals or barrier semaphores. Data moves between devices by JAX's collectives and lax.ppermute only.
A program may use at most 64 MiB of HBM per device.

```python
import jax
import jax.numpy as jnp
from jax import lax

F_IN = 100
HID = 128
CLS = 47
TILE = 256
TILES_DEV = 16
BLOCKS = 32
GROUP = 512
NODES = 8192
N_BLK = 16
N_REP = 2


def draw_tile_values(key, part):
    key = jax.random.fold_in(key, 17)
    chance = 4.0 / TILE
    uniform_draw = jax.random.uniform(key, (BLOCKS, TILES_DEV, TILE, TILE), jnp.float32)
    weights = 0.5 + uniform_draw / chance
    return jnp.where(uniform_draw < chance, weights, 0.0).astype(jnp.bfloat16)


def draw_tile_rows(key, part):
    key = jax.random.fold_in(key, 23)
    device = jnp.arange(BLOCKS, dtype=jnp.int32)[:, None]
    offsets = jax.random.randint(key, (BLOCKS, TILES_DEV), 0, N_REP, jnp.int32)
    return device // N_REP * N_REP + offsets


def draw_tile_columns(key, part):
    key = jax.random.fold_in(key, 31)
    near_key, far_key, pick_key = jax.random.split(key, 3)
    device = jnp.arange(BLOCKS, dtype=jnp.int32)[:, None]
    nearby = jax.random.randint(near_key, (BLOCKS, TILES_DEV), -2, 3, jnp.int32)
    anywhere = jax.random.randint(far_key, (BLOCKS, TILES_DEV), 0, N_BLK, jnp.int32)
    picked = jax.random.randint(pick_key, (BLOCKS, TILES_DEV), 0, 2, jnp.int32)
    panel = jnp.where(picked == 0, (device // N_REP + nearby) % N_BLK, anywhere)
    return panel * N_REP + device % N_REP


def draw_tile_live(key, part):
    key = jax.random.fold_in(key, 41)
    base_key, busy_key = jax.random.split(key)
    counts = jax.random.randint(base_key, (BLOCKS,), TILES_DEV // 4, TILES_DEV // 2 + 1, jnp.int32)
    busiest = jax.random.permutation(busy_key, BLOCKS)[:max(1, BLOCKS // 16)]
    return counts.at[busiest].set(TILES_DEV)


def steps_of(rng, extent, cuts, low, top_value):
    loudness = 1.0
    for position, blocks in cuts:
        steps = jax.random.uniform(jax.random.fold_in(jax.random.fold_in(rng, 6), position), (blocks,), jnp.float32, low / len(cuts), top_value / len(cuts))
        loudness = loudness * jnp.repeat(jnp.exp(steps), extent[position] // blocks).reshape((-1,) + (1,) * (len(extent) - 1 - position))
    return loudness


def normal_values(stream_key, dims, deviation, reach, pieces=(), kind=jnp.bfloat16):
    result = deviation * jax.random.normal(stream_key, dims, jnp.float32)
    if pieces:
        result = result * steps_of(stream_key, dims, pieces, -0.22, 0.18)
    return jnp.clip(result, -reach, reach).astype(kind)


def setup_inputs(seed: int = 0) -> dict:
    arg_keys = jax.random.split(jax.random.key(seed), 11)
    return {
        "features": normal_values(arg_keys[0], (NODES, F_IN), 1.0, 6.0, ((0, 32),)),
        "node_order": jax.vmap(lambda own: jax.random.permutation(own, GROUP))(jax.random.split(arg_keys[1], N_BLK)).reshape((N_BLK, GROUP)).astype(jnp.int32),
        "tile_values": draw_tile_values(jax.random.fold_in(arg_keys[10], 71), 0),
        "tile_rows": draw_tile_rows(jax.random.fold_in(arg_keys[10], 71), 0),
        "tile_columns": draw_tile_columns(jax.random.fold_in(arg_keys[10], 71), 0),
        "tile_live": draw_tile_live(jax.random.fold_in(arg_keys[10], 71), 0),
        "first_weight": normal_values(arg_keys[6], (F_IN, HID), F_IN ** -0.5, 0.625),
        "first_bias": normal_values(arg_keys[7], (HID,), 0.5, 3.0, (), jnp.float32),
        "second_weight": normal_values(arg_keys[8], (HID, CLS), HID ** -0.5, 0.5),
        "second_bias": normal_values(arg_keys[9], (CLS,), 0.5, 3.0, (), jnp.float32),
    }


def aggregate(tile_values, tile_rows, tile_columns, tile_live, panels):
    columns = panels.shape[1]

    def slot_step(slot_index, running):
        device = (slot_index // TILES_DEV).astype(jnp.int32)
        within = (slot_index % TILES_DEV).astype(jnp.int32)
        row_start = (tile_rows[device, within] * TILE).astype(jnp.int32)
        column_start = (tile_columns[device, within] * TILE).astype(jnp.int32)

        def add_tile(current):
            device_tiles = lax.dynamic_index_in_dim(tile_values, device, 0, False)
            tile_block = lax.dynamic_index_in_dim(device_tiles, within, 0, False)
            window = lax.dynamic_slice_in_dim(panels, column_start, TILE, 0)
            product = jnp.dot(tile_block, window, preferred_element_type=jnp.float32)
            existing = lax.dynamic_slice_in_dim(current, row_start, TILE, 0)
            return lax.dynamic_update_slice_in_dim(current, existing + product, row_start, 0)
        return lax.cond(within < tile_live[device], add_tile, lambda current: current, running)
    initial = jnp.zeros((NODES, columns), jnp.float32)
    return lax.fori_loop(0, BLOCKS * TILES_DEV, slot_step, initial)

def reference(features, node_order, tile_values, tile_rows, tile_columns, tile_live, first_weight, first_bias, second_weight, second_bias):
    grouped = features.reshape(N_BLK, GROUP, F_IN)
    ordered = jnp.take_along_axis(grouped, node_order[:, :, None], axis=1).reshape(NODES, F_IN)
    hidden_in = jnp.dot(ordered, first_weight, preferred_element_type=jnp.float32).astype(jnp.bfloat16)
    degree = aggregate(tile_values, tile_rows, tile_columns, tile_live, jnp.ones((NODES, 1), jnp.bfloat16))[:, 0]
    scaling = lax.rsqrt(1.0 + degree)[:, None]
    summed = aggregate(tile_values, tile_rows, tile_columns, tile_live, hidden_in)
    hidden_out = jax.nn.relu(scaling * (summed + hidden_in.astype(jnp.float32)) + first_bias).astype(jnp.bfloat16)
    classes_in = jnp.dot(hidden_out, second_weight, preferred_element_type=jnp.float32).astype(jnp.bfloat16)
    summed_second = aggregate(tile_values, tile_rows, tile_columns, tile_live, classes_in)
    return scaling * (summed_second + classes_in.astype(jnp.float32)) + second_bias
```

```python
import functools

import jax
import jax.numpy as jnp
from jax import lax
from jax.experimental import pallas as pl
from jax.experimental.pallas import tpu as pltpu
from jax.sharding import PartitionSpec as P

BF16 = jnp.bfloat16
F32 = jnp.float32
ONES_ROWS = 16
VMEM_LIMIT = 32 * 1024 * 1024


def nn(a, b):
    return lax.dot_general(a, b, (((1,), (0,)), ((), ())), preferred_element_type=F32)


def nt(a, b):
    return lax.dot_general(a, b, (((1,), (1,)), ((), ())), preferred_element_type=F32)


def call(kernel, outs, n_smem, n_vmem):
    return pl.pallas_call(
        kernel,
        out_shape=outs,
        in_specs=[pl.BlockSpec(memory_space=pltpu.SMEM)] * n_smem
        + [pl.BlockSpec(memory_space=pltpu.VMEM)] * n_vmem,
        compiler_params=pltpu.CompilerParams(vmem_limit_bytes=VMEM_LIMIT),
    )


def order_project(ids, order, weight_t, *rest):
    *features, out = rest
    reps = len(features)
    tile = features[0].shape[1]
    member = ids[1]
    wanted = order[:, pl.ds(pl.multiple_of(member * tile, tile), tile)]
    total = jnp.zeros(out.shape, F32)
    for step in range(reps):
        owner = lax.rem(member + step, reps)
        hidden = nn(weight_t[...], features[step][...]).astype(BF16)
        source = lax.broadcasted_iota(jnp.int32, (tile, tile), 0) + owner * tile
        pick = jnp.where(source == wanted, 1.0, 0.0).astype(BF16)
        total = total + nn(hidden, pick)
    out[...] = total.astype(BF16)


def aggregate(reps, count_rows, ids, live, rows, columns, tiles, near, far, *outs):
    slots, tile = tiles.shape[0], tiles.shape[1]
    height = near.shape[1]
    half = near.shape[0]
    outer = half // 2
    block, member = ids[0], ids[1]
    my_outer, my_inner, my_core = block // 4, (block // 2) % 2, block % 2
    extra = ONES_ROWS if count_rows else 0
    total = jnp.zeros((reps * (height + extra), tile), F32)
    for slot in range(slots):
        panel = lax.clamp(0, columns[0, slot] // reps, 2 * half - 1)
        d_outer = lax.rem(panel // 4 - my_outer + outer, outer)
        d_inner = lax.rem((panel // 2) % 2 + my_inner, 2)
        d_core = lax.rem(panel % 2 + my_core, 2)
        place = d_inner * outer + d_outer
        values = jnp.where(d_core == 0, near[place], far[place])
        local = rows[0, slot] - block * reps
        pieces = []
        for step in range(reps):
            wanted = lax.rem(member + step, reps)
            used = ((local == wanted) & (slot < live[0])).astype(F32)
            pieces.append(values * used.astype(BF16))
            if extra:
                pieces.append(jnp.full((extra, tile), used, F32).astype(BF16))
        total = total + nt(jnp.concatenate(pieces, axis=0), tiles[slot])
    for step in range(reps):
        start = step * (height + extra)
        outs[step][...] = total[start : start + outs[step].shape[0]]


def combine(reps, hidden_in, bias, weight_t, own, *rest):
    arrived, (out, scale_out) = rest[: reps - 1], rest[reps - 1 :]
    height = hidden_in.shape[0]
    total = own[...]
    for part in arrived:
        total = total + part[...]
    scaling = lax.rsqrt(1.0 + total[height : height + 1])
    hidden = scaling * (total[:height] + hidden_in[...].astype(F32)) + bias[...]
    hidden = jnp.maximum(hidden, 0.0).astype(BF16)
    classes = nn(weight_t[...], hidden).astype(BF16)
    out[: classes.shape[0]] = classes
    scale_out[...] = scaling


def finish(reps, classes_in, scaling, bias, own, *rest):
    arrived, out = rest[: reps - 1], rest[reps - 1]
    total = own[...]
    for part in arrived:
        total = total + part[...]
    classes = out.shape[0]
    whole = total + classes_in[...].astype(F32)
    out[...] = scaling[...] * whole[:classes] + bias[...]


def shifted(value, axis, step):
    size = lax.axis_size(axis)
    return lax.ppermute(value, axis, [((d + step) % size, d) for d in range(size)])


def gather_blocks(value):
    size = lax.axis_size("blk")
    outer = size // 4
    along = [value]
    for step in range(1, outer):
        along.append(lax.ppermute(value, "blk", [((d + 4 * step) % size, d) for d in range(size)]))
    column = jnp.stack(along)
    across = lax.ppermute(column, "blk", [(d ^ 2, d) for d in range(size)])
    near = jnp.concatenate([column, across])
    far = lax.ppermute(near, "blk", [(d ^ 1, d) for d in range(size)])
    return near, far


def body(
    features,
    node_order,
    tile_values,
    tile_rows,
    tile_columns,
    tile_live,
    first_weight,
    first_bias,
    second_weight,
    second_bias,
):
    tile = features.shape[0]
    reps = lax.axis_size("rep")
    hidden, classes = second_weight.shape
    padded = -(-classes // 16) * 16
    ids = jnp.stack([lax.axis_index("blk"), lax.axis_index("rep")]).astype(jnp.int32)
    tiles = tile_values[0]

    own_t = features.T
    parts = [own_t] + [shifted(own_t, "rep", step) for step in range(1, reps)]
    hidden_in = call(
        order_project, jax.ShapeDtypeStruct((hidden, tile), BF16), 1, 2 + reps
    )(ids, node_order, first_weight.T, *parts)

    near, far = gather_blocks(hidden_in)
    sums = call(
        functools.partial(aggregate, reps, True),
        [jax.ShapeDtypeStruct((hidden + 8, tile), F32)] * reps,
        4,
        3,
    )(ids, tile_live, tile_rows, tile_columns, tiles, near, far)
    arrived = [shifted(sums[reps - step], "rep", step) for step in range(1, reps)]
    classes_in, scaling = call(
        functools.partial(combine, reps),
        [jax.ShapeDtypeStruct((padded, tile), BF16), jax.ShapeDtypeStruct((1, tile), F32)],
        0,
        4 + reps - 1,
    )(
        hidden_in,
        first_bias[:, None],
        jnp.pad(second_weight.T, ((0, padded - classes), (0, 0))),
        sums[0],
        *arrived,
    )

    near, far = gather_blocks(classes_in)
    sums = call(
        functools.partial(aggregate, reps, False),
        [jax.ShapeDtypeStruct((padded, tile), F32)] * reps,
        4,
        3,
    )(ids, tile_live, tile_rows, tile_columns, tiles, near, far)
    arrived = [shifted(sums[reps - step], "rep", step) for step in range(1, reps)]
    logits = call(
        functools.partial(finish, reps),
        jax.ShapeDtypeStruct((classes, tile), F32),
        0,
        4 + reps - 1,
    )(classes_in, scaling, second_bias[:, None], sums[0], *arrived)
    return logits.T


def solution(mesh):
    placed = (
        P(("blk", "rep"), None),
        P("blk", None),
        P(("blk", "rep"), None, None, None),
        P(("blk", "rep"), None),
        P(("blk", "rep"), None),
        P(("blk", "rep")),
        P(),
        P(),
        P(),
        P(),
    )
    return jax.shard_map(
        body, mesh=mesh, in_specs=placed, out_specs=P(("blk", "rep"), None), check_vma=False
    )
```

```python
import functools

import jax
import jax.numpy as jnp
from jax import lax
from jax.experimental import pallas as pl
from jax.experimental.pallas import tpu as pltpu
from jax.sharding import PartitionSpec as P

BF16 = jnp.bfloat16
F32 = jnp.float32
ONES_ROWS = 16
VMEM_LIMIT = 32 * 1024 * 1024


def nn(a, b):
    return lax.dot_general(a, b, (((1,), (0,)), ((), ())), preferred_element_type=F32)


def nt(a, b):
    return lax.dot_general(a, b, (((1,), (1,)), ((), ())), preferred_element_type=F32)


def call(kernel, outs, n_smem, n_vmem, n_hbm=0, scratch=(), flops=0):
    return pl.pallas_call(
        kernel,
        out_shape=outs,
        in_specs=[pl.BlockSpec(memory_space=pltpu.SMEM)] * n_smem
        + [pl.BlockSpec(memory_space=pltpu.VMEM)] * n_vmem
        + [pl.BlockSpec(memory_space=pltpu.HBM)] * n_hbm,
        scratch_shapes=scratch,
        compiler_params=pltpu.CompilerParams(vmem_limit_bytes=VMEM_LIMIT),
        cost_estimate=pl.CostEstimate(flops=flops, bytes_accessed=1 << 20, transcendentals=0),
    )


def in_hbm(value):
    return pltpu.with_memory_space_constraint(value, pltpu.HBM)


def picked(weight_t, features, wanted, owner):
    tile = features.shape[1]
    hidden = nn(weight_t[...], features[...]).astype(BF16)
    source = lax.broadcasted_iota(jnp.int32, (tile, tile), 0) + owner * tile
    return nn(hidden, jnp.where(source == wanted, 1.0, 0.0).astype(BF16))


def prepare(plan, weight_t, order, features, tiles, *rest):
    part, wanted_out, weight_out, tiles_out, order_in, features_in, sems = rest
    fetches = [
        pltpu.make_async_copy(order, order_in, sems.at[0]),
        pltpu.make_async_copy(features, features_in, sems.at[1]),
        pltpu.make_async_copy(tiles, tiles_out, sems.at[2]),
    ]
    for fetch in fetches:
        fetch.start()
    weight_out[...] = weight_t[...]
    fetches[0].wait()
    fetches[1].wait()
    tile = features.shape[1]
    member = plan[1]
    wanted = order_in[:, pl.ds(pl.multiple_of(member * tile, tile), tile)]
    wanted_out[...] = wanted
    part[...] = picked(weight_t, features_in, wanted, member).astype(BF16)
    fetches[2].wait()


def order_project(plan, part, wanted, weight_t, *rest):
    *features, out = rest
    reps = len(features) + 1
    total = part[...].astype(F32)
    for step in range(1, reps):
        owner = lax.rem(plan[1] + step, reps)
        total = total + picked(weight_t, features[step - 1], wanted[...], owner)
    out[...] = total.astype(BF16)


def aggregate(reps, count_rows, plan, tiles, near, far, *outs):
    slots, tile = tiles.shape[0], tiles.shape[1]
    height = near.shape[1]
    half = near.shape[0]
    block, member, live = plan[0], plan[1], plan[2]
    extra = ONES_ROWS if count_rows else 0
    total = jnp.zeros((reps * (height + extra), tile), F32)
    for slot in range(slots):
        panel = lax.clamp(0, plan[3 + slots + slot] // reps, 2 * half - 1)
        place = panel // 2
        values = jnp.where(panel % 2 == block % 2, near[place], far[place])
        local = plan[3 + slot] - block * reps
        pieces = []
        for step in range(reps):
            wanted = lax.rem(member + step, reps)
            used = ((local == wanted) & (slot < live)).astype(F32)
            pieces.append(values * used.astype(BF16))
            if extra:
                pieces.append(jnp.full((extra, tile), used, F32).astype(BF16))
        total = total + nt(jnp.concatenate(pieces, axis=0), tiles[slot])
    for step in range(reps):
        start = step * (height + extra)
        outs[step][...] = total[start : start + outs[step].shape[0]]


def combine(reps, hidden_in, bias, weight_t, own, *rest):
    arrived, (out, scale_out) = rest[: reps - 1], rest[reps - 1 :]
    height = hidden_in.shape[0]
    total = own[...]
    for part in arrived:
        total = total + part[...]
    scaling = lax.rsqrt(1.0 + total[height : height + 1])
    hidden = scaling * (total[:height] + hidden_in[...].astype(F32)) + bias[...]
    hidden = jnp.maximum(hidden, 0.0).astype(BF16)
    classes = nn(weight_t[...], hidden).astype(BF16)
    out[: classes.shape[0]] = classes
    scale_out[...] = scaling


def finish(reps, classes_in, scaling, bias, own, *rest):
    arrived, out = rest[: reps - 1], rest[reps - 1]
    total = own[...]
    for part in arrived:
        total = total + part[...]
    classes = out.shape[0]
    whole = total + classes_in[...].astype(F32)
    out[...] = scaling[...] * whole[:classes] + bias[...]


def shifted(value, axis, step):
    size = lax.axis_size(axis)
    return lax.ppermute(value, axis, [((d + step) % size, d) for d in range(size)])


def gather_blocks(value):
    size = lax.axis_size("blk")
    groups = [list(range(core, size, 2)) for core in range(2)]
    copies = jnp.broadcast_to(value[None], (size // 2, *value.shape))
    near = lax.all_to_all(copies, "blk", 0, 0, axis_index_groups=groups)
    far = lax.ppermute(near, "blk", [(d ^ 1, d) for d in range(size)])
    return near, far


def body(
    features,
    node_order,
    tile_values,
    tile_rows,
    tile_columns,
    tile_live,
    first_weight,
    first_bias,
    second_weight,
    second_bias,
):
    tile = features.shape[0]
    reps = lax.axis_size("rep")
    hidden, classes = second_weight.shape
    padded = -(-classes // 16) * 16
    ids = [lax.axis_index("blk"), lax.axis_index("rep")]
    plan = jnp.concatenate(
        [jnp.stack(ids).astype(jnp.int32), tile_live, tile_rows[0], tile_columns[0]]
    )
    shape = jax.ShapeDtypeStruct

    own_t = features.T
    others = [shifted(own_t, "rep", step) for step in range(1, reps)]
    part, wanted, weight_t, tiles = call(
        prepare,
        [
            shape((hidden, tile), BF16),
            shape((1, tile), jnp.int32),
            shape(first_weight.shape[::-1], BF16),
            shape(tile_values.shape[1:], BF16),
        ],
        1,
        1,
        3,
        [
            pltpu.VMEM(node_order.shape, jnp.int32),
            pltpu.VMEM(own_t.shape, BF16),
            pltpu.SemaphoreType.DMA((3,)),
        ],
        1 << 28,
    )(plan, first_weight.T, *map(in_hbm, (node_order, own_t, tile_values[0])))
    hidden_in = call(order_project, shape((hidden, tile), BF16), 1, 3 + reps - 1)(
        plan, part, wanted, weight_t, *others
    )

    near, far = gather_blocks(hidden_in)
    sums = call(
        functools.partial(aggregate, reps, True),
        [shape((hidden + 8, tile), F32)] * reps,
        1,
        3,
    )(plan, tiles, near, far)
    arrived = [shifted(sums[reps - step], "rep", step) for step in range(1, reps)]
    classes_in, scaling = call(
        functools.partial(combine, reps),
        [shape((padded, tile), BF16), shape((1, tile), F32)],
        0,
        4 + reps - 1,
    )(
        hidden_in,
        first_bias[:, None],
        jnp.pad(second_weight.T, ((0, padded - classes), (0, 0))),
        sums[0],
        *arrived,
    )

    near, far = gather_blocks(classes_in)
    sums = call(
        functools.partial(aggregate, reps, False),
        [shape((padded, tile), F32)] * reps,
        1,
        3,
    )(plan, tiles, near, far)
    arrived = [shifted(sums[reps - step], "rep", step) for step in range(1, reps)]
    logits = call(
        functools.partial(finish, reps),
        shape((classes, tile), F32),
        0,
        4 + reps - 1,
    )(classes_in, scaling, second_bias[:, None], sums[0], *arrived)
    return logits.T


def solution(mesh):
    placed = (
        P(("blk", "rep"), None),
        P("blk", None),
        P(("blk", "rep"), None, None, None),
        P(("blk", "rep"), None),
        P(("blk", "rep"), None),
        P(("blk", "rep")),
        P(),
        P(),
        P(),
        P(),
    )
    return jax.shard_map(
        body, mesh=mesh, in_specs=placed, out_specs=P(("blk", "rep"), None), check_vma=False
    )
```

```python
import functools

import jax
import jax.numpy as jnp
from jax import lax
from jax.experimental import pallas as pl
from jax.experimental.pallas import tpu as pltpu
from jax.sharding import PartitionSpec as P

BF16 = jnp.bfloat16
F32 = jnp.float32
ONES_ROWS = 16
VMEM_LIMIT = 32 * 1024 * 1024


def nn(a, b):
    return lax.dot_general(a, b, (((1,), (0,)), ((), ())), preferred_element_type=F32)


def nt(a, b):
    return lax.dot_general(a, b, (((1,), (1,)), ((), ())), preferred_element_type=F32)


def tn(a, b):
    return lax.dot_general(a, b, (((0,), (0,)), ((), ())), preferred_element_type=F32)


def call(kernel, outs, n_smem, n_vmem, n_hbm=0, scratch=(), cost=1 << 20):
    return pl.pallas_call(
        kernel,
        out_shape=outs,
        in_specs=[pl.BlockSpec(memory_space=pltpu.SMEM)] * n_smem
        + [pl.BlockSpec(memory_space=pltpu.VMEM)] * n_vmem
        + [pl.BlockSpec(memory_space=pltpu.HBM)] * n_hbm,
        scratch_shapes=scratch,
        compiler_params=pltpu.CompilerParams(vmem_limit_bytes=VMEM_LIMIT),
        cost_estimate=pl.CostEstimate(flops=cost, bytes_accessed=cost, transcendentals=0),
    )


def in_hbm(value):
    return pltpu.with_memory_space_constraint(value, pltpu.HBM)


def picked(weight_t, features, wanted, owner):
    tile = features.shape[1]
    hidden = nn(weight_t, features[...]).astype(BF16)
    source = lax.broadcasted_iota(jnp.int32, (tile, tile), 0) + owner * tile
    return nn(hidden, jnp.where(source == wanted, 1.0, 0.0).astype(BF16))


def prepare(order, features, weight, part, wanted_out, weight_out, *rest):
    order_in, features_in, weight_in, sems = rest
    fetches = [
        pltpu.make_async_copy(order, order_in, sems.at[0]),
        pltpu.make_async_copy(weight, weight_in, sems.at[1]),
        pltpu.make_async_copy(features, features_in, sems.at[2]),
    ]
    for fetch in fetches:
        fetch.start()
    for fetch in fetches:
        fetch.wait()
    tile = features.shape[1]
    member = lax.axis_index("rep")
    wanted = order_in[:, pl.ds(pl.multiple_of(member * tile, tile), tile)]
    wanted_out[...] = wanted
    weight_t = weight_in[...].astype(F32).T.astype(BF16)
    weight_out[...] = weight_t
    part[...] = picked(weight_t, features_in, wanted, member).astype(BF16)


def fetch_tiles(tiles, out, sem):
    fetch = pltpu.make_async_copy(tiles, out, sem)
    fetch.start()
    fetch.wait()


def order_project(part, wanted, weight_t, *rest):
    *features, out = rest
    reps = len(features) + 1
    member = lax.axis_index("rep")
    total = part[...].astype(F32)
    for step in range(1, reps):
        owner = lax.rem(member + step, reps)
        total = total + picked(weight_t[...], features[step - 1], wanted[...], owner)
    out[...] = total.astype(BF16)


def aggregate(reps, first, count_rows, plan, tiles, near, far, *outs):
    slots, tile = tiles.shape[0], tiles.shape[1]
    height = near.shape[1]
    half = near.shape[0]
    block, member, live = plan[0], plan[1], plan[2]
    extra = ONES_ROWS if count_rows else 0
    total = jnp.zeros((len(outs) * (height + extra), tile), F32)
    for slot in range(slots):
        panel = lax.clamp(0, plan[3 + slots + slot] // reps, 2 * half - 1)
        place = (panel // 2) ^ (block // 2)
        values = jnp.where(panel % 2 == block % 2, near[place], far[place])
        local = plan[3 + slot] - block * reps
        pieces = []
        for step in range(len(outs)):
            wanted = lax.rem(member + first + step, reps)
            used = ((local == wanted) & (slot < live)).astype(F32)
            pieces.append(values * used.astype(BF16))
            if extra:
                pieces.append(jnp.full((extra, tile), used, F32).astype(BF16))
        total = total + nt(jnp.concatenate(pieces, axis=0), tiles[slot])
    for step, out in enumerate(outs):
        start = step * (height + extra)
        out[...] = total[start : start + out.shape[0]]


def combine(reps, hidden_in, bias, weight_t, own, *rest):
    arrived, (out, scale_out) = rest[: reps - 1], rest[reps - 1 :]
    height = hidden_in.shape[0]
    total = own[...]
    for part in arrived:
        total = total + part[...]
    scaling = lax.rsqrt(1.0 + total[height : height + 1])
    hidden = scaling * (total[:height] + hidden_in[...].astype(F32)) + bias[...]
    hidden = jnp.maximum(hidden, 0.0).astype(BF16)
    out[...] = nn(weight_t[...], hidden).astype(BF16)
    scale_out[...] = scaling


def finish(reps, classes_in, scaling, bias, own, *rest):
    arrived, out = rest[: reps - 1], rest[reps - 1]
    total = own[...]
    for part in arrived:
        total = total + part[...]
    classes = out.shape[0]
    whole = total + classes_in[...].astype(F32)
    out[...] = scaling[...] * whole[:classes] + bias[...]


def shifted(value, axis, step):
    size = lax.axis_size(axis)
    return lax.ppermute(value, axis, [((d + step) % size, d) for d in range(size)])


def swapped(value, mask):
    return lax.ppermute(value, "blk", [(d ^ mask, d) for d in range(lax.axis_size("blk"))])


def gather_blocks(value):
    chips = lax.axis_size("blk") // 2
    parts = {0: value}
    for step in range(2, chips, 2):
        parts[step] = swapped(value, 2 * step)
    for step in range(0, chips, 2):
        parts[step + 1] = swapped(parts[step], 2)
    near = jnp.stack([parts[step] for step in range(chips)])
    return near, swapped(near, 1)


def body(
    features,
    node_order,
    tile_values,
    tile_rows,
    tile_columns,
    tile_live,
    first_weight,
    first_bias,
    second_weight,
    second_bias,
):
    tile = features.shape[0]
    reps = lax.axis_size("rep")
    hidden, classes = second_weight.shape
    padded = -(-classes // 16) * 16
    shape = jax.ShapeDtypeStruct
    ids = [lax.axis_index("blk"), lax.axis_index("rep")]
    plan = jnp.concatenate(
        [jnp.stack(ids).astype(jnp.int32), tile_live, tile_rows[0], tile_columns[0]]
    )

    def aggregated(near, far, tiles, rows, count_rows):
        others = call(
            functools.partial(aggregate, reps, 1, count_rows),
            [shape((rows, tile), F32)] * (reps - 1),
            1,
            3,
        )(plan, tiles, near, far)
        arrived = [shifted(others[reps - 1 - step], "rep", step) for step in range(1, reps)]
        own = call(
            functools.partial(aggregate, reps, 0, count_rows), [shape((rows, tile), F32)], 1, 3
        )(plan, tiles, near, far)
        return [*own, *arrived]

    own_t = features.T
    others = [shifted(own_t, "rep", step) for step in range(1, reps)]
    part, wanted, weight_t = call(
        prepare,
        [
            shape((hidden, tile), BF16),
            shape((1, tile), jnp.int32),
            shape(first_weight.shape[::-1], BF16),
        ],
        0,
        0,
        3,
        [
            pltpu.VMEM(node_order.shape, jnp.int32),
            pltpu.VMEM(own_t.shape, BF16),
            pltpu.VMEM(first_weight.shape, BF16),
            pltpu.SemaphoreType.DMA((3,)),
        ],
    )(*map(in_hbm, (node_order, own_t, first_weight)))
    hidden_in = call(order_project, shape((hidden, tile), BF16), 0, 3 + reps - 1)(
        part, wanted, weight_t, *others
    )

    tiles = call(
        fetch_tiles,
        shape(tile_values.shape[1:], BF16),
        0,
        0,
        1,
        [pltpu.SemaphoreType.DMA],
    )(in_hbm(tile_values[0]))
    sums = aggregated(*gather_blocks(hidden_in), tiles, hidden + 8, True)
    classes_in, scaling = call(
        functools.partial(combine, reps),
        [shape((padded, tile), BF16), shape((1, tile), F32)],
        0,
        3 + reps,
    )(
        hidden_in,
        first_bias[:, None],
        jnp.pad(second_weight.T, ((0, padded - classes), (0, 0))),
        *sums,
    )

    sums = aggregated(*gather_blocks(classes_in), tiles, padded, False)
    logits = call(functools.partial(finish, reps), shape((classes, tile), F32), 0, 3 + reps)(
        classes_in, scaling, second_bias[:, None], *sums
    )
    return logits.T


def solution(mesh):
    placed = (
        P(("blk", "rep"), None),
        P("blk", None),
        P(("blk", "rep"), None, None, None),
        P(("blk", "rep"), None),
        P(("blk", "rep"), None),
        P(("blk", "rep")),
        P(),
        P(),
        P(),
        P(),
    )
    return jax.shard_map(
        body, mesh=mesh, in_specs=placed, out_specs=P(("blk", "rep"), None), check_vma=False
    )
```

```python
import functools

import jax
import jax.numpy as jnp
from jax import lax
from jax.experimental import pallas as pl
from jax.experimental.pallas import tpu as pltpu
from jax.sharding import PartitionSpec as P

BF16 = jnp.bfloat16
F32 = jnp.float32
ONES_ROWS = 16
VMEM_LIMIT = 32 * 1024 * 1024


def nn(a, b):
    return lax.dot_general(a, b, (((1,), (0,)), ((), ())), preferred_element_type=F32)


def nt(a, b):
    return lax.dot_general(a, b, (((1,), (1,)), ((), ())), preferred_element_type=F32)


def tn(a, b):
    return lax.dot_general(a, b, (((0,), (0,)), ((), ())), preferred_element_type=F32)


def call(kernel, outs, n_smem, n_vmem, n_hbm=0, scratch=(), cost=1 << 20):
    return pl.pallas_call(
        kernel,
        out_shape=outs,
        in_specs=[pl.BlockSpec(memory_space=pltpu.SMEM)] * n_smem
        + [pl.BlockSpec(memory_space=pltpu.VMEM)] * n_vmem
        + [pl.BlockSpec(memory_space=pltpu.HBM)] * n_hbm,
        scratch_shapes=scratch,
        compiler_params=pltpu.CompilerParams(vmem_limit_bytes=VMEM_LIMIT),
        cost_estimate=pl.CostEstimate(flops=cost, bytes_accessed=cost, transcendentals=0),
    )


def in_hbm(value):
    return pltpu.with_memory_space_constraint(value, pltpu.HBM)


def picked(weight_t, features, wanted, owner):
    tile = features.shape[1]
    hidden = nn(weight_t, features[...]).astype(BF16)
    source = lax.broadcasted_iota(jnp.int32, (tile, tile), 0) + owner * tile
    return nn(hidden, jnp.where(source == wanted, 1.0, 0.0).astype(BF16))


def prepare(order, features, weight, part, wanted_out, weight_out, *rest):
    order_in, features_in, weight_in, sems = rest
    fetches = [
        pltpu.make_async_copy(order, order_in, sems.at[0]),
        pltpu.make_async_copy(weight, weight_in, sems.at[1]),
        pltpu.make_async_copy(features, features_in, sems.at[2]),
    ]
    for fetch in fetches:
        fetch.start()
    for fetch in fetches:
        fetch.wait()
    tile = features.shape[1]
    member = lax.axis_index("rep")
    wanted = order_in[:, pl.ds(pl.multiple_of(member * tile, tile), tile)]
    wanted_out[...] = wanted
    weight_t = weight_in[...].astype(F32).T.astype(BF16)
    weight_out[...] = weight_t
    part[...] = picked(weight_t, features_in, wanted, member).astype(BF16)


def fetch_tiles(tiles, out, sem):
    fetch = pltpu.make_async_copy(tiles, out, sem)
    fetch.start()
    fetch.wait()


def order_project(part, wanted, weight_t, *rest):
    *features, out = rest
    reps = len(features) + 1
    member = lax.axis_index("rep")
    total = part[...].astype(F32)
    for step in range(1, reps):
        owner = lax.rem(member + step, reps)
        total = total + picked(weight_t[...], features[step - 1], wanted[...], owner)
    out[...] = total.astype(BF16)


def aggregate(reps, first, count_rows, plan, tiles, near, far, *outs):
    slots, tile = tiles.shape[0], tiles.shape[1]
    height = near.shape[1]
    half = near.shape[0]
    block, member, live = plan[0], plan[1], plan[2]
    extra = ONES_ROWS if count_rows else 0
    total = jnp.zeros((len(outs) * (height + extra), tile), F32)
    for slot in range(slots):
        panel = lax.clamp(0, plan[3 + slots + slot] // reps, 2 * half - 1)
        place = panel // 2
        values = jnp.where(panel % 2 == block % 2, near[place], far[place])
        local = plan[3 + slot] - block * reps
        pieces = []
        for step in range(len(outs)):
            wanted = lax.rem(member + first + step, reps)
            used = ((local == wanted) & (slot < live)).astype(F32)
            pieces.append(values * used.astype(BF16))
            if extra:
                pieces.append(jnp.full((extra, tile), used, F32).astype(BF16))
        total = total + nt(jnp.concatenate(pieces, axis=0), tiles[slot])
    for step, out in enumerate(outs):
        start = step * (height + extra)
        out[...] = total[start : start + out.shape[0]]


def combine(reps, hidden_in, bias, weight_t, own, *rest):
    arrived, (out, scale_out) = rest[: reps - 1], rest[reps - 1 :]
    height = hidden_in.shape[0]
    total = own[...]
    for part in arrived:
        total = total + part[...]
    scaling = lax.rsqrt(1.0 + total[height : height + 1])
    hidden = scaling * (total[:height] + hidden_in[...].astype(F32)) + bias[...]
    hidden = jnp.maximum(hidden, 0.0).astype(BF16)
    out[...] = nn(weight_t[...], hidden).astype(BF16)
    scale_out[...] = scaling


def finish(reps, classes_in, scaling, bias, own, *rest):
    arrived, out = rest[: reps - 1], rest[reps - 1]
    total = own[...]
    for part in arrived:
        total = total + part[...]
    classes = out.shape[0]
    whole = total + classes_in[...].astype(F32)
    out[...] = scaling[...] * whole[:classes] + bias[...]


def shifted(value, axis, step):
    size = lax.axis_size(axis)
    return lax.ppermute(value, axis, [((d + step) % size, d) for d in range(size)])


def swapped(value, mask):
    return lax.ppermute(value, "blk", [(d ^ mask, d) for d in range(lax.axis_size("blk"))])


def gather_blocks(value):
    size = lax.axis_size("blk")
    groups = [list(range(core, size, 2)) for core in range(2)]
    near = lax.all_gather(value, "blk", axis_index_groups=groups)
    return near, swapped(near, 1)


def body(
    features,
    node_order,
    tile_values,
    tile_rows,
    tile_columns,
    tile_live,
    first_weight,
    first_bias,
    second_weight,
    second_bias,
):
    tile = features.shape[0]
    reps = lax.axis_size("rep")
    hidden, classes = second_weight.shape
    padded = -(-classes // 16) * 16
    shape = jax.ShapeDtypeStruct
    ids = [lax.axis_index("blk"), lax.axis_index("rep")]
    plan = jnp.concatenate(
        [jnp.stack(ids).astype(jnp.int32), tile_live, tile_rows[0], tile_columns[0]]
    )

    def aggregated(near, far, tiles, rows, count_rows):
        others = call(
            functools.partial(aggregate, reps, 1, count_rows),
            [shape((rows, tile), F32)] * (reps - 1),
            1,
            3,
        )(plan, tiles, near, far)
        arrived = [shifted(others[reps - 1 - step], "rep", step) for step in range(1, reps)]
        own = call(
            functools.partial(aggregate, reps, 0, count_rows), [shape((rows, tile), F32)], 1, 3
        )(plan, tiles, near, far)
        return [*own, *arrived]

    own_t = features.T
    others = [shifted(own_t, "rep", step) for step in range(1, reps)]
    part, wanted, weight_t = call(
        prepare,
        [
            shape((hidden, tile), BF16),
            shape((1, tile), jnp.int32),
            shape(first_weight.shape[::-1], BF16),
        ],
        0,
        0,
        3,
        [
            pltpu.VMEM(node_order.shape, jnp.int32),
            pltpu.VMEM(own_t.shape, BF16),
            pltpu.VMEM(first_weight.shape, BF16),
            pltpu.SemaphoreType.DMA((3,)),
        ],
    )(*map(in_hbm, (node_order, own_t, first_weight)))
    hidden_in = call(order_project, shape((hidden, tile), BF16), 0, 3 + reps - 1)(
        part, wanted, weight_t, *others
    )

    tiles = call(
        fetch_tiles,
        shape(tile_values.shape[1:], BF16),
        0,
        0,
        1,
        [pltpu.SemaphoreType.DMA],
    )(in_hbm(tile_values[0]))
    sums = aggregated(*gather_blocks(hidden_in), tiles, hidden + 8, True)
    classes_in, scaling = call(
        functools.partial(combine, reps),
        [shape((padded, tile), BF16), shape((1, tile), F32)],
        0,
        3 + reps,
    )(
        hidden_in,
        first_bias[:, None],
        jnp.pad(second_weight.T, ((0, padded - classes), (0, 0))),
        *sums,
    )

    sums = aggregated(*gather_blocks(classes_in), tiles, padded, False)
    logits = call(functools.partial(finish, reps), shape((classes, tile), F32), 0, 3 + reps)(
        classes_in, scaling, second_bias[:, None], *sums
    )
    return logits.T


def solution(mesh):
    placed = (
        P(("blk", "rep"), None),
        P("blk", None),
        P(("blk", "rep"), None, None, None),
        P(("blk", "rep"), None),
        P(("blk", "rep"), None),
        P(("blk", "rep")),
        P(),
        P(),
        P(),
        P(),
    )
    return jax.shard_map(
        body, mesh=mesh, in_specs=placed, out_specs=P(("blk", "rep"), None), check_vma=False
    )
```

```python
import functools

import jax
import jax.numpy as jnp
from jax import lax
from jax.experimental import pallas as pl
from jax.experimental.pallas import tpu as pltpu
from jax.sharding import PartitionSpec as P

BF16 = jnp.bfloat16
F32 = jnp.float32
ONES_ROWS = 16
VMEM_LIMIT = 32 * 1024 * 1024


def nn(a, b):
    return lax.dot_general(a, b, (((1,), (0,)), ((), ())), preferred_element_type=F32)


def nt(a, b):
    return lax.dot_general(a, b, (((1,), (1,)), ((), ())), preferred_element_type=F32)


def call(kernel, outs, smem=(), vmem=(), hbm=(), scratch=(), smem_outs=0, cost=1 << 20):
    spaces = [pltpu.SMEM] * len(smem) + [pltpu.VMEM] * len(vmem) + [pltpu.HBM] * len(hbm)
    out_spaces = [pltpu.SMEM] * smem_outs + [pltpu.VMEM] * (len(outs) - smem_outs)
    return pl.pallas_call(
        kernel,
        out_shape=outs,
        in_specs=[pl.BlockSpec(memory_space=space) for space in spaces],
        out_specs=[pl.BlockSpec(memory_space=space) for space in out_spaces],
        scratch_shapes=scratch,
        compiler_params=pltpu.CompilerParams(vmem_limit_bytes=VMEM_LIMIT),
        cost_estimate=pl.CostEstimate(flops=cost, bytes_accessed=cost, transcendentals=0),
    )(*smem, *vmem, *[pltpu.with_memory_space_constraint(value, pltpu.HBM) for value in hbm])


def fetched(sources, targets, sems):
    copies = [
        pltpu.make_async_copy(source, target, sems.at[index])
        for index, (source, target) in enumerate(zip(sources, targets))
    ]
    for copy in copies:
        copy.start()
    return copies


def picked(weight_t, features, wanted, owner):
    tile = features.shape[1]
    hidden = nn(weight_t, features[...]).astype(BF16)
    source = lax.broadcasted_iota(jnp.int32, (tile, tile), 0) + owner * tile
    return nn(hidden, jnp.where(source == wanted, 1.0, 0.0).astype(BF16))


def prepare(order, features, weight, part, wanted_out, weight_out, *rest):
    order_in, features_in, weight_in, sems = rest
    for copy in fetched((order, weight, features), (order_in, weight_in, features_in), sems):
        copy.wait()
    tile = features.shape[1]
    member = lax.axis_index("rep")
    wanted = order_in[:, pl.ds(pl.multiple_of(member * tile, tile), tile)]
    wanted_out[...] = wanted
    weight_t = weight_in[...].astype(F32).T.astype(BF16)
    weight_out[...] = weight_t
    part[...] = picked(weight_t, features_in, wanted, member).astype(BF16)


def order_project(part, wanted, weight_t, *rest):
    *features, out = rest
    reps = len(features) + 1
    member = lax.axis_index("rep")
    total = part[...].astype(F32)
    for step in range(1, reps):
        owner = lax.rem(member + step, reps)
        total = total + picked(weight_t[...], features[step - 1], wanted[...], owner)
    out[...] = total.astype(BF16)


def stage(reps, places, live, _, *refs):
    sources, (plan, bias_1, bias_2, weight, tiles), scratch = refs[:6], refs[6:11], refs[11:]
    rows_in, columns_in, row_1, row_2, sems = scratch
    slots = tiles.shape[0]
    copies = fetched(sources, (rows_in, columns_in, row_1, row_2, weight, tiles), sems)
    for copy in copies[:4]:
        copy.wait()
    bias_1[...] = jnp.broadcast_to(row_1[...], (8, row_1.shape[1])).T[:, :1]
    bias_2[...] = jnp.broadcast_to(row_2[...], (8, row_2.shape[1])).T[:, :1]
    block, member = lax.axis_index("blk"), lax.axis_index("rep")
    for slot in range(slots):
        panel = lax.clamp(0, columns_in[0, slot] // reps, len(places[0]) - 1)
        apart = panel ^ block
        place = jnp.int32(0)
        for core in range(2):
            for index, value in enumerate(places[core]):
                place = jnp.where((apart == index) & (block % 2 == core), value, place)
        local = rows_in[0, slot] - block * reps
        step = lax.rem(local - member + reps, reps)
        plan[slot] = place
        plan[slots + slot] = jnp.where((slot < live[0]) & (local >= 0) & (local < reps), step, -1)
    for copy in copies[4:]:
        copy.wait()


def aggregate(count_rows, plan, tiles, *rest):
    parts, outs, panels = rest[:3], rest[3:-1], rest[-1]
    slots, tile = tiles.shape[0], tiles.shape[1]
    height = panels.shape[1]
    extra = ONES_ROWS if count_rows else 0
    start = 0
    for part in parts:
        panels[start : start + part.shape[0]] = part[...]
        start += part.shape[0]
    total = jnp.zeros((len(outs) * (height + extra), tile), F32)
    for slot in range(slots):
        values = panels[plan[slot]]
        pieces = []
        for step in range(len(outs)):
            used = (plan[slots + slot] == step).astype(F32)
            pieces.append(values * used.astype(BF16))
            if extra:
                pieces.append(jnp.full((extra, tile), used, F32).astype(BF16))
        total = total + nt(jnp.concatenate(pieces, axis=0), tiles[slot])
    for step, out in enumerate(outs):
        start = step * (height + extra)
        out[...] = total[start : start + out.shape[0]]


def combine(hidden_in, bias, weight_t, own, *rest):
    *arrived, out, scale_out = rest
    height = hidden_in.shape[0]
    total = own[...]
    for part in arrived:
        total = total + part[...]
    scaling = lax.rsqrt(1.0 + total[height : height + 1])
    hidden = scaling * (total[:height] + hidden_in[...].astype(F32)) + bias[...]
    hidden = jnp.maximum(hidden, 0.0).astype(BF16)
    classes = nn(weight_t[...], hidden)
    blank = jnp.zeros((out.shape[0] - classes.shape[0], classes.shape[1]), F32)
    out[...] = jnp.concatenate([classes, blank], axis=0).astype(BF16)
    scale_out[...] = scaling


def finish(classes_in, scaling, bias, own, *rest):
    *arrived, out = rest
    total = own[...]
    for part in arrived:
        total = total + part[...]
    classes = out.shape[0]
    whole = total + classes_in[...].astype(F32)
    out[...] = scaling[...] * whole[:classes] + bias[...]


def relay(arrived, out):
    out[...] = arrived[...]


def shifted(value, axis, step):
    size = lax.axis_size(axis)
    return lax.ppermute(value, axis, [((d + step) % size, d) for d in range(size)])


def swapped(value, masks):
    return lax.ppermute(value, "blk", [(d ^ masks[d % 2], d) for d in range(lax.axis_size("blk"))])


def chip_order(chips):
    far = [step for step in range(chips - 1, 0, -1) if step % 2 == 0]
    near = [step for step in range(chips - 1, 0, -1) if step % 2]
    order = sorted(far + near, key=lambda step: (step < chips // 2, step % 2, -step))
    return order[0], list(zip(order[1::2], order[2::2]))


def panel_places(chips):
    first, pairs = chip_order(chips)
    tables = []
    for core in range(2):
        near = [2 * first] + [2 * pair[core] + e for pair in pairs for e in range(2)]
        far = [2 * first + 1] + [2 * pair[1 - core] + 1 - e for pair in pairs for e in range(2)]
        stack = [0, 1, *near, *far]
        tables.append([stack.index(apart) for apart in range(2 * chips)])
    return tables


def gather_blocks(value, aside):
    chips = lax.axis_size("blk") // 2
    first, pairs = chip_order(chips)
    parts = [swapped(value, (2 * first, 2 * first))[None]]
    other = swapped(value, (1, 1))
    both = jnp.stack([value, other])
    for pair in pairs:
        parts.append(swapped(both, (2 * pair[0], 2 * pair[1])))
    parts[0], beside = lax.optimization_barrier(aside(parts[0]))
    near = jnp.concatenate(parts)
    return (both, near, swapped(near, (1, 1))), beside


def body(
    features,
    node_order,
    tile_values,
    tile_rows,
    tile_columns,
    tile_live,
    first_weight,
    first_bias,
    second_weight,
    second_bias,
):
    tile = features.shape[0]
    slots = tile_values.shape[1]
    reps = lax.axis_size("rep")
    blocks = lax.axis_size("blk")
    hidden, classes = second_weight.shape
    padded = -(-classes // 16) * 16
    shape = jax.ShapeDtypeStruct

    own_t = features.T
    others = [shifted(own_t, "rep", step) for step in range(1, reps)]
    prepared = call(
        prepare,
        [
            shape((hidden, tile), BF16),
            shape((1, tile), jnp.int32),
            shape(first_weight.shape[::-1], BF16),
        ],
        hbm=(node_order, own_t, first_weight),
        scratch=[
            pltpu.VMEM(node_order.shape, jnp.int32),
            pltpu.VMEM(own_t.shape, BF16),
            pltpu.VMEM(first_weight.shape, BF16),
            pltpu.SemaphoreType.DMA((3,)),
        ],
    )
    (hidden_in,) = call(order_project, [shape((hidden, tile), BF16)], vmem=(*prepared, *others))
    def staged(arrived):
        values = call(
            functools.partial(stage, reps, panel_places(blocks // 2)),
            [
                shape((2 * slots,), jnp.int32),
                shape((hidden, 1), F32),
                shape((classes, 1), F32),
                shape((classes, hidden), BF16),
                shape(tile_values.shape[1:], BF16),
            ],
            smem=(tile_live,),
            vmem=(arrived,),
            hbm=(
                tile_rows,
                tile_columns,
                first_bias[None],
                second_bias[None],
                second_weight.T,
                tile_values[0],
            ),
            scratch=[
                pltpu.SMEM((1, slots), jnp.int32),
                pltpu.SMEM((1, slots), jnp.int32),
                pltpu.VMEM((1, hidden), F32),
                pltpu.VMEM((1, classes), F32),
                pltpu.SemaphoreType.DMA((6,)),
            ],
            smem_outs=1,
        )
        return arrived, values

    def relayed(arrived):
        return call(relay, [shape(arrived.shape, BF16)], vmem=(arrived,), cost=1 << 28)[0], ()

    def aggregated(parts, rows, count_rows):
        sums = call(
            functools.partial(aggregate, count_rows),
            [shape((rows, tile), F32)] * reps,
            smem=(plan,),
            vmem=(tiles, *parts),
            scratch=[pltpu.VMEM((blocks, *parts[0].shape[1:]), BF16)],
        )
        return [sums[0]] + [shifted(sums[reps - step], "rep", step) for step in range(1, reps)]

    parts, (plan, bias_1, bias_2, weight_2, tiles) = gather_blocks(hidden_in, staged)
    sums = aggregated(parts, hidden + 8, True)
    classes_in, scaling = call(
        combine,
        [shape((padded, tile), BF16), shape((1, tile), F32)],
        vmem=(hidden_in, bias_1, weight_2, *sums),
    )
    parts, _ = gather_blocks(classes_in, relayed)
    sums = aggregated(parts, padded, False)
    (logits,) = call(
        finish, [shape((classes, tile), F32)], vmem=(classes_in, scaling, bias_2, *sums)
    )
    return logits.T


def solution(mesh):
    placed = (
        P(("blk", "rep"), None),
        P("blk", None),
        P(("blk", "rep"), None, None, None),
        P(("blk", "rep"), None),
        P(("blk", "rep"), None),
        P(("blk", "rep")),
        P(),
        P(),
        P(),
        P(),
    )
    return jax.shard_map(
        body, mesh=mesh, in_specs=placed, out_specs=P(("blk", "rep"), None), check_vma=False
    )
```

```python
import functools

import jax
import jax.numpy as jnp
from jax import lax
from jax.experimental import pallas as pl
from jax.experimental.pallas import tpu as pltpu
from jax.sharding import PartitionSpec as P

BF16 = jnp.bfloat16
F32 = jnp.float32
ONES_ROWS = 16
VMEM_LIMIT = 32 * 1024 * 1024


def nn(a, b):
    return lax.dot_general(a, b, (((1,), (0,)), ((), ())), preferred_element_type=F32)


def nt(a, b):
    return lax.dot_general(a, b, (((1,), (1,)), ((), ())), preferred_element_type=F32)


def call(kernel, outs, smem=(), vmem=(), hbm=(), scratch=(), smem_outs=0, cost=1 << 20):
    spaces = [pltpu.VMEM] * len(vmem) + [pltpu.SMEM] * len(smem) + [pltpu.HBM] * len(hbm)
    out_spaces = [pltpu.SMEM] * smem_outs + [pltpu.VMEM] * (len(outs) - smem_outs)
    return pl.pallas_call(
        kernel,
        out_shape=outs,
        in_specs=[pl.BlockSpec(memory_space=space) for space in spaces],
        out_specs=[pl.BlockSpec(memory_space=space) for space in out_spaces],
        scratch_shapes=scratch,
        compiler_params=pltpu.CompilerParams(vmem_limit_bytes=VMEM_LIMIT),
        cost_estimate=pl.CostEstimate(flops=cost, bytes_accessed=cost, transcendentals=0),
    )(*vmem, *smem, *[pltpu.with_memory_space_constraint(value, pltpu.HBM) for value in hbm])


def fetched(sources, targets, sems):
    copies = [
        pltpu.make_async_copy(source, target, sems.at[index])
        for index, (source, target) in enumerate(zip(sources, targets))
    ]
    for copy in copies:
        copy.start()
    return copies


def picked(weight_t, features, wanted, owner):
    tile = features.shape[1]
    hidden = nn(weight_t, features[...]).astype(BF16)
    source = lax.broadcasted_iota(jnp.int32, (tile, tile), 0) + owner * tile
    return nn(hidden, jnp.where(source == wanted, 1.0, 0.0).astype(BF16))


def prepare(order, features, weight, part, wanted_out, weight_out, *rest):
    order_in, features_in, weight_in, sems = rest
    for copy in fetched((order, weight, features), (order_in, weight_in, features_in), sems):
        copy.wait()
    tile = features.shape[1]
    member = lax.axis_index("rep")
    wanted = order_in[:, pl.ds(pl.multiple_of(member * tile, tile), tile)]
    wanted_out[...] = wanted
    weight_t = weight_in[...].astype(F32).T.astype(BF16)
    weight_out[...] = weight_t
    part[...] = picked(weight_t, features_in, wanted, member).astype(BF16)


def order_project(part, wanted, weight_t, *rest):
    *features, out = rest
    reps = len(features) + 1
    member = lax.axis_index("rep")
    total = part[...].astype(F32)
    for step in range(1, reps):
        owner = lax.rem(member + step, reps)
        total = total + picked(weight_t[...], features[step - 1], wanted[...], owner)
    out[...] = total.astype(BF16)


def stage(reps, places, arrived, live, *refs):
    sources, (plan, bias_1, bias_2, weight, tiles), scratch = refs[:6], refs[6:11], refs[12:]
    rows_in, columns_in, row_1, row_2, sems = scratch
    slots = tiles.shape[0]
    copies = fetched(sources, (rows_in, columns_in, row_1, row_2, weight, tiles), sems)
    refs[11][...] = arrived[...]
    for copy in copies[:4]:
        copy.wait()
    bias_1[...] = jnp.broadcast_to(row_1[...], (8, row_1.shape[1])).T[:, :1]
    bias_2[...] = jnp.broadcast_to(row_2[...], (8, row_2.shape[1])).T[:, :1]
    block, member = lax.axis_index("blk"), lax.axis_index("rep")
    for slot in range(slots):
        panel = lax.clamp(0, columns_in[0, slot] // reps, len(places[0]) - 1)
        apart = panel ^ block
        place = jnp.int32(0)
        for core in range(2):
            for index, value in enumerate(places[core]):
                place = jnp.where((apart == index) & (block % 2 == core), value, place)
        local = rows_in[0, slot] - block * reps
        step = lax.rem(local - member + reps, reps)
        plan[slot] = place
        plan[slots + slot] = jnp.where((slot < live[0]) & (local >= 0) & (local < reps), step, -1)
    for copy in copies[4:]:
        copy.wait()


def aggregate(count_rows, *refs):
    parts, (tiles, plan), outs, panels = refs[:3], refs[3:5], refs[5:-1], refs[-1]
    slots, tile = tiles.shape[0], tiles.shape[1]
    height = panels.shape[1]
    extra = ONES_ROWS if count_rows else 0
    start = 0
    for part in parts:
        panels[start : start + part.shape[0]] = part[...]
        start += part.shape[0]
    total = jnp.zeros((len(outs) * (height + extra), tile), F32)
    for slot in range(slots):
        values = panels[plan[slot]]
        pieces = []
        for step in range(len(outs)):
            used = (plan[slots + slot] == step).astype(F32)
            pieces.append(values * used.astype(BF16))
            if extra:
                pieces.append(jnp.full((extra, tile), used, F32).astype(BF16))
        total = total + nt(jnp.concatenate(pieces, axis=0), tiles[slot])
    for step, out in enumerate(outs):
        start = step * (height + extra)
        out[...] = total[start : start + out.shape[0]]


def combine(hidden_in, bias, weight_t, own, *rest):
    *arrived, out, scale_out = rest
    height = hidden_in.shape[0]
    total = own[...]
    for part in arrived:
        total = total + part[...]
    scaling = lax.rsqrt(1.0 + total[height : height + 1])
    hidden = scaling * (total[:height] + hidden_in[...].astype(F32)) + bias[...]
    hidden = jnp.maximum(hidden, 0.0).astype(BF16)
    classes = nn(weight_t[...], hidden)
    blank = jnp.zeros((out.shape[0] - classes.shape[0], classes.shape[1]), F32)
    out[...] = jnp.concatenate([classes, blank], axis=0).astype(BF16)
    scale_out[...] = scaling


def finish(classes_in, scaling, bias, own, *rest):
    *arrived, out = rest
    total = own[...]
    for part in arrived:
        total = total + part[...]
    classes = out.shape[0]
    whole = total + classes_in[...].astype(F32)
    out[...] = scaling[...] * whole[:classes] + bias[...]


def relay(arrived, out):
    out[...] = arrived[...]


def shifted(value, axis, step):
    size = lax.axis_size(axis)
    return lax.ppermute(value, axis, [((d + step) % size, d) for d in range(size)])


def swapped(value, masks):
    return lax.ppermute(value, "blk", [(d ^ masks[d % 2], d) for d in range(lax.axis_size("blk"))])


def outer_order(outer):
    first = outer // 2
    rest = [step for step in range(outer - 1, 0, -1) if step != first]
    return first, list(zip(rest[0::2], rest[1::2]))


def panel_places(outer):
    first, pairs = outer_order(outer)
    lists = []
    for core in range(2):
        across = [4 * pair[core] + e for pair in pairs for e in range(2)]
        over = [2, 4 * first + 2] + [apart + 2 for apart in across]
        lists.append([4 * first, *across, *over])
    tables = []
    for core in range(2):
        stack = [0, 1, *lists[core], *[apart ^ 1 for apart in lists[1 - core]]]
        tables.append([stack.index(apart) for apart in range(4 * outer)])
    return tables


def packed(*parts):
    def pack(*refs):
        for index, ref in enumerate(refs[:-1]):
            refs[-1][index] = ref[...]

    return call(pack, [jax.ShapeDtypeStruct((len(parts), *parts[0].shape), BF16)], vmem=parts, cost=1 << 32)[0]


def gather_blocks(value, aside):
    outer = lax.axis_size("blk") // 4
    first, pairs = outer_order(outer)
    other = swapped(value, (1, 1))
    ahead = swapped(value, (4 * first, 4 * first))
    both = jnp.stack([value, other])
    across = [swapped(both, (4 * pair[0], 4 * pair[1])) for pair in pairs]
    across = across[0] if len(across) == 1 else jnp.concatenate(across)
    over = swapped(packed(value, ahead), (2, 2))
    beyond = swapped(across, (2, 2))
    over, beside = aside(over)
    near = jnp.concatenate([ahead[None], across, over, beyond])
    return (both, near, swapped(near, (1, 1))), beside


def body(
    features,
    node_order,
    tile_values,
    tile_rows,
    tile_columns,
    tile_live,
    first_weight,
    first_bias,
    second_weight,
    second_bias,
):
    tile = features.shape[0]
    slots = tile_values.shape[1]
    reps = lax.axis_size("rep")
    blocks = lax.axis_size("blk")
    hidden, classes = second_weight.shape
    padded = -(-classes // 16) * 16
    shape = jax.ShapeDtypeStruct

    own_t = features.T
    others = [shifted(own_t, "rep", step) for step in range(1, reps)]
    prepared = call(
        prepare,
        [
            shape((hidden, tile), BF16),
            shape((1, tile), jnp.int32),
            shape(first_weight.shape[::-1], BF16),
        ],
        hbm=(node_order, own_t, first_weight),
        scratch=[
            pltpu.VMEM(node_order.shape, jnp.int32),
            pltpu.VMEM(own_t.shape, BF16),
            pltpu.VMEM(first_weight.shape, BF16),
            pltpu.SemaphoreType.DMA((3,)),
        ],
    )
    (hidden_in,) = call(order_project, [shape((hidden, tile), BF16)], vmem=(*prepared, *others))
    def staged(arrived):
        values = call(
            functools.partial(stage, reps, panel_places(blocks // 4)),
            [
                shape((2 * slots,), jnp.int32),
                shape((hidden, 1), F32),
                shape((classes, 1), F32),
                shape((classes, hidden), BF16),
                shape(tile_values.shape[1:], BF16),
                shape(arrived.shape, BF16),
            ],
            smem=(tile_live,),
            vmem=(arrived,),
            hbm=(
                tile_rows,
                tile_columns,
                first_bias[None],
                second_bias[None],
                second_weight.T,
                tile_values[0],
            ),
            scratch=[
                pltpu.SMEM((1, slots), jnp.int32),
                pltpu.SMEM((1, slots), jnp.int32),
                pltpu.VMEM((1, hidden), F32),
                pltpu.VMEM((1, classes), F32),
                pltpu.SemaphoreType.DMA((6,)),
            ],
            smem_outs=1,
            cost=1 << 28,
        )
        return values[-1], values[:-1]

    def relayed(arrived):
        return call(relay, [shape(arrived.shape, BF16)], vmem=(arrived,), cost=1 << 28)[0], ()

    def aggregated(parts, rows, count_rows):
        sums = call(
            functools.partial(aggregate, count_rows),
            [shape((rows, tile), F32)] * reps,
            smem=(plan,),
            vmem=(*parts, tiles),
            scratch=[pltpu.VMEM((blocks, *parts[0].shape[1:]), BF16)],
        )
        return [sums[0]] + [shifted(sums[reps - step], "rep", step) for step in range(1, reps)]

    parts, (plan, bias_1, bias_2, weight_2, tiles) = gather_blocks(hidden_in, staged)
    sums = aggregated(parts, hidden + 8, True)
    classes_in, scaling = call(
        combine,
        [shape((padded, tile), BF16), shape((1, tile), F32)],
        vmem=(hidden_in, bias_1, weight_2, *sums),
    )
    parts, _ = gather_blocks(classes_in, relayed)
    sums = aggregated(parts, padded, False)
    (logits,) = call(
        finish, [shape((classes, tile), F32)], vmem=(classes_in, scaling, bias_2, *sums)
    )
    return logits.T


def solution(mesh):
    placed = (
        P(("blk", "rep"), None),
        P("blk", None),
        P(("blk", "rep"), None, None, None),
        P(("blk", "rep"), None),
        P(("blk", "rep"), None),
        P(("blk", "rep")),
        P(),
        P(),
        P(),
        P(),
    )
    return jax.shard_map(
        body, mesh=mesh, in_specs=placed, out_specs=P(("blk", "rep"), None), check_vma=False
    )
```

```python
import functools

import jax
import jax.numpy as jnp
from jax import lax
from jax.experimental import pallas as pl
from jax.experimental.pallas import tpu as pltpu
from jax.sharding import PartitionSpec as P

BF16 = jnp.bfloat16
F32 = jnp.float32
ONES_ROWS = 16
VMEM_LIMIT = 32 * 1024 * 1024


def nn(a, b):
    return lax.dot_general(a, b, (((1,), (0,)), ((), ())), preferred_element_type=F32)


def nt(a, b):
    return lax.dot_general(a, b, (((1,), (1,)), ((), ())), preferred_element_type=F32)


def call(kernel, outs, smem=(), vmem=(), hbm=(), scratch=(), smem_outs=0, cost=1 << 20):
    spaces = [pltpu.VMEM] * len(vmem) + [pltpu.SMEM] * len(smem) + [pltpu.HBM] * len(hbm)
    out_spaces = [pltpu.SMEM] * smem_outs + [pltpu.VMEM] * (len(outs) - smem_outs)
    return pl.pallas_call(
        kernel,
        out_shape=outs,
        in_specs=[pl.BlockSpec(memory_space=space) for space in spaces],
        out_specs=[pl.BlockSpec(memory_space=space) for space in out_spaces],
        scratch_shapes=scratch,
        compiler_params=pltpu.CompilerParams(vmem_limit_bytes=VMEM_LIMIT),
        cost_estimate=pl.CostEstimate(flops=cost, bytes_accessed=cost, transcendentals=0),
    )(*vmem, *smem, *[pltpu.with_memory_space_constraint(value, pltpu.HBM) for value in hbm])


def fetched(sources, targets, sems):
    copies = [
        pltpu.make_async_copy(source, target, sems.at[index])
        for index, (source, target) in enumerate(zip(sources, targets))
    ]
    for copy in copies:
        copy.start()
    return copies


def picked(features, wanted, owner):
    tile = features.shape[1]
    source = lax.broadcasted_iota(jnp.int32, (tile, tile), 0) + owner * tile
    return nn(features[...], jnp.where(source == wanted, 1.0, 0.0).astype(BF16))


def prepare(order, features, part, wanted_out, *rest):
    order_in, features_in, sems = rest
    for copy in fetched((order, features), (order_in, features_in), sems):
        copy.wait()
    tile = features.shape[1]
    member = lax.axis_index("rep")
    wanted = order_in[:, pl.ds(pl.multiple_of(member * tile, tile), tile)]
    wanted_out[...] = wanted
    part[...] = picked(features_in, wanted, member)


def arrange(part, wanted, *rest):
    *features, out = rest
    reps = len(features) + 1
    member = lax.axis_index("rep")
    total = part[...]
    for step in range(1, reps):
        owner = lax.rem(member + step, reps)
        total = total + picked(features[step - 1], wanted[...], owner)
    out[...] = total.astype(BF16)


def stage(reps, _, live, *refs):
    sources, (plan, bias_1, bias_2, weight_1, weight_2, tiles), scratch = refs[:7], refs[7:13], refs[13:]
    rows_in, columns_in, row_1, row_2, weight_in, sems = scratch
    slots = tiles.shape[0]
    blocks = lax.axis_size("blk")
    copies = fetched(sources, (rows_in, columns_in, row_1, row_2, weight_in, weight_2, tiles), sems)
    for copy in copies[:5]:
        copy.wait()
    bias_1[...] = jnp.broadcast_to(row_1[...], (8, row_1.shape[1])).T[:, :1]
    bias_2[...] = jnp.broadcast_to(row_2[...], (8, row_2.shape[1])).T[:, :1]
    weight_1[...] = weight_in[...].astype(F32).T.astype(BF16)
    block, member = lax.axis_index("blk"), lax.axis_index("rep")
    for slot in range(slots):
        plan[slot] = lax.clamp(0, columns_in[0, slot] // reps, blocks - 1) ^ block
        local = rows_in[0, slot] - block * reps
        step = lax.rem(local - member + reps, reps)
        plan[slots + slot] = jnp.where((slot < live[0]) & (local >= 0) & (local < reps), step, -1)
    for copy in copies[5:]:
        copy.wait()


def project(weight_t, *refs):
    *stacks, out = refs
    start = 0
    for stack in stacks:
        for index in range(stack.shape[0]):
            out[start + index] = nn(weight_t[...], stack[index]).astype(BF16)
        start += stack.shape[0]


def summed(panels, plan, tiles, count, extra):
    slots, tile = tiles.shape[0], tiles.shape[1]
    height = panels.shape[1] + extra
    total = jnp.zeros((count * height, tile), F32)
    for slot in range(slots):
        values = panels[plan[slot]]
        pieces = []
        for step in range(count):
            used = (plan[slots + slot] == step).astype(F32)
            pieces.append(values * used.astype(BF16))
            if extra:
                pieces.append(jnp.full((extra, tile), used, F32).astype(BF16))
        total = total + nt(jnp.concatenate(pieces, axis=0), tiles[slot])
    return [total[step * height : (step + 1) * height] for step in range(count)]


def in_thirds(row):
    first = row.astype(BF16).astype(F32)
    second = (row - first).astype(BF16).astype(F32)
    return first, second, row - first - second


def aggregate_hidden(projected, far, weight_t, tiles, plan, own, *rest):
    others, panels = rest[:-1], rest[-1]
    mine, opposite = panel_order(panels.shape[0] // 4, lax.axis_index("blk") % 2)
    for index, place in enumerate(mine):
        panels[place] = projected[index]
    for index, place in enumerate(opposite):
        panels[place] = nn(weight_t[...], far[index]).astype(BF16)
    height = panels.shape[1]
    sums = summed(panels, plan, tiles, 1 + len(others), ONES_ROWS)
    own[...] = sums[0][: own.shape[0]]
    row = lax.broadcasted_iota(jnp.int32, (ONES_ROWS, tiles.shape[1]), 0)
    for part, out in zip(sums[1:], others):
        first, second, third = in_thirds(part[height:])
        degree = jnp.where(row == 0, first, jnp.where(row == 1, second, jnp.where(row == 2, third, 0.0)))
        out[...] = jnp.concatenate([part[:height], degree], axis=0).astype(BF16)


def aggregate_classes(near, far, tiles, plan, *rest):
    outs, panels = rest[:-1], rest[-1]
    chip = lax.axis_index("blk") // 2
    for index in range(near.shape[0]):
        panels[2 * (index ^ chip)] = near[index]
        panels[2 * (index ^ chip) + 1] = far[index]
    for out, part in zip(outs, summed(panels, plan, tiles, len(outs), 0)):
        out[...] = part


def combine(hidden_in, bias, weight_t, own, *rest):
    *arrived, out, scale_out = rest
    height = hidden_in.shape[1]
    total, degree = own[:height], own[height : height + 1]
    for part in arrived:
        values = part[...].astype(F32)
        total = total + values[:height]
        terms = [values[height + index : height + index + 1] for index in range(3)]
        degree = degree + (terms[0] + (terms[1] + terms[2]))
    scaling = lax.rsqrt(1.0 + degree)
    hidden = scaling * (total + hidden_in[0].astype(F32)) + bias[...]
    hidden = jnp.maximum(hidden, 0.0).astype(BF16)
    classes = nn(weight_t[...], hidden)
    blank = jnp.zeros((out.shape[0] - classes.shape[0], classes.shape[1]), F32)
    out[...] = jnp.concatenate([classes, blank], axis=0).astype(BF16)
    scale_out[...] = scaling


def finish(classes_in, scaling, bias, own, *rest):
    *arrived, out = rest
    total = own[...]
    for part in arrived:
        total = total + part[...]
    classes = out.shape[0]
    whole = total + classes_in[...].astype(F32)
    out[...] = scaling[...] * whole[:classes] + bias[...]


def shifted(value, axis, step):
    size = lax.axis_size(axis)
    return lax.ppermute(value, axis, [((d + step) % size, d) for d in range(size)])


def swapped(value, masks):
    return lax.ppermute(value, "blk", [(d ^ masks[d % 2], d) for d in range(lax.axis_size("blk"))])


def outer_order(outer):
    first = outer // 2
    rest = [step for step in range(outer - 1, 0, -1) if step != first]
    return first, list(zip(rest[0::2], rest[1::2]))


def panel_order(outer, core):
    first, pairs = outer_order(outer)
    lists = []
    for here in (core, 1 - core):
        across = [jnp.where(here == 0, 4 * pair[0], 4 * pair[1]) + e for pair in pairs for e in range(2)]
        lists.append([4 * first, *across, 2, 4 * first + 2, *[apart + 2 for apart in across]])
    return [0, 1, *lists[0]], [apart ^ 1 for apart in lists[1]]


def packed(parts, after):
    def pack(*refs):
        for index in range(len(parts)):
            refs[-1][index] = refs[index][...]

    out = jax.ShapeDtypeStruct((len(parts), *parts[0].shape), BF16)
    return call(pack, [out], vmem=(*parts, after), cost=1 << 32)[0]


def gather_features(value, aside):
    outer = lax.axis_size("blk") // 4
    first, pairs = outer_order(outer)
    other = swapped(value, (1, 1))
    ahead = swapped(value, (4 * first, 4 * first))
    both = jnp.stack([value, other])
    beside = aside(both)
    across = [swapped(both, (4 * pair[0], 4 * pair[1])) for pair in pairs]
    across = across[0] if len(across) == 1 else jnp.concatenate(across)
    over = swapped(packed((value, ahead), beside[1]), (2, 2))
    beyond = swapped(across, (2, 2))
    near = jnp.concatenate([ahead[None], across, over, beyond])
    return (both, near, swapped(near, (1, 1))), beside


def gather_classes(value):
    size = lax.axis_size("blk")
    groups = [list(range(core, size, 2)) for core in range(2)]
    copies = jnp.broadcast_to(value[None], (size // 2, *value.shape))
    near = lax.all_to_all(copies, "blk", 0, 0, axis_index_groups=groups)
    return near, swapped(near, (1, 1))


def body(
    features,
    node_order,
    tile_values,
    tile_rows,
    tile_columns,
    tile_live,
    first_weight,
    first_bias,
    second_weight,
    second_bias,
):
    tile, width = features.shape
    slots = tile_values.shape[1]
    reps = lax.axis_size("rep")
    blocks = lax.axis_size("blk")
    hidden, classes = second_weight.shape
    padded = -(-classes // 16) * 16
    shape = jax.ShapeDtypeStruct

    def exchanged(sums):
        return [shifted(sums[reps - 1 - step], "rep", step) for step in range(1, reps)]

    own_t = features.T
    others = [shifted(own_t, "rep", step) for step in range(1, reps)]
    prepared = call(
        prepare,
        [shape((width, tile), F32), shape((1, tile), jnp.int32)],
        hbm=(node_order, own_t),
        scratch=[
            pltpu.VMEM(node_order.shape, jnp.int32),
            pltpu.VMEM(own_t.shape, BF16),
            pltpu.SemaphoreType.DMA((2,)),
        ],
    )
    (ordered,) = call(arrange, [shape((width, tile), BF16)], vmem=(*prepared, *others))

    def staged(after):
        return call(
            functools.partial(stage, reps),
            [
                shape((2 * slots,), jnp.int32),
                shape((hidden, 1), F32),
                shape((classes, 1), F32),
                shape((hidden, width), BF16),
                shape((classes, hidden), BF16),
                shape(tile_values.shape[1:], BF16),
            ],
            vmem=(after,),
            smem=(tile_live,),
            hbm=(
                tile_rows,
                tile_columns,
                first_bias[None],
                second_bias[None],
                first_weight,
                second_weight.T,
                tile_values[0],
            ),
            scratch=[
                pltpu.SMEM((1, slots), jnp.int32),
                pltpu.SMEM((1, slots), jnp.int32),
                pltpu.VMEM((1, hidden), F32),
                pltpu.VMEM((1, classes), F32),
                pltpu.VMEM(first_weight.shape, BF16),
                pltpu.SemaphoreType.DMA((7,)),
            ],
            smem_outs=1,
        )

    (both, near, far), values = gather_features(ordered, staged)
    plan, bias_1, bias_2, weight_1, weight_2, tiles = values
    (projected,) = call(
        project,
        [shape((2 + near.shape[0], hidden, tile), BF16)],
        vmem=(weight_1, both, near),
    )
    own, *sums = call(
        aggregate_hidden,
        [shape((hidden + 8, tile), F32)] + [shape((hidden + ONES_ROWS, tile), BF16)] * (reps - 1),
        vmem=(projected, far, weight_1, tiles),
        smem=(plan,),
        scratch=[pltpu.VMEM((blocks, hidden, tile), BF16)],
    )
    classes_in, scaling = call(
        combine,
        [shape((padded, tile), BF16), shape((1, tile), F32)],
        vmem=(projected, bias_1, weight_2, own, *exchanged(sums)),
    )
    own, *sums = call(
        aggregate_classes,
        [shape((padded, tile), F32)] * reps,
        vmem=(*gather_classes(classes_in), tiles),
        smem=(plan,),
        scratch=[pltpu.VMEM((blocks, padded, tile), BF16)],
    )
    (logits,) = call(
        finish,
        [shape((classes, tile), F32)],
        vmem=(classes_in, scaling, bias_2, own, *exchanged(sums)),
    )
    return logits.T


def solution(mesh):
    placed = (
        P(("blk", "rep"), None),
        P("blk", None),
        P(("blk", "rep"), None, None, None),
        P(("blk", "rep"), None),
        P(("blk", "rep"), None),
        P(("blk", "rep")),
        P(),
        P(),
        P(),
        P(),
    )
    return jax.shard_map(
        body, mesh=mesh, in_specs=placed, out_specs=P(("blk", "rep"), None), check_vma=False
    )
```

```python
import functools

import jax
import jax.numpy as jnp
from jax import lax
from jax.experimental import pallas as pl
from jax.experimental.pallas import tpu as pltpu
from jax.sharding import PartitionSpec as P

BF16 = jnp.bfloat16
F32 = jnp.float32
ONES_ROWS = 16
VMEM_LIMIT = 32 * 1024 * 1024


def nn(a, b):
    return lax.dot_general(a, b, (((1,), (0,)), ((), ())), preferred_element_type=F32)


def nt(a, b):
    return lax.dot_general(a, b, (((1,), (1,)), ((), ())), preferred_element_type=F32)


def call(kernel, outs, smem=(), vmem=(), hbm=(), scratch=(), smem_outs=0, cost=1 << 20):
    spaces = [pltpu.VMEM] * len(vmem) + [pltpu.SMEM] * len(smem) + [pltpu.HBM] * len(hbm)
    out_spaces = [pltpu.SMEM] * smem_outs + [pltpu.VMEM] * (len(outs) - smem_outs)
    return pl.pallas_call(
        kernel,
        out_shape=outs,
        in_specs=[pl.BlockSpec(memory_space=space) for space in spaces],
        out_specs=[pl.BlockSpec(memory_space=space) for space in out_spaces],
        scratch_shapes=scratch,
        compiler_params=pltpu.CompilerParams(vmem_limit_bytes=VMEM_LIMIT),
        cost_estimate=pl.CostEstimate(flops=cost, bytes_accessed=cost, transcendentals=0),
    )(*vmem, *smem, *[pltpu.with_memory_space_constraint(value, pltpu.HBM) for value in hbm])


def fetched(sources, targets, sems):
    copies = [
        pltpu.make_async_copy(source, target, sems.at[index])
        for index, (source, target) in enumerate(zip(sources, targets))
    ]
    for copy in copies:
        copy.start()
    return copies


def picked(features, wanted, owner):
    tile = features.shape[1]
    source = lax.broadcasted_iota(jnp.int32, (tile, tile), 0) + owner * tile
    return nn(features[...], jnp.where(source == wanted, 1.0, 0.0).astype(BF16))


def prepare(order, features, part, wanted_out, *rest):
    order_in, features_in, sems = rest
    for copy in fetched((order, features), (order_in, features_in), sems):
        copy.wait()
    tile = features.shape[1]
    member = lax.axis_index("rep")
    wanted = order_in[:, pl.ds(pl.multiple_of(member * tile, tile), tile)]
    wanted_out[...] = wanted
    part[...] = picked(features_in, wanted, member)


def arrange(part, wanted, *rest):
    *features, out = rest
    reps = len(features) + 1
    member = lax.axis_index("rep")
    total = part[...]
    for step in range(1, reps):
        owner = lax.rem(member + step, reps)
        total = total + picked(features[step - 1], wanted[...], owner)
    out[...] = total.astype(BF16)


def stage(reps, _, live, *refs):
    sources, (plan, bias_1, bias_2, weight_1, weight_2, tiles), scratch = refs[:7], refs[7:13], refs[13:]
    rows_in, columns_in, row_1, row_2, weight_in, sems = scratch
    slots = tiles.shape[0]
    blocks = lax.axis_size("blk")
    copies = fetched(sources, (rows_in, columns_in, row_1, row_2, weight_in, weight_2, tiles), sems)
    for copy in copies[:5]:
        copy.wait()
    bias_1[...] = jnp.broadcast_to(row_1[...], (8, row_1.shape[1])).T[:, :1]
    bias_2[...] = jnp.broadcast_to(row_2[...], (8, row_2.shape[1])).T[:, :1]
    weight_1[...] = weight_in[...].astype(F32).T.astype(BF16)
    block, member = lax.axis_index("blk"), lax.axis_index("rep")
    for slot in range(slots):
        plan[slot] = lax.clamp(0, columns_in[0, slot] // reps, blocks - 1) ^ block
        local = rows_in[0, slot] - block * reps
        step = lax.rem(local - member + reps, reps)
        plan[slots + slot] = jnp.where((slot < live[0]) & (local >= 0) & (local < reps), step, -1)
    for copy in copies[5:]:
        copy.wait()


def project(weight_t, *refs):
    *stacks, out = refs
    start = 0
    for stack in stacks:
        for index in range(stack.shape[0]):
            out[start + index] = nn(weight_t[...], stack[index]).astype(BF16)
        start += stack.shape[0]


def summed(panels, plan, tiles, count, extra):
    slots, tile = tiles.shape[0], tiles.shape[1]
    height = panels.shape[1] + extra
    total = jnp.zeros((count * height, tile), F32)
    for slot in range(slots):
        values = panels[plan[slot]]
        pieces = []
        for step in range(count):
            used = (plan[slots + slot] == step).astype(F32)
            pieces.append(values * used.astype(BF16))
            if extra:
                pieces.append(jnp.full((extra, tile), used, F32).astype(BF16))
        total = total + nt(jnp.concatenate(pieces, axis=0), tiles[slot])
    return [total[step * height : (step + 1) * height] for step in range(count)]


def in_thirds(row):
    first = row.astype(BF16).astype(F32)
    second = (row - first).astype(BF16).astype(F32)
    return first, second, row - first - second


def aggregate_hidden(projected, far, weight_t, tiles, plan, own, *rest):
    others, panels = rest[:-1], rest[-1]
    mine, opposite = panel_order(panels.shape[0] // 4, lax.axis_index("blk") % 2)
    for index, place in enumerate(mine):
        panels[place] = projected[index]
    for index, place in enumerate(opposite):
        panels[place] = nn(weight_t[...], far[index]).astype(BF16)
    height = panels.shape[1]
    sums = summed(panels, plan, tiles, 1 + len(others), ONES_ROWS)
    own[...] = sums[0][: own.shape[0]]
    row = lax.broadcasted_iota(jnp.int32, (ONES_ROWS, tiles.shape[1]), 0)
    for part, out in zip(sums[1:], others):
        first, second, third = in_thirds(part[height:])
        degree = jnp.where(row == 0, first, jnp.where(row == 1, second, jnp.where(row == 2, third, 0.0)))
        out[...] = jnp.concatenate([part[:height], degree], axis=0).astype(BF16)


def aggregate_classes(near, far, tiles, plan, *rest):
    outs, panels = rest[:-1], rest[-1]
    chip = lax.axis_index("blk") // 2
    for index in range(near.shape[0]):
        panels[2 * (index ^ chip)] = near[index]
        panels[2 * (index ^ chip) + 1] = far[index]
    for out, part in zip(outs, summed(panels, plan, tiles, len(outs), 0)):
        out[...] = part


def combine(hidden_in, bias, weight_t, own, *rest):
    *arrived, out, scale_out = rest
    height = hidden_in.shape[1]
    total, degree = own[:height], own[height : height + 1]
    for part in arrived:
        values = part[...].astype(F32)
        total = total + values[:height]
        terms = [values[height + index : height + index + 1] for index in range(3)]
        degree = degree + (terms[0] + (terms[1] + terms[2]))
    scaling = lax.rsqrt(1.0 + degree)
    hidden = scaling * (total + hidden_in[0].astype(F32)) + bias[...]
    hidden = jnp.maximum(hidden, 0.0).astype(BF16)
    classes = nn(weight_t[...], hidden)
    blank = jnp.zeros((out.shape[0] - classes.shape[0], classes.shape[1]), F32)
    out[...] = jnp.concatenate([classes, blank], axis=0).astype(BF16)
    scale_out[...] = scaling


def finish(classes_in, scaling, bias, own, *rest):
    *arrived, out = rest
    total = own[...]
    for part in arrived:
        total = total + part[...]
    classes = out.shape[0]
    whole = total + classes_in[...].astype(F32)
    out[...] = scaling[...] * whole[:classes] + bias[...]


def shifted(value, axis, step):
    size = lax.axis_size(axis)
    return lax.ppermute(value, axis, [((d + step) % size, d) for d in range(size)])


def swapped(value, masks):
    return lax.ppermute(value, "blk", [(d ^ masks[d % 2], d) for d in range(lax.axis_size("blk"))])


def outer_order(outer):
    rest = list(range(2, outer))
    return 1, list(zip(rest[0::2], rest[1::2]))


def panel_order(outer, core):
    first, pairs = outer_order(outer)
    lists = []
    for here in (core, 1 - core):
        across = [jnp.where(here == 0, 4 * pair[0], 4 * pair[1]) + e for pair in pairs for e in range(2)]
        lists.append([4 * first, *across, 2, 4 * first + 2, *[apart + 2 for apart in across]])
    return [0, 1, *lists[0]], [apart ^ 1 for apart in lists[1]]


def packed(*parts, after=()):
    def pack(*refs):
        for index in range(len(parts)):
            refs[-1][index] = refs[index][...]

    out = jax.ShapeDtypeStruct((len(parts), *parts[0].shape), BF16)
    return call(pack, [out], vmem=(*parts, *after), cost=1 << 32)[0]


def gather_features(value, aside):
    outer = lax.axis_size("blk") // 4
    first, pairs = outer_order(outer)
    other = swapped(value, (1, 1))
    ahead = swapped(value, (4 * first, 4 * first))
    both = jnp.stack([value, other])
    across = [swapped(both, (4 * pair[0], 4 * pair[1])) for pair in pairs]
    across = across[0] if len(across) == 1 else jnp.concatenate(across)
    here = packed(value, ahead)
    over = swapped(here, (2, 2))
    beside = aside(here)
    across = packed(across, after=(beside[1],))[0]
    beyond = swapped(across, (2, 2))
    near = jnp.concatenate([ahead[None], across, over, beyond])
    return (both, near, swapped(near, (1, 1))), beside


def gather_classes(value):
    size = lax.axis_size("blk")
    groups = [list(range(core, size, 2)) for core in range(2)]
    copies = jnp.broadcast_to(value[None], (size // 2, *value.shape))
    near = lax.all_to_all(copies, "blk", 0, 0, axis_index_groups=groups)
    return near, swapped(near, (1, 1))


def body(
    features,
    node_order,
    tile_values,
    tile_rows,
    tile_columns,
    tile_live,
    first_weight,
    first_bias,
    second_weight,
    second_bias,
):
    tile, width = features.shape
    slots = tile_values.shape[1]
    reps = lax.axis_size("rep")
    blocks = lax.axis_size("blk")
    hidden, classes = second_weight.shape
    padded = -(-classes // 16) * 16
    shape = jax.ShapeDtypeStruct

    def exchanged(sums):
        return [shifted(sums[reps - 1 - step], "rep", step) for step in range(1, reps)]

    own_t = features.T
    others = [shifted(own_t, "rep", step) for step in range(1, reps)]
    prepared = call(
        prepare,
        [shape((width, tile), F32), shape((1, tile), jnp.int32)],
        hbm=(node_order, own_t),
        scratch=[
            pltpu.VMEM(node_order.shape, jnp.int32),
            pltpu.VMEM(own_t.shape, BF16),
            pltpu.SemaphoreType.DMA((2,)),
        ],
    )
    (ordered,) = call(arrange, [shape((width, tile), BF16)], vmem=(*prepared, *others))

    def staged(after):
        return call(
            functools.partial(stage, reps),
            [
                shape((2 * slots,), jnp.int32),
                shape((hidden, 1), F32),
                shape((classes, 1), F32),
                shape((hidden, width), BF16),
                shape((classes, hidden), BF16),
                shape(tile_values.shape[1:], BF16),
            ],
            vmem=(after,),
            smem=(tile_live,),
            hbm=(
                tile_rows,
                tile_columns,
                first_bias[None],
                second_bias[None],
                first_weight,
                second_weight.T,
                tile_values[0],
            ),
            scratch=[
                pltpu.SMEM((1, slots), jnp.int32),
                pltpu.SMEM((1, slots), jnp.int32),
                pltpu.VMEM((1, hidden), F32),
                pltpu.VMEM((1, classes), F32),
                pltpu.VMEM(first_weight.shape, BF16),
                pltpu.SemaphoreType.DMA((7,)),
            ],
            smem_outs=1,
        )

    (both, near, far), values = gather_features(ordered, staged)
    plan, bias_1, bias_2, weight_1, weight_2, tiles = values
    (projected,) = call(
        project,
        [shape((2 + near.shape[0], hidden, tile), BF16)],
        vmem=(weight_1, both, near),
    )
    own, *sums = call(
        aggregate_hidden,
        [shape((hidden + 8, tile), F32)] + [shape((hidden + ONES_ROWS, tile), BF16)] * (reps - 1),
        vmem=(projected, far, weight_1, tiles),
        smem=(plan,),
        scratch=[pltpu.VMEM((blocks, hidden, tile), BF16)],
    )
    classes_in, scaling = call(
        combine,
        [shape((padded, tile), BF16), shape((1, tile), F32)],
        vmem=(projected, bias_1, weight_2, own, *exchanged(sums)),
    )
    own, *sums = call(
        aggregate_classes,
        [shape((padded, tile), F32)] * reps,
        vmem=(*gather_classes(classes_in), tiles),
        smem=(plan,),
        scratch=[pltpu.VMEM((blocks, padded, tile), BF16)],
    )
    (logits,) = call(
        finish,
        [shape((classes, tile), F32)],
        vmem=(classes_in, scaling, bias_2, own, *exchanged(sums)),
    )
    return logits.T


def solution(mesh):
    placed = (
        P(("blk", "rep"), None),
        P("blk", None),
        P(("blk", "rep"), None, None, None),
        P(("blk", "rep"), None),
        P(("blk", "rep"), None),
        P(("blk", "rep")),
        P(),
        P(),
        P(),
        P(),
    )
    return jax.shard_map(
        body, mesh=mesh, in_specs=placed, out_specs=P(("blk", "rep"), None), check_vma=False
    )
```

```python
import functools

import jax
import jax.numpy as jnp
from jax import lax
from jax.experimental import pallas as pl
from jax.experimental.pallas import tpu as pltpu
from jax.sharding import PartitionSpec as P

BF16 = jnp.bfloat16
F32 = jnp.float32
ONES_ROWS = 16
VMEM_LIMIT = 32 * 1024 * 1024


def nn(a, b):
    return lax.dot_general(a, b, (((1,), (0,)), ((), ())), preferred_element_type=F32)


def nt(a, b):
    return lax.dot_general(a, b, (((1,), (1,)), ((), ())), preferred_element_type=F32)


def call(kernel, outs, smem=(), vmem=(), hbm=(), scratch=(), smem_outs=0, cost=1 << 20):
    spaces = [pltpu.VMEM] * len(vmem) + [pltpu.SMEM] * len(smem) + [pltpu.HBM] * len(hbm)
    out_spaces = [pltpu.SMEM] * smem_outs + [pltpu.VMEM] * (len(outs) - smem_outs)
    return pl.pallas_call(
        kernel,
        out_shape=outs,
        in_specs=[pl.BlockSpec(memory_space=space) for space in spaces],
        out_specs=[pl.BlockSpec(memory_space=space) for space in out_spaces],
        scratch_shapes=scratch,
        compiler_params=pltpu.CompilerParams(vmem_limit_bytes=VMEM_LIMIT),
        cost_estimate=pl.CostEstimate(flops=cost, bytes_accessed=cost, transcendentals=0),
    )(*vmem, *smem, *[pltpu.with_memory_space_constraint(value, pltpu.HBM) for value in hbm])


def fetched(sources, targets, sems):
    copies = [
        pltpu.make_async_copy(source, target, sems.at[index])
        for index, (source, target) in enumerate(zip(sources, targets))
    ]
    for copy in copies:
        copy.start()
    return copies


def picked(features, wanted, owner):
    tile = features.shape[1]
    source = lax.broadcasted_iota(jnp.int32, (tile, tile), 0) + owner * tile
    return nn(features[...], jnp.where(source == wanted, 1.0, 0.0).astype(BF16))


def prepare(order, features, part, wanted_out, *rest):
    order_in, features_in, sems = rest
    for copy in fetched((order, features), (order_in, features_in), sems):
        copy.wait()
    tile = features.shape[1]
    member = lax.axis_index("rep")
    wanted = order_in[:, pl.ds(pl.multiple_of(member * tile, tile), tile)]
    wanted_out[...] = wanted
    part[...] = picked(features_in, wanted, member)


def arrange(part, wanted, *rest):
    *features, out = rest
    reps = len(features) + 1
    member = lax.axis_index("rep")
    total = part[...]
    for step in range(1, reps):
        owner = lax.rem(member + step, reps)
        total = total + picked(features[step - 1], wanted[...], owner)
    out[...] = total.astype(BF16)


def stage(reps, _, live, *refs):
    sources, (plan, bias_1, bias_2, weight_1, weight_2, tiles), scratch = refs[:7], refs[7:13], refs[13:]
    rows_in, columns_in, row_1, row_2, weight_in, sems = scratch
    slots = tiles.shape[0]
    blocks = lax.axis_size("blk")
    copies = fetched(sources, (rows_in, columns_in, row_1, row_2, weight_in, weight_2, tiles), sems)
    for copy in copies[:5]:
        copy.wait()
    bias_1[...] = jnp.broadcast_to(row_1[...], (8, row_1.shape[1])).T[:, :1]
    bias_2[...] = jnp.broadcast_to(row_2[...], (8, row_2.shape[1])).T[:, :1]
    weight_1[...] = weight_in[...].astype(F32).T.astype(BF16)
    block, member = lax.axis_index("blk"), lax.axis_index("rep")
    for slot in range(slots):
        plan[slot] = lax.clamp(0, columns_in[0, slot] // reps, blocks - 1) ^ block
        local = rows_in[0, slot] - block * reps
        step = lax.rem(local - member + reps, reps)
        plan[slots + slot] = jnp.where((slot < live[0]) & (local >= 0) & (local < reps), step, -1)
    for copy in copies[5:]:
        copy.wait()


def project(weight_t, *refs):
    *stacks, out = refs
    start = 0
    for stack in stacks:
        for index in range(stack.shape[0]):
            out[start + index] = nn(weight_t[...], stack[index]).astype(BF16)
        start += stack.shape[0]


def turn(tiles, arrived, plan, arrived_out, tiles_t, degrees):
    arrived_out[...] = arrived[...]
    slots, tile = tiles.shape[0], tiles.shape[1]
    count = degrees.shape[0]
    total = jnp.zeros((count * ONES_ROWS, tile), F32)
    for slot in range(slots):
        values = tiles[slot]
        tiles_t[slot] = values.T
        ones = [
            jnp.full((ONES_ROWS, tile), (plan[slots + slot] == step).astype(F32), F32).astype(BF16)
            for step in range(count)
        ]
        total = total + nt(jnp.concatenate(ones, axis=0), values)
    for step in range(count):
        degrees[step] = total[step * ONES_ROWS : step * ONES_ROWS + 8]


def summed(panels, plan, tiles_t, count):
    slots, tile = tiles_t.shape[0], tiles_t.shape[1]
    height = panels.shape[1]
    total = jnp.zeros((count * height, tile), F32)
    for slot in range(slots):
        values = panels[plan[slot]]
        pieces = [
            values * (plan[slots + slot] == step).astype(F32).astype(BF16) for step in range(count)
        ]
        total = total + nn(jnp.concatenate(pieces, axis=0), tiles_t[slot])
    return [total[step * height : (step + 1) * height] for step in range(count)]


def in_thirds(row):
    first = row.astype(BF16).astype(F32)
    second = (row - first).astype(BF16).astype(F32)
    return first, second, row - first - second


def aggregate_hidden(projected, far, weight_t, tiles_t, degrees, plan, own, *rest):
    others, panels = rest[:-1], rest[-1]
    mine, opposite = panel_order(panels.shape[0] // 4, lax.axis_index("blk") % 2)
    for index, place in enumerate(mine):
        panels[place] = projected[index]
    for index, place in enumerate(opposite):
        panels[place] = nn(weight_t[...], far[index]).astype(BF16)
    sums = summed(panels, plan, tiles_t, 1 + len(others))
    own[...] = sums[0]
    row = lax.broadcasted_iota(jnp.int32, (8, own.shape[1]), 0)
    for step, (part, out) in enumerate(zip(sums[1:], others), 1):
        first, second, third = in_thirds(degrees[step])
        terms = jnp.where(row == 0, first, jnp.where(row == 1, second, jnp.where(row == 2, third, 0.0)))
        out[...] = jnp.concatenate([part, terms, jnp.zeros_like(terms)], axis=0).astype(BF16)


def aggregate_classes(near, far, tiles_t, plan, *rest):
    outs, panels = rest[:-1], rest[-1]
    chip = lax.axis_index("blk") // 2
    for index in range(near.shape[0]):
        panels[2 * (index ^ chip)] = near[index]
        panels[2 * (index ^ chip) + 1] = far[index]
    for out, part in zip(outs, summed(panels, plan, tiles_t, len(outs))):
        out[...] = part


def combine(hidden_in, bias, weight_t, degrees, own, *rest):
    *arrived, out, scale_out = rest
    height = hidden_in.shape[1]
    total, degree = own[...], degrees[0, :1]
    for part in arrived:
        values = part[...].astype(F32)
        total = total + values[:height]
        terms = [values[height + index : height + index + 1] for index in range(3)]
        degree = degree + (terms[0] + (terms[1] + terms[2]))
    scaling = lax.rsqrt(1.0 + degree)
    hidden = scaling * (total + hidden_in[0].astype(F32)) + bias[...]
    hidden = jnp.maximum(hidden, 0.0).astype(BF16)
    classes = nn(weight_t[...], hidden)
    blank = jnp.zeros((out.shape[0] - classes.shape[0], classes.shape[1]), F32)
    out[...] = jnp.concatenate([classes, blank], axis=0).astype(BF16)
    scale_out[...] = scaling


def finish(classes_in, scaling, bias, own, *rest):
    *arrived, out = rest
    total = own[...]
    for part in arrived:
        total = total + part[...]
    classes = out.shape[0]
    whole = total + classes_in[...].astype(F32)
    out[...] = scaling[...] * whole[:classes] + bias[...]


def shifted(value, axis, step):
    size = lax.axis_size(axis)
    return lax.ppermute(value, axis, [((d + step) % size, d) for d in range(size)])


def swapped(value, masks):
    return lax.ppermute(value, "blk", [(d ^ masks[d % 2], d) for d in range(lax.axis_size("blk"))])


def outer_order(outer):
    rest = list(range(2, outer))
    return 1, list(zip(rest[0::2], rest[1::2]))


def panel_order(outer, core):
    first, pairs = outer_order(outer)
    lists = []
    for here in (core, 1 - core):
        across = [jnp.where(here == 0, 4 * pair[0], 4 * pair[1]) + e for pair in pairs for e in range(2)]
        lists.append([4 * first, *across, 2, 4 * first + 2, *[apart + 2 for apart in across]])
    return [0, 1, *lists[0]], [apart ^ 1 for apart in lists[1]]


def packed(*parts, after=()):
    def pack(*refs):
        for index in range(len(parts)):
            refs[-1][index] = refs[index][...]

    out = jax.ShapeDtypeStruct((len(parts), *parts[0].shape), BF16)
    return call(pack, [out], vmem=(*parts, *after), cost=1 << 32)[0]


def gather_features(value, aside, later):
    outer = lax.axis_size("blk") // 4
    first, pairs = outer_order(outer)
    other = swapped(value, (1, 1))
    ahead = swapped(value, (4 * first, 4 * first))
    both = jnp.stack([value, other])
    across = [swapped(both, (4 * pair[0], 4 * pair[1])) for pair in pairs]
    across = across[0] if len(across) == 1 else jnp.concatenate(across)
    here = packed(value, ahead)
    over = swapped(here, (2, 2))
    beside = aside(here)
    across = packed(across, after=(beside[1],))[0]
    beyond = swapped(across, (2, 2))
    over, *behind = later(over, beside)
    near = jnp.concatenate([ahead[None], across, over, beyond])
    return (both, near, swapped(near, (1, 1))), beside, behind


def gather_classes(value):
    size = lax.axis_size("blk")
    groups = [list(range(core, size, 2)) for core in range(2)]
    copies = jnp.broadcast_to(value[None], (size // 2, *value.shape))
    near = lax.all_to_all(copies, "blk", 0, 0, axis_index_groups=groups)
    return near, swapped(near, (1, 1))


def body(
    features,
    node_order,
    tile_values,
    tile_rows,
    tile_columns,
    tile_live,
    first_weight,
    first_bias,
    second_weight,
    second_bias,
):
    tile, width = features.shape
    slots = tile_values.shape[1]
    reps = lax.axis_size("rep")
    blocks = lax.axis_size("blk")
    hidden, classes = second_weight.shape
    padded = -(-classes // 16) * 16
    shape = jax.ShapeDtypeStruct

    def exchanged(sums):
        return [shifted(sums[reps - 1 - step], "rep", step) for step in range(1, reps)]

    own_t = features.T
    others = [shifted(own_t, "rep", step) for step in range(1, reps)]
    prepared = call(
        prepare,
        [shape((width, tile), F32), shape((1, tile), jnp.int32)],
        hbm=(node_order, own_t),
        scratch=[
            pltpu.VMEM(node_order.shape, jnp.int32),
            pltpu.VMEM(own_t.shape, BF16),
            pltpu.SemaphoreType.DMA((2,)),
        ],
    )
    (ordered,) = call(arrange, [shape((width, tile), BF16)], vmem=(*prepared, *others))

    def staged(after):
        return call(
            functools.partial(stage, reps),
            [
                shape((2 * slots,), jnp.int32),
                shape((hidden, 1), F32),
                shape((classes, 1), F32),
                shape((hidden, width), BF16),
                shape((classes, hidden), BF16),
                shape(tile_values.shape[1:], BF16),
            ],
            vmem=(after,),
            smem=(tile_live,),
            hbm=(
                tile_rows,
                tile_columns,
                first_bias[None],
                second_bias[None],
                first_weight,
                second_weight.T,
                tile_values[0],
            ),
            scratch=[
                pltpu.SMEM((1, slots), jnp.int32),
                pltpu.SMEM((1, slots), jnp.int32),
                pltpu.VMEM((1, hidden), F32),
                pltpu.VMEM((1, classes), F32),
                pltpu.VMEM(first_weight.shape, BF16),
                pltpu.SemaphoreType.DMA((7,)),
            ],
            smem_outs=1,
        )

    def turned(arrived, values):
        tiles = values[-1]
        return call(
            turn,
            [
                shape(arrived.shape, BF16),
                shape(tiles.shape, BF16),
                shape((reps, 8, tile), F32),
            ],
            vmem=(tiles, arrived),
            smem=(values[0],),
        )

    (both, near, far), values, (tiles, degrees) = gather_features(ordered, staged, turned)
    plan, bias_1, bias_2, weight_1, weight_2, _ = values
    (projected,) = call(
        project,
        [shape((2 + near.shape[0], hidden, tile), BF16)],
        vmem=(weight_1, both, near),
    )
    own, *sums = call(
        aggregate_hidden,
        [shape((hidden, tile), F32)] + [shape((hidden + ONES_ROWS, tile), BF16)] * (reps - 1),
        vmem=(projected, far, weight_1, tiles, degrees),
        smem=(plan,),
        scratch=[pltpu.VMEM((blocks, hidden, tile), BF16)],
    )
    classes_in, scaling = call(
        combine,
        [shape((padded, tile), BF16), shape((1, tile), F32)],
        vmem=(projected, bias_1, weight_2, degrees, own, *exchanged(sums)),
    )
    own, *sums = call(
        aggregate_classes,
        [shape((padded, tile), F32)] * reps,
        vmem=(*gather_classes(classes_in), tiles),
        smem=(plan,),
        scratch=[pltpu.VMEM((blocks, padded, tile), BF16)],
    )
    (logits,) = call(
        finish,
        [shape((classes, tile), F32)],
        vmem=(classes_in, scaling, bias_2, own, *exchanged(sums)),
    )
    return logits.T


def solution(mesh):
    placed = (
        P(("blk", "rep"), None),
        P("blk", None),
        P(("blk", "rep"), None, None, None),
        P(("blk", "rep"), None),
        P(("blk", "rep"), None),
        P(("blk", "rep")),
        P(),
        P(),
        P(),
        P(),
    )
    return jax.shard_map(
        body, mesh=mesh, in_specs=placed, out_specs=P(("blk", "rep"), None), check_vma=False
    )
```

```python
import functools

import jax
import jax.numpy as jnp
from jax import lax
from jax.experimental import pallas as pl
from jax.experimental.pallas import tpu as pltpu
from jax.sharding import PartitionSpec as P

BF16 = jnp.bfloat16
F32 = jnp.float32
ONES_ROWS = 16
VMEM_LIMIT = 32 * 1024 * 1024


def nn(a, b):
    return lax.dot_general(a, b, (((1,), (0,)), ((), ())), preferred_element_type=F32)


def nt(a, b):
    return lax.dot_general(a, b, (((1,), (1,)), ((), ())), preferred_element_type=F32)


def in_smem(value):
    return value if value.size == 1 else pltpu.with_memory_space_constraint(value, pltpu.SMEM)


def call(kernel, outs, smem=(), vmem=(), hbm=(), scratch=(), smem_outs=0, cost=1 << 20):
    spaces = [pltpu.VMEM] * len(vmem) + [pltpu.SMEM] * len(smem) + [pltpu.HBM] * len(hbm)
    out_spaces = [pltpu.SMEM] * smem_outs + [pltpu.VMEM] * (len(outs) - smem_outs)
    return pl.pallas_call(
        kernel,
        out_shape=outs,
        in_specs=[pl.BlockSpec(memory_space=space) for space in spaces],
        out_specs=[pl.BlockSpec(memory_space=space) for space in out_spaces],
        scratch_shapes=scratch,
        compiler_params=pltpu.CompilerParams(vmem_limit_bytes=VMEM_LIMIT),
        cost_estimate=pl.CostEstimate(flops=cost, bytes_accessed=cost, transcendentals=0),
    )(*vmem, *[in_smem(value) for value in smem], *[pltpu.with_memory_space_constraint(value, pltpu.HBM) for value in hbm])


def fetched(sources, targets, sems):
    copies = [
        pltpu.make_async_copy(source, target, sems.at[index])
        for index, (source, target) in enumerate(zip(sources, targets))
    ]
    for copy in copies:
        copy.start()
    return copies


def picked(features, wanted, owner):
    tile = features.shape[1]
    source = lax.broadcasted_iota(jnp.int32, (tile, tile), 0) + owner * tile
    return nn(features[...], jnp.where(source == wanted, 1.0, 0.0).astype(BF16))


def prepare(order, features, tiles, part, wanted_out, tiles_out, *rest):
    order_in, features_in, sems = rest
    copies = fetched((order, features, tiles), (order_in, features_in, tiles_out), sems)
    for copy in copies[:2]:
        copy.wait()
    tile = features.shape[1]
    member = lax.axis_index("rep")
    wanted = order_in[:, pl.ds(pl.multiple_of(member * tile, tile), tile)]
    wanted_out[...] = wanted
    part[...] = picked(features_in, wanted, member)
    copies[2].wait()


def arrange(part, wanted, *rest):
    *features, out = rest
    reps = len(features) + 1
    member = lax.axis_index("rep")
    total = part[...]
    for step in range(1, reps):
        owner = lax.rem(member + step, reps)
        total = total + picked(features[step - 1], wanted[...], owner)
    out[...] = total.astype(BF16)


def stage(reps, _, live, *refs):
    sources, (plan, bias_1, bias_2, weight_1, weight_2), scratch = refs[:6], refs[6:11], refs[11:]
    rows_in, columns_in, row_1, row_2, weight_in, sems = scratch
    slots = rows_in.shape[1]
    blocks = lax.axis_size("blk")
    for copy in fetched(sources, (rows_in, columns_in, row_1, row_2, weight_in, weight_2), sems):
        copy.wait()
    bias_1[...] = jnp.broadcast_to(row_1[...], (8, row_1.shape[1])).T[:, :1]
    bias_2[...] = jnp.broadcast_to(row_2[...], (8, row_2.shape[1])).T[:, :1]
    weight_1[...] = weight_in[...].astype(F32).T.astype(BF16)
    block, member = lax.axis_index("blk"), lax.axis_index("rep")
    for slot in range(slots):
        plan[slot] = lax.clamp(0, columns_in[0, slot] // reps, blocks - 1) ^ block
        local = rows_in[0, slot] - block * reps
        step = lax.rem(local - member + reps, reps)
        plan[slots + slot] = jnp.where((slot < live[0]) & (local >= 0) & (local < reps), step, -1)


def project(weight_t, stack, out):
    for index in range(stack.shape[0]):
        out[index] = nn(weight_t[...], stack[index]).astype(BF16)


def turn(tiles, arrived, plan, arrived_out, tiles_t, degrees):
    arrived_out[...] = arrived[...]
    slots, tile = tiles.shape[0], tiles.shape[1]
    count = degrees.shape[0]
    total = jnp.zeros((count * ONES_ROWS, tile), F32)
    for slot in range(slots):
        values = tiles[slot]
        tiles_t[slot] = values.T
        ones = [
            jnp.full((ONES_ROWS, tile), (plan[slots + slot] == step).astype(F32), F32).astype(BF16)
            for step in range(count)
        ]
        total = total + nt(jnp.concatenate(ones, axis=0), values)
    for step in range(count):
        degrees[step] = total[step * ONES_ROWS : step * ONES_ROWS + 8]


def summed(panels, plan, tiles_t, count):
    slots, tile = tiles_t.shape[0], tiles_t.shape[1]
    height = panels.shape[1]
    total = jnp.zeros((count * height, tile), F32)
    for slot in range(slots):
        values = panels[plan[slot]]
        pieces = [
            values * (plan[slots + slot] == step).astype(F32).astype(BF16) for step in range(count)
        ]
        total = total + nn(jnp.concatenate(pieces, axis=0), tiles_t[slot])
    return [total[step * height : (step + 1) * height] for step in range(count)]


def in_thirds(row):
    first = row.astype(BF16).astype(F32)
    second = (row - first).astype(BF16).astype(F32)
    return first, second, row - first - second


def aggregate_hidden(projected, far, weight_t, tiles_t, degrees, plan, own, *rest):
    others, panels = rest[:-1], rest[-1]
    mine, opposite = panel_order(panels.shape[0] // 4, lax.axis_index("blk") % 2)
    for index, place in enumerate(mine):
        panels[place] = projected[index]
    for index, place in enumerate(opposite):
        panels[place] = nn(weight_t[...], far[index]).astype(BF16)
    sums = summed(panels, plan, tiles_t, 1 + len(others))
    own[...] = sums[0]
    row = lax.broadcasted_iota(jnp.int32, (8, own.shape[1]), 0)
    for step, (part, out) in enumerate(zip(sums[1:], others), 1):
        first, second, third = in_thirds(degrees[step])
        terms = jnp.where(row == 0, first, jnp.where(row == 1, second, jnp.where(row == 2, third, 0.0)))
        out[...] = jnp.concatenate([part, terms, jnp.zeros_like(terms)], axis=0).astype(BF16)


def aggregate_classes(near, far, tiles_t, plan, *rest):
    outs, panels = rest[:-1], rest[-1]
    chip = lax.axis_index("blk") // 2
    for index in range(near.shape[0]):
        panels[2 * (index ^ chip)] = near[index]
        panels[2 * (index ^ chip) + 1] = far[index]
    for out, part in zip(outs, summed(panels, plan, tiles_t, len(outs))):
        out[...] = part


def combine(hidden_in, bias, weight_t, degrees, own, *rest):
    *arrived, out, scale_out = rest
    height = hidden_in.shape[1]
    total, degree = own[...], degrees[0, :1]
    for part in arrived:
        values = part[...].astype(F32)
        total = total + values[:height]
        terms = [values[height + index : height + index + 1] for index in range(3)]
        degree = degree + (terms[0] + (terms[1] + terms[2]))
    scaling = lax.rsqrt(1.0 + degree)
    hidden = scaling * (total + hidden_in[0].astype(F32)) + bias[...]
    hidden = jnp.maximum(hidden, 0.0).astype(BF16)
    classes = nn(weight_t[...], hidden)
    blank = jnp.zeros((out.shape[0] - classes.shape[0], classes.shape[1]), F32)
    out[...] = jnp.concatenate([classes, blank], axis=0).astype(BF16)
    scale_out[...] = scaling


def finish(classes_in, scaling, bias, own, *rest):
    *arrived, out = rest
    total = own[...]
    for part in arrived:
        total = total + part[...]
    classes = out.shape[0]
    whole = total + classes_in[...].astype(F32)
    out[...] = scaling[...] * whole[:classes] + bias[...]


def shifted(value, axis, step):
    size = lax.axis_size(axis)
    return lax.ppermute(value, axis, [((d + step) % size, d) for d in range(size)])


def swapped(value, masks):
    return lax.ppermute(value, "blk", [(d ^ masks[d % 2], d) for d in range(lax.axis_size("blk"))])


def outer_order(outer):
    rest = list(range(2, outer))
    return 1, list(zip(rest[0::2], rest[1::2]))


def two_ways(pairs):
    return pairs + [(pair[1], pair[0]) for pair in pairs]


def panel_order(outer, core):
    first, pairs = outer_order(outer)
    lists = []
    for here in (core, 1 - core):
        across = [jnp.where(here == 0, *sides) for sides in two_ways(pairs)]
        across = [4 * first, *[4 * apart for apart in across]]
        lists.append([0, *across, 2, *[apart + 2 for apart in across]])
    return lists[0], [apart ^ 1 for apart in lists[1]]


def packed(*parts):
    def pack(*refs):
        for index in range(len(parts)):
            refs[-1][index] = refs[index][...]

    out = jax.ShapeDtypeStruct((len(parts), *parts[0].shape), BF16)
    return call(pack, [out], vmem=parts)[0]


def gather_features(value, aside, later):
    outer = lax.axis_size("blk") // 4
    first, pairs = outer_order(outer)
    ahead = swapped(value, (4 * first, 4 * first))
    across = [swapped(value, (4 * sides[0], 4 * sides[1])) for sides in two_ways(pairs)]
    here = packed(value, ahead)
    over = swapped(here, (2, 2))
    early, late = packed(*across[: len(pairs)]), packed(*across[len(pairs) :])
    beyond = [swapped(early, (2, 2)), swapped(late, (2, 2))]
    beside = aside(over)
    over, *behind = later(over, beside)
    near = jnp.concatenate([here, early, late, over, *beyond])
    return (near, swapped(near, (1, 1))), beside, behind


def gather_classes(value):
    size = lax.axis_size("blk")
    groups = [list(range(core, size, 2)) for core in range(2)]
    copies = jnp.broadcast_to(value[None], (size // 2, *value.shape))
    near = lax.all_to_all(copies, "blk", 0, 0, axis_index_groups=groups)
    return near, swapped(near, (1, 1))


def body(
    features,
    node_order,
    tile_values,
    tile_rows,
    tile_columns,
    tile_live,
    first_weight,
    first_bias,
    second_weight,
    second_bias,
):
    tile, width = features.shape
    slots = tile_values.shape[1]
    reps = lax.axis_size("rep")
    blocks = lax.axis_size("blk")
    hidden, classes = second_weight.shape
    padded = -(-classes // 16) * 16
    shape = jax.ShapeDtypeStruct

    def exchanged(sums):
        return [shifted(sums[reps - 1 - step], "rep", step) for step in range(1, reps)]

    own_t = features.T
    others = [shifted(own_t, "rep", step) for step in range(1, reps)]
    part, wanted, tiles = call(
        prepare,
        [
            shape((width, tile), F32),
            shape((1, tile), jnp.int32),
            shape(tile_values.shape[1:], BF16),
        ],
        hbm=(node_order, own_t, tile_values[0]),
        scratch=[
            pltpu.VMEM(node_order.shape, jnp.int32),
            pltpu.VMEM(own_t.shape, BF16),
            pltpu.SemaphoreType.DMA((3,)),
        ],
    )
    (ordered,) = call(arrange, [shape((width, tile), BF16)], vmem=(part, wanted, *others))

    def staged(after):
        return call(
            functools.partial(stage, reps),
            [
                pltpu.SMEM((2 * slots,), jnp.int32),
                shape((hidden, 1), F32),
                shape((classes, 1), F32),
                shape((hidden, width), BF16),
                shape((classes, hidden), BF16),
            ],
            vmem=(after,),
            smem=(tile_live,),
            hbm=(
                tile_rows,
                tile_columns,
                first_bias[None],
                second_bias[None],
                first_weight,
                second_weight.T,
            ),
            scratch=[
                pltpu.SMEM((1, slots), jnp.int32),
                pltpu.SMEM((1, slots), jnp.int32),
                pltpu.VMEM((1, hidden), F32),
                pltpu.VMEM((1, classes), F32),
                pltpu.VMEM(first_weight.shape, BF16),
                pltpu.SemaphoreType.DMA((6,)),
            ],
            smem_outs=1,
        )

    def turned(arrived, values):
        return call(
            turn,
            [
                shape(arrived.shape, BF16),
                shape(tiles.shape, BF16),
                shape((reps, 8, tile), F32),
            ],
            vmem=(tiles, arrived),
            smem=(values[0],),
        )

    (near, far), values, (tiles_t, degrees) = gather_features(ordered, staged, turned)
    plan, bias_1, bias_2, weight_1, weight_2 = values
    (projected,) = call(
        project,
        [shape((near.shape[0], hidden, tile), BF16)],
        vmem=(weight_1, near),
    )
    own, *sums = call(
        aggregate_hidden,
        [shape((hidden, tile), F32)] + [shape((hidden + ONES_ROWS, tile), BF16)] * (reps - 1),
        vmem=(projected, far, weight_1, tiles_t, degrees),
        smem=(plan,),
        scratch=[pltpu.VMEM((blocks, hidden, tile), BF16)],
    )
    classes_in, scaling = call(
        combine,
        [shape((padded, tile), BF16), shape((1, tile), F32)],
        vmem=(projected, bias_1, weight_2, degrees, own, *exchanged(sums)),
    )
    own, *sums = call(
        aggregate_classes,
        [shape((padded, tile), F32)] * reps,
        vmem=(*gather_classes(classes_in), tiles_t),
        smem=(plan,),
        scratch=[pltpu.VMEM((blocks, padded, tile), BF16)],
    )
    (logits,) = call(
        finish,
        [shape((classes, tile), F32)],
        vmem=(classes_in, scaling, bias_2, own, *exchanged(sums)),
    )
    return logits.T


def solution(mesh):
    placed = (
        P(("blk", "rep"), None),
        P("blk", None),
        P(("blk", "rep"), None, None, None),
        P(("blk", "rep"), None),
        P(("blk", "rep"), None),
        P(("blk", "rep")),
        P(),
        P(),
        P(),
        P(),
    )
    return jax.shard_map(
        body, mesh=mesh, in_specs=placed, out_specs=P(("blk", "rep"), None), check_vma=False
    )
```

```python
import functools

import jax
import jax.numpy as jnp
from jax import lax
from jax.experimental import pallas as pl
from jax.experimental.pallas import tpu as pltpu
from jax.sharding import PartitionSpec as P

BF16 = jnp.bfloat16
F32 = jnp.float32
ONES_ROWS = 16
VMEM_LIMIT = 32 * 1024 * 1024


def nn(a, b):
    return lax.dot_general(a, b, (((1,), (0,)), ((), ())), preferred_element_type=F32)


def nt(a, b):
    return lax.dot_general(a, b, (((1,), (1,)), ((), ())), preferred_element_type=F32)


def in_smem(value):
    return value if value.size == 1 else pltpu.with_memory_space_constraint(value, pltpu.SMEM)


def call(kernel, outs, smem=(), vmem=(), hbm=(), scratch=(), smem_outs=0, cost=1 << 20):
    spaces = [pltpu.VMEM] * len(vmem) + [pltpu.SMEM] * len(smem) + [pltpu.HBM] * len(hbm)
    out_spaces = [pltpu.SMEM] * smem_outs + [pltpu.VMEM] * (len(outs) - smem_outs)
    return pl.pallas_call(
        kernel,
        out_shape=outs,
        in_specs=[pl.BlockSpec(memory_space=space) for space in spaces],
        out_specs=[pl.BlockSpec(memory_space=space) for space in out_spaces],
        scratch_shapes=scratch,
        compiler_params=pltpu.CompilerParams(vmem_limit_bytes=VMEM_LIMIT),
        cost_estimate=pl.CostEstimate(flops=cost, bytes_accessed=cost, transcendentals=0),
    )(*vmem, *[in_smem(value) for value in smem], *[pltpu.with_memory_space_constraint(value, pltpu.HBM) for value in hbm])


def fetched(sources, targets, sems):
    copies = [
        pltpu.make_async_copy(source, target, sems.at[index])
        for index, (source, target) in enumerate(zip(sources, targets))
    ]
    for copy in copies:
        copy.start()
    return copies


def picked(features, wanted, owner):
    tile = features.shape[1]
    source = lax.broadcasted_iota(jnp.int32, (tile, tile), 0) + owner * tile
    return nn(features[...], jnp.where(source == wanted, 1.0, 0.0).astype(BF16))


def prepare(live, order, features, tiles, live_out, part, wanted_out, tiles_out, *rest):
    live_out[0] = live[0]
    order_in, features_in, sems = rest
    copies = fetched((order, features, tiles), (order_in, features_in, tiles_out), sems)
    for copy in copies[:2]:
        copy.wait()
    tile = features.shape[1]
    member = lax.axis_index("rep")
    wanted = order_in[:, pl.ds(pl.multiple_of(member * tile, tile), tile)]
    wanted_out[...] = wanted
    part[...] = picked(features_in, wanted, member)
    copies[2].wait()


def arrange(part, wanted, *rest):
    *features, out = rest
    reps = len(features) + 1
    member = lax.axis_index("rep")
    total = part[...]
    for step in range(1, reps):
        owner = lax.rem(member + step, reps)
        total = total + picked(features[step - 1], wanted[...], owner)
    out[...] = total.astype(BF16)


def stage(reps, _, live, *refs):
    sources, (plan, bias_1, bias_2, weight_1, weight_2), scratch = refs[:6], refs[6:11], refs[11:]
    rows_in, columns_in, row_1, row_2, weight_in, sems = scratch
    slots = rows_in.shape[1]
    blocks = lax.axis_size("blk")
    for copy in fetched(sources, (rows_in, columns_in, row_1, row_2, weight_in, weight_2), sems):
        copy.wait()
    bias_1[...] = jnp.broadcast_to(row_1[...], (8, row_1.shape[1])).T[:, :1]
    bias_2[...] = jnp.broadcast_to(row_2[...], (8, row_2.shape[1])).T[:, :1]
    weight_1[...] = weight_in[...].astype(F32).T.astype(BF16)
    block, member = lax.axis_index("blk"), lax.axis_index("rep")
    for slot in range(slots):
        plan[slot] = lax.clamp(0, columns_in[0, slot] // reps, blocks - 1) ^ block
        local = rows_in[0, slot] - block * reps
        step = lax.rem(local - member + reps, reps)
        plan[slots + slot] = jnp.where((slot < live[0]) & (local >= 0) & (local < reps), step, -1)


def project(weight_t, stack, out):
    for index in range(stack.shape[0]):
        out[index] = nn(weight_t[...], stack[index]).astype(BF16)


def turn(tiles, arrived, plan, arrived_out, tiles_t, degrees):
    arrived_out[...] = arrived[...]
    slots, tile = tiles.shape[0], tiles.shape[1]
    count = degrees.shape[0]
    total = jnp.zeros((count * ONES_ROWS, tile), F32)
    for slot in range(slots):
        values = tiles[slot]
        tiles_t[slot] = values.T
        ones = [
            jnp.full((ONES_ROWS, tile), (plan[slots + slot] == step).astype(F32), F32).astype(BF16)
            for step in range(count)
        ]
        total = total + nt(jnp.concatenate(ones, axis=0), values)
    for step in range(count):
        degrees[step] = total[step * ONES_ROWS : step * ONES_ROWS + 8]


def summed(panels, plan, tiles_t, count):
    slots, tile = tiles_t.shape[0], tiles_t.shape[1]
    height = panels.shape[1]
    total = jnp.zeros((count * height, tile), F32)
    for slot in range(slots):
        values = panels[plan[slot]]
        pieces = [
            values * (plan[slots + slot] == step).astype(F32).astype(BF16) for step in range(count)
        ]
        total = total + nn(jnp.concatenate(pieces, axis=0), tiles_t[slot])
    return [total[step * height : (step + 1) * height] for step in range(count)]


def coded(values):
    top = jnp.max(jnp.abs(values), axis=0, keepdims=True)
    power = jnp.ceil(jnp.log2(jnp.maximum(top, 1e-30)))
    return jnp.round(values * jnp.exp2(14.0 - power)).astype(jnp.int32), power.astype(jnp.int32)


def decoded(codes, power):
    return codes.astype(F32) * jnp.exp2(power.astype(F32) - 14.0)


def in_thirds(row):
    first = jnp.floor(row)
    second = jnp.floor((row - first) * 16384.0)
    third = jnp.round(((row - first) * 16384.0 - second) * 16384.0)
    return [part.astype(jnp.int32) for part in (first, second, third)]


def aggregate_hidden(projected, far, weight_t, tiles_t, degrees, plan, own, *rest):
    others, panels = rest[:-1], rest[-1]
    mine, opposite = panel_order(panels.shape[0] // 4, lax.axis_index("blk") % 2)
    for index, place in enumerate(mine):
        panels[place] = projected[index]
    for index, place in enumerate(opposite):
        panels[place] = nn(weight_t[...], far[index]).astype(BF16)
    sums = summed(panels, plan, tiles_t, 1 + len(others))
    own[...] = sums[0]
    row = lax.broadcasted_iota(jnp.int32, (ONES_ROWS, own.shape[1]), 0)
    for step, (part, out) in enumerate(zip(sums[1:], others), 1):
        codes, power = coded(part)
        terms = jnp.zeros(row.shape, jnp.int32)
        for index, term in enumerate([power, *in_thirds(degrees[step, :1])]):
            terms = jnp.where(row == index, term, terms)
        out[...] = jnp.concatenate([codes, terms], axis=0).astype(jnp.int16)


def aggregate_classes(near, far, tiles_t, plan, own, *rest):
    others, panels = rest[:-1], rest[-1]
    chip = lax.axis_index("blk") // 2
    for index in range(near.shape[0]):
        panels[2 * (index ^ chip)] = near[index]
        panels[2 * (index ^ chip) + 1] = far[index]
    sums = summed(panels, plan, tiles_t, 1 + len(others))
    own[...] = sums[0]
    row = lax.broadcasted_iota(jnp.int32, own.shape, 0)
    for part, out in zip(sums[1:], others):
        codes, power = coded(part)
        out[...] = jnp.where(row == own.shape[0] - 1, power, codes).astype(jnp.int16)


def combine(hidden_in, bias, weight_t, degrees, own, *rest):
    *arrived, out, scale_out = rest
    height = hidden_in.shape[1]
    total, degree = own[...], degrees[0, :1]
    for part in arrived:
        codes = part[...].astype(jnp.int32)
        total = total + decoded(codes[:height], codes[height : height + 1])
        terms = [codes[height + 1 + index : height + 2 + index].astype(F32) for index in range(3)]
        degree = degree + (terms[0] + (terms[1] + terms[2] * 2.0**-14) * 2.0**-14)
    scaling = lax.rsqrt(1.0 + degree)
    hidden = scaling * (total + hidden_in[0].astype(F32)) + bias[...]
    hidden = jnp.maximum(hidden, 0.0).astype(BF16)
    classes = nn(weight_t[...], hidden)
    blank = jnp.zeros((out.shape[0] - classes.shape[0], classes.shape[1]), F32)
    out[...] = jnp.concatenate([classes, blank], axis=0).astype(BF16)
    scale_out[...] = scaling


def finish(classes_in, scaling, bias, own, *rest):
    *arrived, out = rest
    classes = out.shape[0]
    total = own[...]
    for part in arrived:
        codes = part[...].astype(jnp.int32)
        total = total + decoded(codes, codes[-1:])
    whole = total + classes_in[...].astype(F32)
    out[...] = scaling[...] * whole[:classes] + bias[...]


def shifted(value, axis, step):
    size = lax.axis_size(axis)
    return lax.ppermute(value, axis, [((d + step) % size, d) for d in range(size)])


def swapped(value, masks):
    return lax.ppermute(value, "blk", [(d ^ masks[d % 2], d) for d in range(lax.axis_size("blk"))])


def outer_order(outer):
    rest = list(range(2, outer))
    return 1, list(zip(rest[0::2], rest[1::2]))


def two_ways(pairs):
    return pairs + [(pair[1], pair[0]) for pair in pairs]


def panel_order(outer, core):
    first, pairs = outer_order(outer)
    lists = []
    for here in (core, 1 - core):
        across = [jnp.where(here == 0, *sides) for sides in two_ways(pairs)]
        across = [4 * first, *[4 * apart for apart in across]]
        lists.append([0, *across, 2, *[apart + 2 for apart in across]])
    return lists[0], [apart ^ 1 for apart in lists[1]]


def packed(*parts):
    def pack(*refs):
        for index in range(len(parts)):
            refs[-1][index] = refs[index][...]

    out = jax.ShapeDtypeStruct((len(parts), *parts[0].shape), BF16)
    return call(pack, [out], vmem=parts)[0]


def gather_features(value, aside, later):
    outer = lax.axis_size("blk") // 4
    first, pairs = outer_order(outer)
    ahead = swapped(value, (4 * first, 4 * first))
    across = [swapped(value, (4 * sides[0], 4 * sides[1])) for sides in two_ways(pairs)]
    here = packed(value, ahead)
    over = swapped(here, (2, 2))
    early, late = packed(*across[: len(pairs)]), packed(*across[len(pairs) :])
    beyond = [swapped(early, (2, 2)), swapped(late, (2, 2))]
    beside = aside(over)
    over, *behind = later(over, beside)
    near = jnp.concatenate([here, early, late, over, *beyond])
    return (near, swapped(near, (1, 1))), beside, behind


def gather_classes(value):
    size = lax.axis_size("blk")
    groups = [list(range(core, size, 2)) for core in range(2)]
    copies = jnp.broadcast_to(value[None], (size // 2, *value.shape))
    near = lax.all_to_all(copies, "blk", 0, 0, axis_index_groups=groups)
    return near, swapped(near, (1, 1))


def body(
    features,
    node_order,
    tile_values,
    tile_rows,
    tile_columns,
    tile_live,
    first_weight,
    first_bias,
    second_weight,
    second_bias,
):
    tile, width = features.shape
    slots = tile_values.shape[1]
    reps = lax.axis_size("rep")
    blocks = lax.axis_size("blk")
    hidden, classes = second_weight.shape
    padded = -(-(classes + 1) // 16) * 16
    shape = jax.ShapeDtypeStruct

    def exchanged(sums):
        return [shifted(sums[reps - 1 - step], "rep", step) for step in range(1, reps)]

    own_t = features.T
    others = [shifted(own_t, "rep", step) for step in range(1, reps)]
    live, part, wanted, tiles = call(
        prepare,
        [
            pltpu.SMEM((8,), jnp.int32),
            shape((width, tile), F32),
            shape((1, tile), jnp.int32),
            shape(tile_values.shape[1:], BF16),
        ],
        smem=(tile_live,),
        hbm=(node_order, own_t, tile_values[0]),
        scratch=[
            pltpu.VMEM(node_order.shape, jnp.int32),
            pltpu.VMEM(own_t.shape, BF16),
            pltpu.SemaphoreType.DMA((3,)),
        ],
        smem_outs=1,
    )
    (ordered,) = call(arrange, [shape((width, tile), BF16)], vmem=(part, wanted, *others))

    def staged(after):
        return call(
            functools.partial(stage, reps),
            [
                pltpu.SMEM((2 * slots,), jnp.int32),
                shape((hidden, 1), F32),
                shape((classes, 1), F32),
                shape((hidden, width), BF16),
                shape((classes, hidden), BF16),
            ],
            vmem=(after,),
            smem=(live,),
            hbm=(
                tile_rows,
                tile_columns,
                first_bias[None],
                second_bias[None],
                first_weight,
                second_weight.T,
            ),
            scratch=[
                pltpu.SMEM((1, slots), jnp.int32),
                pltpu.SMEM((1, slots), jnp.int32),
                pltpu.VMEM((1, hidden), F32),
                pltpu.VMEM((1, classes), F32),
                pltpu.VMEM(first_weight.shape, BF16),
                pltpu.SemaphoreType.DMA((6,)),
            ],
            smem_outs=1,
        )

    def turned(arrived, values):
        return call(
            turn,
            [
                shape(arrived.shape, BF16),
                shape(tiles.shape, BF16),
                shape((reps, 8, tile), F32),
            ],
            vmem=(tiles, arrived),
            smem=(values[0],),
        )

    (near, far), values, (tiles_t, degrees) = gather_features(ordered, staged, turned)
    plan, bias_1, bias_2, weight_1, weight_2 = values
    (projected,) = call(
        project,
        [shape((near.shape[0], hidden, tile), BF16)],
        vmem=(weight_1, near),
    )
    own, *sums = call(
        aggregate_hidden,
        [shape((hidden, tile), F32)] + [shape((hidden + ONES_ROWS, tile), jnp.int16)] * (reps - 1),
        vmem=(projected, far, weight_1, tiles_t, degrees),
        smem=(plan,),
        scratch=[pltpu.VMEM((blocks, hidden, tile), BF16)],
    )
    classes_in, scaling = call(
        combine,
        [shape((padded, tile), BF16), shape((1, tile), F32)],
        vmem=(projected, bias_1, weight_2, degrees, own, *exchanged(sums)),
    )
    own, *sums = call(
        aggregate_classes,
        [shape((padded, tile), F32)] + [shape((padded, tile), jnp.int16)] * (reps - 1),
        vmem=(*gather_classes(classes_in), tiles_t),
        smem=(plan,),
        scratch=[pltpu.VMEM((blocks, padded, tile), BF16)],
    )
    (logits,) = call(
        finish,
        [shape((classes, tile), F32)],
        vmem=(classes_in, scaling, bias_2, own, *exchanged(sums)),
    )
    return logits.T


def solution(mesh):
    placed = (
        P(("blk", "rep"), None),
        P("blk", None),
        P(("blk", "rep"), None, None, None),
        P(("blk", "rep"), None),
        P(("blk", "rep"), None),
        P(("blk", "rep")),
        P(),
        P(),
        P(),
        P(),
    )
    return jax.shard_map(
        body, mesh=mesh, in_specs=placed, out_specs=P(("blk", "rep"), None), check_vma=False
    )
```

```python
import functools

import jax
import jax.numpy as jnp
from jax import lax
from jax.experimental import pallas as pl
from jax.experimental.pallas import tpu as pltpu
from jax.sharding import PartitionSpec as P

BF16 = jnp.bfloat16
F32 = jnp.float32
ONES_ROWS = 16
VMEM_LIMIT = 32 * 1024 * 1024


def nn(a, b):
    return lax.dot_general(a, b, (((1,), (0,)), ((), ())), preferred_element_type=F32)


def nt(a, b):
    return lax.dot_general(a, b, (((1,), (1,)), ((), ())), preferred_element_type=F32)


def in_smem(value):
    return value if value.size == 1 else pltpu.with_memory_space_constraint(value, pltpu.SMEM)


def call(kernel, outs, smem=(), vmem=(), hbm=(), scratch=(), smem_outs=0, cost=1 << 20):
    spaces = [pltpu.VMEM] * len(vmem) + [pltpu.SMEM] * len(smem) + [pltpu.HBM] * len(hbm)
    out_spaces = [pltpu.SMEM] * smem_outs + [pltpu.VMEM] * (len(outs) - smem_outs)
    return pl.pallas_call(
        kernel,
        out_shape=outs,
        in_specs=[pl.BlockSpec(memory_space=space) for space in spaces],
        out_specs=[pl.BlockSpec(memory_space=space) for space in out_spaces],
        scratch_shapes=scratch,
        compiler_params=pltpu.CompilerParams(vmem_limit_bytes=VMEM_LIMIT),
        cost_estimate=pl.CostEstimate(flops=cost, bytes_accessed=cost, transcendentals=0),
    )(*vmem, *[in_smem(value) for value in smem], *[pltpu.with_memory_space_constraint(value, pltpu.HBM) for value in hbm])


def fetched(sources, targets, sems):
    copies = [
        pltpu.make_async_copy(source, target, sems.at[index])
        for index, (source, target) in enumerate(zip(sources, targets))
    ]
    for copy in copies:
        copy.start()
    return copies


def picked(features, wanted, owner):
    tile = features.shape[1]
    source = lax.broadcasted_iota(jnp.int32, (tile, tile), 0) + owner * tile
    return nn(features[...], jnp.where(source == wanted, 1.0, 0.0).astype(BF16))


def prepare(live, order, features, tiles, live_out, part, wanted_out, tiles_out, *rest):
    live_out[0] = live[0]
    order_in, features_in, sems = rest
    copies = fetched((order, features, tiles), (order_in, features_in, tiles_out), sems)
    for copy in copies[:2]:
        copy.wait()
    tile = features.shape[1]
    member = lax.axis_index("rep")
    wanted = order_in[:, pl.ds(pl.multiple_of(member * tile, tile), tile)]
    wanted_out[...] = wanted
    part[...] = picked(features_in, wanted, member)
    copies[2].wait()


def arrange(part, wanted, *rest):
    *features, out = rest
    reps = len(features) + 1
    member = lax.axis_index("rep")
    total = part[...]
    for step in range(1, reps):
        owner = lax.rem(member + step, reps)
        total = total + picked(features[step - 1], wanted[...], owner)
    out[...] = total.astype(BF16)


def stage(reps, _, live, *refs):
    sources, (plan, bias_1, bias_2, weight_1, weight_2), scratch = refs[:6], refs[6:11], refs[11:]
    rows_in, columns_in, row_1, row_2, weight_in, sems = scratch
    slots = rows_in.shape[1]
    blocks = lax.axis_size("blk")
    for copy in fetched(sources, (rows_in, columns_in, row_1, row_2, weight_in, weight_2), sems):
        copy.wait()
    bias_1[...] = jnp.broadcast_to(row_1[...], (8, row_1.shape[1])).T[:, :1]
    bias_2[...] = jnp.broadcast_to(row_2[...], (8, row_2.shape[1])).T[:, :1]
    weight_1[...] = weight_in[...].astype(F32).T.astype(BF16)
    block, member = lax.axis_index("blk"), lax.axis_index("rep")
    for slot in range(slots):
        plan[slot] = lax.clamp(0, columns_in[0, slot] // reps, blocks - 1) ^ block
        local = rows_in[0, slot] - block * reps
        step = lax.rem(local - member + reps, reps)
        plan[slots + slot] = jnp.where((slot < live[0]) & (local >= 0) & (local < reps), step, -1)


def project(weight_t, stack, out):
    for index in range(stack.shape[0]):
        out[index] = nn(weight_t[...], stack[index]).astype(BF16)


def turn(tiles, arrived, plan, arrived_out, tiles_t, degrees):
    arrived_out[...] = arrived[...]
    slots, tile = tiles.shape[0], tiles.shape[1]
    count = degrees.shape[0]
    total = jnp.zeros((count * ONES_ROWS, tile), F32)
    for slot in range(slots):
        values = tiles[slot]
        tiles_t[slot] = values.T
        ones = [
            jnp.full((ONES_ROWS, tile), (plan[slots + slot] == step).astype(F32), F32).astype(BF16)
            for step in range(count)
        ]
        total = total + nt(jnp.concatenate(ones, axis=0), values)
    for step in range(count):
        degrees[step] = total[step * ONES_ROWS : step * ONES_ROWS + 8]


def summed(panels, plan, tiles_t, count):
    slots, tile = tiles_t.shape[0], tiles_t.shape[1]
    height = panels.shape[1]
    total = jnp.zeros((count * height, tile), F32)
    for slot in range(slots):
        values = panels[plan[slot]]
        pieces = [
            values * (plan[slots + slot] == step).astype(F32).astype(BF16) for step in range(count)
        ]
        total = total + nn(jnp.concatenate(pieces, axis=0), tiles_t[slot])
    return [total[step * height : (step + 1) * height] for step in range(count)]


def coded(values):
    top = jnp.max(jnp.abs(values), axis=0, keepdims=True)
    power = jnp.ceil(jnp.log2(jnp.maximum(top, 1e-30)))
    return jnp.round(values * jnp.exp2(14.0 - power)).astype(jnp.int32), power.astype(jnp.int32)


def decoded(codes, power):
    return codes.astype(F32) * jnp.exp2(power.astype(F32) - 14.0)


def in_thirds(row):
    first = jnp.floor(row)
    second = jnp.floor((row - first) * 16384.0)
    third = jnp.round(((row - first) * 16384.0 - second) * 16384.0)
    return [part.astype(jnp.int32) for part in (first, second, third)]


def aggregate_hidden(projected, far, weight_t, tiles_t, degrees, plan, own, *rest):
    others, panels = rest[:-1], rest[-1]
    mine, opposite = panel_order(panels.shape[0] // 4, lax.axis_index("blk") % 2)
    for index, place in enumerate(mine):
        panels[place] = projected[index]
    for index, place in enumerate(opposite):
        panels[place] = nn(weight_t[...], far[index]).astype(BF16)
    sums = summed(panels, plan, tiles_t, 1 + len(others))
    own[...] = sums[0]
    row = lax.broadcasted_iota(jnp.int32, (ONES_ROWS, own.shape[1]), 0)
    for step, (part, out) in enumerate(zip(sums[1:], others), 1):
        codes, power = coded(part)
        terms = jnp.zeros(row.shape, jnp.int32)
        for index, term in enumerate([power, *in_thirds(degrees[step, :1])]):
            terms = jnp.where(row == index, term, terms)
        out[...] = jnp.concatenate([codes, terms], axis=0).astype(jnp.int16)


def aggregate_classes(near, far, tiles_t, plan, own, *rest):
    others, panels = rest[:-1], rest[-1]
    chip = lax.axis_index("blk") // 2
    for index in range(near.shape[0]):
        panels[2 * (index ^ chip)] = near[index]
        panels[2 * (index ^ chip) + 1] = far[index]
    sums = summed(panels, plan, tiles_t, 1 + len(others))
    own[...] = sums[0]
    row = lax.broadcasted_iota(jnp.int32, own.shape, 0)
    for part, out in zip(sums[1:], others):
        codes, power = coded(part)
        out[...] = jnp.where(row == own.shape[0] - 1, power, codes).astype(jnp.int16)


def combine(hidden_in, bias, weight_t, degrees, own, *rest):
    *arrived, out, scale_out = rest
    height = hidden_in.shape[1]
    total, degree = own[...], degrees[0, :1]
    for part in arrived:
        codes = part[...].astype(jnp.int32)
        total = total + decoded(codes[:height], codes[height : height + 1])
        terms = [codes[height + 1 + index : height + 2 + index].astype(F32) for index in range(3)]
        degree = degree + (terms[0] + (terms[1] + terms[2] * 2.0**-14) * 2.0**-14)
    scaling = lax.rsqrt(1.0 + degree)
    hidden = scaling * (total + hidden_in[0].astype(F32)) + bias[...]
    hidden = jnp.maximum(hidden, 0.0).astype(BF16)
    classes = nn(weight_t[...], hidden)
    blank = jnp.zeros((out.shape[0] - classes.shape[0], classes.shape[1]), F32)
    out[...] = jnp.concatenate([classes, blank], axis=0).astype(BF16)
    scale_out[...] = scaling


def finish(classes_in, scaling, bias, own, *rest):
    *arrived, out = rest
    classes = out.shape[0]
    total = own[...]
    for part in arrived:
        codes = part[...].astype(jnp.int32)
        total = total + decoded(codes, codes[-1:])
    whole = total + classes_in[...].astype(F32)
    out[...] = scaling[...] * whole[:classes] + bias[...]


def shifted(value, axis, step):
    size = lax.axis_size(axis)
    return lax.ppermute(value, axis, [((d + step) % size, d) for d in range(size)])


def swapped(value, masks):
    return lax.ppermute(value, "blk", [(d ^ masks[d % 2], d) for d in range(lax.axis_size("blk"))])


def outer_order(outer):
    rest = list(range(2, outer))
    return 1, list(zip(rest[0::2], rest[1::2]))


def two_ways(pairs):
    return pairs, [(pair[1], pair[0]) for pair in pairs]


def panel_order(outer, core):
    first, pairs = outer_order(outer)
    lists = []
    for here in (core, 1 - core):
        early, late = ([4 * jnp.where(here == 0, *sides) for sides in way] for way in two_ways(pairs))
        mine = [0, *early, 4 * first, *late]
        lists.append(mine + [apart + 2 for apart in mine])
    return lists[0], [apart ^ 1 for apart in lists[1]]


def packed(*parts):
    def pack(*refs):
        for index in range(len(parts)):
            refs[-1][index] = refs[index][...]

    out = jax.ShapeDtypeStruct((len(parts), *parts[0].shape), BF16)
    return call(pack, [out], vmem=parts)[0]


def gather_features(value, aside, later):
    outer = lax.axis_size("blk") // 4
    first, pairs = outer_order(outer)
    early, late = ([swapped(value, (4 * a, 4 * b)) for a, b in way] for way in two_ways(pairs))
    ahead = swapped(value, (4 * first, 4 * first))
    stacks = packed(value, *early), packed(ahead, *late)
    over = [swapped(stack, (2, 2)) for stack in stacks]
    beside = aside(over[0])
    over[0], *behind = later(over[0], beside)
    near = jnp.concatenate([*stacks, *over])
    return (near, swapped(near, (1, 1))), beside, behind


def gather_classes(value):
    size = lax.axis_size("blk")
    groups = [list(range(core, size, 2)) for core in range(2)]
    copies = jnp.broadcast_to(value[None], (size // 2, *value.shape))
    near = lax.all_to_all(copies, "blk", 0, 0, axis_index_groups=groups)
    return near, swapped(near, (1, 1))


def body(
    features,
    node_order,
    tile_values,
    tile_rows,
    tile_columns,
    tile_live,
    first_weight,
    first_bias,
    second_weight,
    second_bias,
):
    tile, width = features.shape
    slots = tile_values.shape[1]
    reps = lax.axis_size("rep")
    blocks = lax.axis_size("blk")
    hidden, classes = second_weight.shape
    padded = -(-(classes + 1) // 16) * 16
    shape = jax.ShapeDtypeStruct

    def exchanged(sums):
        return [shifted(sums[reps - 1 - step], "rep", step) for step in range(1, reps)]

    own_t = features.T
    others = [shifted(own_t, "rep", step) for step in range(1, reps)]
    live, part, wanted, tiles = call(
        prepare,
        [
            pltpu.SMEM((8,), jnp.int32),
            shape((width, tile), F32),
            shape((1, tile), jnp.int32),
            shape(tile_values.shape[1:], BF16),
        ],
        smem=(tile_live,),
        hbm=(node_order, own_t, tile_values[0]),
        scratch=[
            pltpu.VMEM(node_order.shape, jnp.int32),
            pltpu.VMEM(own_t.shape, BF16),
            pltpu.SemaphoreType.DMA((3,)),
        ],
        smem_outs=1,
    )
    (ordered,) = call(arrange, [shape((width, tile), BF16)], vmem=(part, wanted, *others))

    def staged(after):
        return call(
            functools.partial(stage, reps),
            [
                pltpu.SMEM((2 * slots,), jnp.int32),
                shape((hidden, 1), F32),
                shape((classes, 1), F32),
                shape((hidden, width), BF16),
                shape((classes, hidden), BF16),
            ],
            vmem=(after,),
            smem=(live,),
            hbm=(
                tile_rows,
                tile_columns,
                first_bias[None],
                second_bias[None],
                first_weight,
                second_weight.T,
            ),
            scratch=[
                pltpu.SMEM((1, slots), jnp.int32),
                pltpu.SMEM((1, slots), jnp.int32),
                pltpu.VMEM((1, hidden), F32),
                pltpu.VMEM((1, classes), F32),
                pltpu.VMEM(first_weight.shape, BF16),
                pltpu.SemaphoreType.DMA((6,)),
            ],
            smem_outs=1,
        )

    def turned(arrived, values):
        return call(
            turn,
            [
                shape(arrived.shape, BF16),
                shape(tiles.shape, BF16),
                shape((reps, 8, tile), F32),
            ],
            vmem=(tiles, arrived),
            smem=(values[0],),
        )

    (near, far), values, (tiles_t, degrees) = gather_features(ordered, staged, turned)
    plan, bias_1, bias_2, weight_1, weight_2 = values
    (projected,) = call(
        project,
        [shape((near.shape[0], hidden, tile), BF16)],
        vmem=(weight_1, near),
    )
    own, *sums = call(
        aggregate_hidden,
        [shape((hidden, tile), F32)] + [shape((hidden + ONES_ROWS, tile), jnp.int16)] * (reps - 1),
        vmem=(projected, far, weight_1, tiles_t, degrees),
        smem=(plan,),
        scratch=[pltpu.VMEM((blocks, hidden, tile), BF16)],
    )
    classes_in, scaling = call(
        combine,
        [shape((padded, tile), BF16), shape((1, tile), F32)],
        vmem=(projected, bias_1, weight_2, degrees, own, *exchanged(sums)),
    )
    own, *sums = call(
        aggregate_classes,
        [shape((padded, tile), F32)] + [shape((padded, tile), jnp.int16)] * (reps - 1),
        vmem=(*gather_classes(classes_in), tiles_t),
        smem=(plan,),
        scratch=[pltpu.VMEM((blocks, padded, tile), BF16)],
    )
    (logits,) = call(
        finish,
        [shape((classes, tile), F32)],
        vmem=(classes_in, scaling, bias_2, own, *exchanged(sums)),
    )
    return logits.T


def solution(mesh):
    placed = (
        P(("blk", "rep"), None),
        P("blk", None),
        P(("blk", "rep"), None, None, None),
        P(("blk", "rep"), None),
        P(("blk", "rep"), None),
        P(("blk", "rep")),
        P(),
        P(),
        P(),
        P(),
    )
    return jax.shard_map(
        body, mesh=mesh, in_specs=placed, out_specs=P(("blk", "rep"), None), check_vma=False
    )
```

```python
import functools

import jax
import jax.numpy as jnp
from jax import lax
from jax.experimental import pallas as pl
from jax.experimental.pallas import tpu as pltpu
from jax.sharding import PartitionSpec as P

BF16 = jnp.bfloat16
F32 = jnp.float32
ONES_ROWS = 16
VMEM_LIMIT = 32 * 1024 * 1024


def nn(a, b):
    return lax.dot_general(a, b, (((1,), (0,)), ((), ())), preferred_element_type=F32)


def nt(a, b):
    return lax.dot_general(a, b, (((1,), (1,)), ((), ())), preferred_element_type=F32)


def in_smem(value):
    return value if value.size == 1 else pltpu.with_memory_space_constraint(value, pltpu.SMEM)


def call(kernel, outs, smem=(), vmem=(), hbm=(), scratch=(), smem_outs=0, cost=1 << 20):
    spaces = [pltpu.VMEM] * len(vmem) + [pltpu.SMEM] * len(smem) + [pltpu.HBM] * len(hbm)
    out_spaces = [pltpu.SMEM] * smem_outs + [pltpu.VMEM] * (len(outs) - smem_outs)
    return pl.pallas_call(
        kernel,
        out_shape=outs,
        in_specs=[pl.BlockSpec(memory_space=space) for space in spaces],
        out_specs=[pl.BlockSpec(memory_space=space) for space in out_spaces],
        scratch_shapes=scratch,
        compiler_params=pltpu.CompilerParams(vmem_limit_bytes=VMEM_LIMIT),
        cost_estimate=pl.CostEstimate(flops=cost, bytes_accessed=cost, transcendentals=0),
    )(*vmem, *[in_smem(value) for value in smem], *[pltpu.with_memory_space_constraint(value, pltpu.HBM) for value in hbm])


def fetched(sources, targets, sems):
    copies = [
        pltpu.make_async_copy(source, target, sems.at[index])
        for index, (source, target) in enumerate(zip(sources, targets))
    ]
    for copy in copies:
        copy.start()
    return copies


def picked(features, wanted, owner):
    tile = features.shape[1]
    source = lax.broadcasted_iota(jnp.int32, (tile, tile), 0) + owner * tile
    return nn(features[...], jnp.where(source == wanted, 1.0, 0.0).astype(BF16))


def prepare(live, order, features, tiles, live_out, part, wanted_out, tiles_out, *rest):
    live_out[0] = live[0]
    order_in, features_in, sems = rest
    copies = fetched((order, features, tiles), (order_in, features_in, tiles_out), sems)
    for copy in copies[:2]:
        copy.wait()
    tile = features.shape[1]
    member = lax.axis_index("rep")
    wanted = order_in[:, pl.ds(pl.multiple_of(member * tile, tile), tile)]
    wanted_out[...] = wanted
    part[...] = picked(features_in, wanted, member)
    copies[2].wait()


def arrange(part, wanted, *rest):
    *features, out = rest
    reps = len(features) + 1
    member = lax.axis_index("rep")
    total = part[...]
    for step in range(1, reps):
        owner = lax.rem(member + step, reps)
        total = total + picked(features[step - 1], wanted[...], owner)
    out[...] = total.astype(BF16)


def stage(reps, _, live, *refs):
    sources, (plan, bias_1, bias_2, weight_1, weight_2), scratch = refs[:6], refs[6:11], refs[11:]
    rows_in, columns_in, row_1, row_2, weight_in, sems = scratch
    slots = rows_in.shape[1]
    blocks = lax.axis_size("blk")
    for copy in fetched(sources, (rows_in, columns_in, row_1, row_2, weight_in, weight_2), sems):
        copy.wait()
    bias_1[...] = jnp.broadcast_to(row_1[...], (8, row_1.shape[1])).T[:, :1]
    bias_2[...] = jnp.broadcast_to(row_2[...], (8, row_2.shape[1])).T[:, :1]
    weight_1[...] = weight_in[...].astype(F32).T.astype(BF16)
    block, member = lax.axis_index("blk"), lax.axis_index("rep")
    for slot in range(slots):
        plan[slot] = lax.clamp(0, columns_in[0, slot] // reps, blocks - 1) ^ block
        local = rows_in[0, slot] - block * reps
        step = lax.rem(local - member + reps, reps)
        plan[slots + slot] = jnp.where((slot < live[0]) & (local >= 0) & (local < reps), step, -1)


def project(weight_t, stack, out):
    for index in range(stack.shape[0]):
        out[index] = nn(weight_t[...], stack[index]).astype(BF16)


def turn(tiles, arrived, plan, arrived_out, tiles_t, degrees):
    arrived_out[...] = arrived[...]
    slots, tile = tiles.shape[0], tiles.shape[1]
    count = degrees.shape[0]
    total = jnp.zeros((count * ONES_ROWS, tile), F32)
    for slot in range(slots):
        values = tiles[slot]
        tiles_t[slot] = values.T
        ones = [
            jnp.full((ONES_ROWS, tile), (plan[slots + slot] == step).astype(F32), F32).astype(BF16)
            for step in range(count)
        ]
        total = total + nt(jnp.concatenate(ones, axis=0), values)
    for step in range(count):
        degrees[step] = total[step * ONES_ROWS : step * ONES_ROWS + 8]


def summed(panels, plan, tiles_t, count):
    slots, tile = tiles_t.shape[0], tiles_t.shape[1]
    height = panels.shape[1]
    total = jnp.zeros((count * height, tile), F32)
    for slot in range(slots):
        values = panels[plan[slot]]
        pieces = [
            values * (plan[slots + slot] == step).astype(F32).astype(BF16) for step in range(count)
        ]
        total = total + nn(jnp.concatenate(pieces, axis=0), tiles_t[slot])
    return [total[step * height : (step + 1) * height] for step in range(count)]


def coded(values):
    top = jnp.max(jnp.abs(values), axis=0, keepdims=True)
    power = jnp.ceil(jnp.log2(jnp.maximum(top, 1e-30)))
    return jnp.round(values * jnp.exp2(14.0 - power)).astype(jnp.int32), power.astype(jnp.int32)


def decoded(codes, power):
    return codes.astype(F32) * jnp.exp2(power.astype(F32) - 14.0)


def in_thirds(row):
    first = jnp.floor(row)
    second = jnp.floor((row - first) * 16384.0)
    third = jnp.round(((row - first) * 16384.0 - second) * 16384.0)
    return [part.astype(jnp.int32) for part in (first, second, third)]


def aggregate_hidden(projected, far, weight_t, tiles_t, degrees, plan, own, *rest):
    others, panels = rest[:-1], rest[-1]
    mine, opposite = panel_order(panels.shape[0] // 4, lax.axis_index("blk") % 2)
    for index, place in enumerate(mine):
        panels[place] = projected[index]
    for index, place in enumerate(opposite):
        panels[place] = nn(weight_t[...], far[index]).astype(BF16)
    sums = summed(panels, plan, tiles_t, 1 + len(others))
    own[...] = sums[0]
    row = lax.broadcasted_iota(jnp.int32, (ONES_ROWS, own.shape[1]), 0)
    for step, (part, out) in enumerate(zip(sums[1:], others), 1):
        codes, power = coded(part)
        terms = jnp.zeros(row.shape, jnp.int32)
        for index, term in enumerate([power, *in_thirds(degrees[step, :1])]):
            terms = jnp.where(row == index, term, terms)
        out[...] = jnp.concatenate([codes, terms], axis=0).astype(jnp.int16)


def aggregate_classes(near, far, tiles_t, plan, own, *rest):
    others, panels = rest[:-1], rest[-1]
    chip = lax.axis_index("blk") // 2
    for index in range(near.shape[0]):
        panels[2 * (index ^ chip)] = near[index]
        panels[2 * (index ^ chip) + 1] = far[index]
    sums = summed(panels, plan, tiles_t, 1 + len(others))
    own[...] = sums[0]
    row = lax.broadcasted_iota(jnp.int32, own.shape, 0)
    for part, out in zip(sums[1:], others):
        codes, power = coded(part)
        out[...] = jnp.where(row == own.shape[0] - 1, power, codes).astype(jnp.int16)


def combine(place, hidden_in, bias, weight_t, degrees, own, *rest):
    *arrived, out, scale_out = rest
    height = hidden_in.shape[1]
    total, degree = own[...], degrees[0, :1]
    for part in arrived:
        codes = part[...].astype(jnp.int32)
        total = total + decoded(codes[:height], codes[height : height + 1])
        terms = [codes[height + 1 + index : height + 2 + index].astype(F32) for index in range(3)]
        degree = degree + (terms[0] + (terms[1] + terms[2] * 2.0**-14) * 2.0**-14)
    scaling = lax.rsqrt(1.0 + degree)
    hidden = scaling * (total + hidden_in[place].astype(F32)) + bias[...]
    hidden = jnp.maximum(hidden, 0.0).astype(BF16)
    classes = nn(weight_t[...], hidden)
    blank = jnp.zeros((out.shape[0] - classes.shape[0], classes.shape[1]), F32)
    out[...] = jnp.concatenate([classes, blank], axis=0).astype(BF16)
    scale_out[...] = scaling


def finish(classes_in, scaling, bias, own, *rest):
    *arrived, out = rest
    classes = out.shape[0]
    total = own[...]
    for part in arrived:
        codes = part[...].astype(jnp.int32)
        total = total + decoded(codes, codes[-1:])
    whole = total + classes_in[...].astype(F32)
    out[...] = scaling[...] * whole[:classes] + bias[...]


def shifted(value, axis, step):
    size = lax.axis_size(axis)
    return lax.ppermute(value, axis, [((d + step) % size, d) for d in range(size)])


def swapped(value, masks):
    return lax.ppermute(value, "blk", [(d ^ masks[d % 2], d) for d in range(lax.axis_size("blk"))])


def outer_order(outer):
    rest = list(range(2, outer))
    return 1, list(zip(rest[0::2], rest[1::2]))


def two_ways(pairs):
    return pairs, [(pair[1], pair[0]) for pair in pairs]


def panel_order(outer, core):
    first, pairs = outer_order(outer)
    lists = []
    for here in (core, 1 - core):
        early, late = ([4 * jnp.where(here == 0, *sides) for sides in way] for way in two_ways(pairs))
        mine = [*early, 0, 4 * first, *late]
        lists.append(mine + [apart + 2 for apart in mine])
    return lists[0], [apart ^ 1 for apart in lists[1]]


def packed(*parts):
    def pack(*refs):
        for index in range(len(parts)):
            refs[-1][index] = refs[index][...]

    out = jax.ShapeDtypeStruct((len(parts), *parts[0].shape), BF16)
    return call(pack, [out], vmem=parts)[0]


def gather_features(value, aside, later):
    outer = lax.axis_size("blk") // 4
    first, pairs = outer_order(outer)
    early, late = ([swapped(value, (4 * a, 4 * b)) for a, b in way] for way in two_ways(pairs))
    ahead = swapped(value, (4 * first, 4 * first))
    stacks = packed(*early), packed(value, ahead), packed(*late)
    over = [swapped(stack, (2, 2)) for stack in stacks]
    beside = aside(stacks[1])
    over[0], *behind = later(over[0], beside)
    near = jnp.concatenate([*stacks, *over])
    return (near, swapped(near, (1, 1))), beside, behind


def gather_classes(value):
    size = lax.axis_size("blk")
    groups = [list(range(core, size, 2)) for core in range(2)]
    copies = jnp.broadcast_to(value[None], (size // 2, *value.shape))
    near = lax.all_to_all(copies, "blk", 0, 0, axis_index_groups=groups)
    return near, swapped(near, (1, 1))


def body(
    features,
    node_order,
    tile_values,
    tile_rows,
    tile_columns,
    tile_live,
    first_weight,
    first_bias,
    second_weight,
    second_bias,
):
    tile, width = features.shape
    slots = tile_values.shape[1]
    reps = lax.axis_size("rep")
    blocks = lax.axis_size("blk")
    hidden, classes = second_weight.shape
    padded = -(-(classes + 1) // 16) * 16
    shape = jax.ShapeDtypeStruct

    def exchanged(sums):
        return [shifted(sums[reps - 1 - step], "rep", step) for step in range(1, reps)]

    own_t = features.T
    others = [shifted(own_t, "rep", step) for step in range(1, reps)]
    live, part, wanted, tiles = call(
        prepare,
        [
            pltpu.SMEM((8,), jnp.int32),
            shape((width, tile), F32),
            shape((1, tile), jnp.int32),
            shape(tile_values.shape[1:], BF16),
        ],
        smem=(tile_live,),
        hbm=(node_order, own_t, tile_values[0]),
        scratch=[
            pltpu.VMEM(node_order.shape, jnp.int32),
            pltpu.VMEM(own_t.shape, BF16),
            pltpu.SemaphoreType.DMA((3,)),
        ],
        smem_outs=1,
    )
    (ordered,) = call(arrange, [shape((width, tile), BF16)], vmem=(part, wanted, *others))

    def staged(after):
        return call(
            functools.partial(stage, reps),
            [
                pltpu.SMEM((2 * slots,), jnp.int32),
                shape((hidden, 1), F32),
                shape((classes, 1), F32),
                shape((hidden, width), BF16),
                shape((classes, hidden), BF16),
            ],
            vmem=(after,),
            smem=(live,),
            hbm=(
                tile_rows,
                tile_columns,
                first_bias[None],
                second_bias[None],
                first_weight,
                second_weight.T,
            ),
            scratch=[
                pltpu.SMEM((1, slots), jnp.int32),
                pltpu.SMEM((1, slots), jnp.int32),
                pltpu.VMEM((1, hidden), F32),
                pltpu.VMEM((1, classes), F32),
                pltpu.VMEM(first_weight.shape, BF16),
                pltpu.SemaphoreType.DMA((6,)),
            ],
            smem_outs=1,
        )

    def turned(arrived, values):
        return call(
            turn,
            [
                shape(arrived.shape, BF16),
                shape(tiles.shape, BF16),
                shape((reps, 8, tile), F32),
            ],
            vmem=(tiles, arrived),
            smem=(values[0],),
        )

    (near, far), values, (tiles_t, degrees) = gather_features(ordered, staged, turned)
    plan, bias_1, bias_2, weight_1, weight_2 = values
    (projected,) = call(
        project,
        [shape((near.shape[0], hidden, tile), BF16)],
        vmem=(weight_1, near),
    )
    own, *sums = call(
        aggregate_hidden,
        [shape((hidden, tile), F32)] + [shape((hidden + ONES_ROWS, tile), jnp.int16)] * (reps - 1),
        vmem=(projected, far, weight_1, tiles_t, degrees),
        smem=(plan,),
        scratch=[pltpu.VMEM((blocks, hidden, tile), BF16)],
    )
    classes_in, scaling = call(
        functools.partial(combine, len(outer_order(blocks // 4)[1])),
        [shape((padded, tile), BF16), shape((1, tile), F32)],
        vmem=(projected, bias_1, weight_2, degrees, own, *exchanged(sums)),
    )
    own, *sums = call(
        aggregate_classes,
        [shape((padded, tile), F32)] + [shape((padded, tile), jnp.int16)] * (reps - 1),
        vmem=(*gather_classes(classes_in), tiles_t),
        smem=(plan,),
        scratch=[pltpu.VMEM((blocks, padded, tile), BF16)],
    )
    (logits,) = call(
        finish,
        [shape((classes, tile), F32)],
        vmem=(classes_in, scaling, bias_2, own, *exchanged(sums)),
    )
    return logits.T


def solution(mesh):
    placed = (
        P(("blk", "rep"), None),
        P("blk", None),
        P(("blk", "rep"), None, None, None),
        P(("blk", "rep"), None),
        P(("blk", "rep"), None),
        P(("blk", "rep")),
        P(),
        P(),
        P(),
        P(),
    )
    return jax.shard_map(
        body, mesh=mesh, in_specs=placed, out_specs=P(("blk", "rep"), None), check_vma=False
    )
```

```python
import functools

import jax
import jax.numpy as jnp
from jax import lax
from jax.experimental import pallas as pl
from jax.experimental.pallas import tpu as pltpu
from jax.sharding import PartitionSpec as P

BF16 = jnp.bfloat16
F32 = jnp.float32
ONES_ROWS = 16
VMEM_LIMIT = 32 * 1024 * 1024


def nn(a, b):
    return lax.dot_general(a, b, (((1,), (0,)), ((), ())), preferred_element_type=F32)


def nt(a, b):
    return lax.dot_general(a, b, (((1,), (1,)), ((), ())), preferred_element_type=F32)


def in_smem(value):
    return value if value.size == 1 else pltpu.with_memory_space_constraint(value, pltpu.SMEM)


def call(kernel, outs, smem=(), vmem=(), hbm=(), scratch=(), smem_outs=0, cost=1 << 20):
    spaces = [pltpu.VMEM] * len(vmem) + [pltpu.SMEM] * len(smem) + [pltpu.HBM] * len(hbm)
    out_spaces = [pltpu.SMEM] * smem_outs + [pltpu.VMEM] * (len(outs) - smem_outs)
    return pl.pallas_call(
        kernel,
        out_shape=outs,
        in_specs=[pl.BlockSpec(memory_space=space) for space in spaces],
        out_specs=[pl.BlockSpec(memory_space=space) for space in out_spaces],
        scratch_shapes=scratch,
        compiler_params=pltpu.CompilerParams(vmem_limit_bytes=VMEM_LIMIT),
        cost_estimate=pl.CostEstimate(flops=cost, bytes_accessed=cost, transcendentals=0),
    )(*vmem, *[in_smem(value) for value in smem], *[pltpu.with_memory_space_constraint(value, pltpu.HBM) for value in hbm])


def fetched(sources, targets, sems):
    copies = [
        pltpu.make_async_copy(source, target, sems.at[index])
        for index, (source, target) in enumerate(zip(sources, targets))
    ]
    for copy in copies:
        copy.start()
    return copies


def picked(features, wanted, owner):
    tile = features.shape[1]
    source = lax.broadcasted_iota(jnp.int32, (tile, tile), 0) + owner * tile
    return nn(features[...], jnp.where(source == wanted, 1.0, 0.0).astype(BF16))


def prepare(live, order, features, tiles, live_out, part, wanted_out, tiles_out, *rest):
    live_out[0] = live[0]
    order_in, features_in, sems = rest
    copies = fetched((order, features, tiles), (order_in, features_in, tiles_out), sems)
    for copy in copies[:2]:
        copy.wait()
    tile = features.shape[1]
    member = lax.axis_index("rep")
    wanted = order_in[:, pl.ds(pl.multiple_of(member * tile, tile), tile)]
    wanted_out[...] = wanted
    part[...] = picked(features_in, wanted, member)
    copies[2].wait()


def arrange(part, wanted, *rest):
    *features, out = rest
    reps = len(features) + 1
    member = lax.axis_index("rep")
    total = part[...]
    for step in range(1, reps):
        owner = lax.rem(member + step, reps)
        total = total + picked(features[step - 1], wanted[...], owner)
    out[...] = total.astype(BF16)


def stage(reps, _, live, *refs):
    sources, (plan, bias_1, bias_2, weight_1, weight_2), scratch = refs[:6], refs[6:11], refs[11:]
    rows_in, columns_in, row_1, row_2, weight_in, sems = scratch
    slots = rows_in.shape[1]
    blocks = lax.axis_size("blk")
    for copy in fetched(sources, (rows_in, columns_in, row_1, row_2, weight_in, weight_2), sems):
        copy.wait()
    bias_1[...] = jnp.broadcast_to(row_1[...], (8, row_1.shape[1])).T[:, :1]
    bias_2[...] = jnp.broadcast_to(row_2[...], (8, row_2.shape[1])).T[:, :1]
    weight_1[...] = weight_in[...].astype(F32).T.astype(BF16)
    block, member = lax.axis_index("blk"), lax.axis_index("rep")
    for slot in range(slots):
        plan[slot] = lax.clamp(0, columns_in[0, slot] // reps, blocks - 1) ^ block
        local = rows_in[0, slot] - block * reps
        step = lax.rem(local - member + reps, reps)
        plan[slots + slot] = jnp.where((slot < live[0]) & (local >= 0) & (local < reps), step, -1)


def project(weight_t, stack, out):
    for index in range(stack.shape[0]):
        out[index] = nn(weight_t[...], stack[index]).astype(BF16)


def turn(tiles, arrived, plan, arrived_out, tiles_t, degrees):
    arrived_out[...] = arrived[...]
    slots, tile = tiles.shape[0], tiles.shape[1]
    count = degrees.shape[0]
    total = jnp.zeros((count * ONES_ROWS, tile), F32)
    for slot in range(slots):
        values = tiles[slot]
        tiles_t[slot] = values.T
        ones = [
            jnp.full((ONES_ROWS, tile), (plan[slots + slot] == step).astype(F32), F32).astype(BF16)
            for step in range(count)
        ]
        total = total + nt(jnp.concatenate(ones, axis=0), values)
    for step in range(count):
        degrees[step] = total[step * ONES_ROWS : step * ONES_ROWS + 8]


def summed(panels, plan, tiles_t, count):
    slots, tile = tiles_t.shape[0], tiles_t.shape[1]
    height = panels.shape[1]
    total = jnp.zeros((count * height, tile), F32)
    for slot in range(slots):
        values = panels[plan[slot]]
        pieces = [
            values * (plan[slots + slot] == step).astype(F32).astype(BF16) for step in range(count)
        ]
        total = total + nn(jnp.concatenate(pieces, axis=0), tiles_t[slot])
    return [total[step * height : (step + 1) * height] for step in range(count)]


def coded(values):
    top = jnp.max(jnp.abs(values), axis=0, keepdims=True)
    power = jnp.ceil(jnp.log2(jnp.maximum(top, 1e-30)))
    return jnp.round(values * jnp.exp2(14.0 - power)).astype(jnp.int32), power.astype(jnp.int32)


def decoded(codes, power):
    return codes.astype(F32) * jnp.exp2(power.astype(F32) - 14.0)


def in_thirds(row):
    first = jnp.floor(row)
    second = jnp.floor((row - first) * 16384.0)
    third = jnp.round(((row - first) * 16384.0 - second) * 16384.0)
    return [part.astype(jnp.int32) for part in (first, second, third)]


def aggregate_hidden(projected, far, weight_t, tiles_t, degrees, plan, own, *rest):
    others, panels = rest[:-1], rest[-1]
    mine, opposite = panel_order(panels.shape[0] // 4)
    for index, place in enumerate(mine):
        panels[place] = projected[index]
    for index, place in enumerate(opposite):
        panels[place] = nn(weight_t[...], far[index]).astype(BF16)
    sums = summed(panels, plan, tiles_t, 1 + len(others))
    own[...] = sums[0]
    row = lax.broadcasted_iota(jnp.int32, (ONES_ROWS, own.shape[1]), 0)
    for step, (part, out) in enumerate(zip(sums[1:], others), 1):
        codes, power = coded(part)
        terms = jnp.zeros(row.shape, jnp.int32)
        for index, term in enumerate([power, *in_thirds(degrees[step, :1])]):
            terms = jnp.where(row == index, term, terms)
        out[...] = jnp.concatenate([codes, terms], axis=0).astype(jnp.int16)


def aggregate_classes(near, far, tiles_t, plan, own, *rest):
    others, panels = rest[:-1], rest[-1]
    chip = lax.axis_index("blk") // 2
    for index in range(near.shape[0]):
        panels[2 * (index ^ chip)] = near[index]
        panels[2 * (index ^ chip) + 1] = far[index]
    sums = summed(panels, plan, tiles_t, 1 + len(others))
    own[...] = sums[0]
    row = lax.broadcasted_iota(jnp.int32, own.shape, 0)
    for part, out in zip(sums[1:], others):
        codes, power = coded(part)
        out[...] = jnp.where(row == own.shape[0] - 1, power, codes).astype(jnp.int16)


def combine(place, hidden_in, bias, weight_t, degrees, own, *rest):
    *arrived, out, scale_out = rest
    height = hidden_in.shape[1]
    total, degree = own[...], degrees[0, :1]
    for part in arrived:
        codes = part[...].astype(jnp.int32)
        total = total + decoded(codes[:height], codes[height : height + 1])
        terms = [codes[height + 1 + index : height + 2 + index].astype(F32) for index in range(3)]
        degree = degree + (terms[0] + (terms[1] + terms[2] * 2.0**-14) * 2.0**-14)
    scaling = lax.rsqrt(1.0 + degree)
    hidden = scaling * (total + hidden_in[place].astype(F32)) + bias[...]
    hidden = jnp.maximum(hidden, 0.0).astype(BF16)
    classes = nn(weight_t[...], hidden)
    blank = jnp.zeros((out.shape[0] - classes.shape[0], classes.shape[1]), F32)
    out[...] = jnp.concatenate([classes, blank], axis=0).astype(BF16)
    scale_out[...] = scaling


def finish(classes_in, scaling, bias, own, *rest):
    *arrived, out = rest
    classes = out.shape[0]
    total = own[...]
    for part in arrived:
        codes = part[...].astype(jnp.int32)
        total = total + decoded(codes, codes[-1:])
    whole = total + classes_in[...].astype(F32)
    out[...] = scaling[...] * whole[:classes] + bias[...]


def shifted(value, axis, step):
    size = lax.axis_size(axis)
    return lax.ppermute(value, axis, [((d + step) % size, d) for d in range(size)])


def swapped(value, mask):
    return lax.ppermute(value, "blk", [(d ^ mask, d) for d in range(lax.axis_size("blk"))])


def panel_order(outer):
    direct = [4 * step for step in range(2, outer, 2)]
    mine = [*direct, 0, 4, *[apart + 4 for apart in direct]]
    mine = mine + [apart + 2 for apart in mine]
    return mine, [apart ^ 1 for apart in mine]


def packed(*parts):
    def pack(*refs):
        for index in range(len(parts)):
            refs[-1][index] = refs[index][...]

    out = jax.ShapeDtypeStruct((len(parts), *parts[0].shape), BF16)
    return call(pack, [out], vmem=parts)[0]


def gather_features(value, aside, later):
    outer = lax.axis_size("blk") // 4
    direct = packed(*[swapped(value, 4 * step) for step in range(2, outer, 2)])
    ahead = swapped(value, 4)
    relayed = swapped(direct, 4)
    stacks = direct, packed(value, ahead), packed(relayed)[0]
    over = [swapped(stack, 2) for stack in stacks]
    beside = aside(over[0])
    over[0], *behind = later(over[0], beside)
    near = jnp.concatenate([*stacks, *over])
    return (near, swapped(near, 1)), beside, behind


def gather_classes(value):
    size = lax.axis_size("blk")
    groups = [list(range(core, size, 2)) for core in range(2)]
    copies = jnp.broadcast_to(value[None], (size // 2, *value.shape))
    near = lax.all_to_all(copies, "blk", 0, 0, axis_index_groups=groups)
    return near, swapped(near, 1)


def body(
    features,
    node_order,
    tile_values,
    tile_rows,
    tile_columns,
    tile_live,
    first_weight,
    first_bias,
    second_weight,
    second_bias,
):
    tile, width = features.shape
    slots = tile_values.shape[1]
    reps = lax.axis_size("rep")
    blocks = lax.axis_size("blk")
    hidden, classes = second_weight.shape
    padded = -(-(classes + 1) // 16) * 16
    shape = jax.ShapeDtypeStruct

    def exchanged(sums):
        return [shifted(sums[reps - 1 - step], "rep", step) for step in range(1, reps)]

    own_t = features.T
    others = [shifted(own_t, "rep", step) for step in range(1, reps)]
    live, part, wanted, tiles = call(
        prepare,
        [
            pltpu.SMEM((8,), jnp.int32),
            shape((width, tile), F32),
            shape((1, tile), jnp.int32),
            shape(tile_values.shape[1:], BF16),
        ],
        smem=(tile_live,),
        hbm=(node_order, own_t, tile_values[0]),
        scratch=[
            pltpu.VMEM(node_order.shape, jnp.int32),
            pltpu.VMEM(own_t.shape, BF16),
            pltpu.SemaphoreType.DMA((3,)),
        ],
        smem_outs=1,
    )
    (ordered,) = call(arrange, [shape((width, tile), BF16)], vmem=(part, wanted, *others))

    def staged(after):
        return call(
            functools.partial(stage, reps),
            [
                pltpu.SMEM((2 * slots,), jnp.int32),
                shape((hidden, 1), F32),
                shape((classes, 1), F32),
                shape((hidden, width), BF16),
                shape((classes, hidden), BF16),
            ],
            vmem=(after,),
            smem=(live,),
            hbm=(
                tile_rows,
                tile_columns,
                first_bias[None],
                second_bias[None],
                first_weight,
                second_weight.T,
            ),
            scratch=[
                pltpu.SMEM((1, slots), jnp.int32),
                pltpu.SMEM((1, slots), jnp.int32),
                pltpu.VMEM((1, hidden), F32),
                pltpu.VMEM((1, classes), F32),
                pltpu.VMEM(first_weight.shape, BF16),
                pltpu.SemaphoreType.DMA((6,)),
            ],
            smem_outs=1,
        )

    def turned(arrived, values):
        return call(
            turn,
            [
                shape(arrived.shape, BF16),
                shape(tiles.shape, BF16),
                shape((reps, 8, tile), F32),
            ],
            vmem=(tiles, arrived),
            smem=(values[0],),
        )

    (near, far), values, (tiles_t, degrees) = gather_features(ordered, staged, turned)
    plan, bias_1, bias_2, weight_1, weight_2 = values
    (projected,) = call(
        project,
        [shape((near.shape[0], hidden, tile), BF16)],
        vmem=(weight_1, near),
    )
    own, *sums = call(
        aggregate_hidden,
        [shape((hidden, tile), F32)] + [shape((hidden + ONES_ROWS, tile), jnp.int16)] * (reps - 1),
        vmem=(projected, far, weight_1, tiles_t, degrees),
        smem=(plan,),
        scratch=[pltpu.VMEM((blocks, hidden, tile), BF16)],
    )
    classes_in, scaling = call(
        functools.partial(combine, blocks // 8 - 1),
        [shape((padded, tile), BF16), shape((1, tile), F32)],
        vmem=(projected, bias_1, weight_2, degrees, own, *exchanged(sums)),
    )
    own, *sums = call(
        aggregate_classes,
        [shape((padded, tile), F32)] + [shape((padded, tile), jnp.int16)] * (reps - 1),
        vmem=(*gather_classes(classes_in), tiles_t),
        smem=(plan,),
        scratch=[pltpu.VMEM((blocks, padded, tile), BF16)],
    )
    (logits,) = call(
        finish,
        [shape((classes, tile), F32)],
        vmem=(classes_in, scaling, bias_2, own, *exchanged(sums)),
    )
    return logits.T


def solution(mesh):
    placed = (
        P(("blk", "rep"), None),
        P("blk", None),
        P(("blk", "rep"), None, None, None),
        P(("blk", "rep"), None),
        P(("blk", "rep"), None),
        P(("blk", "rep")),
        P(),
        P(),
        P(),
        P(),
    )
    return jax.shard_map(
        body, mesh=mesh, in_specs=placed, out_specs=P(("blk", "rep"), None), check_vma=False
    )
```

```python
import functools

import jax
import jax.numpy as jnp
from jax import lax
from jax.experimental import pallas as pl
from jax.experimental.pallas import tpu as pltpu
from jax.sharding import PartitionSpec as P

BF16 = jnp.bfloat16
F32 = jnp.float32
ONES_ROWS = 16
VMEM_LIMIT = 32 * 1024 * 1024


def nn(a, b):
    return lax.dot_general(a, b, (((1,), (0,)), ((), ())), preferred_element_type=F32)


def nt(a, b):
    return lax.dot_general(a, b, (((1,), (1,)), ((), ())), preferred_element_type=F32)


def in_smem(value):
    return value if value.size == 1 else pltpu.with_memory_space_constraint(value, pltpu.SMEM)


def call(kernel, outs, smem=(), vmem=(), hbm=(), scratch=(), smem_outs=0, cost=1 << 20):
    spaces = [pltpu.VMEM] * len(vmem) + [pltpu.SMEM] * len(smem) + [pltpu.HBM] * len(hbm)
    out_spaces = [pltpu.SMEM] * smem_outs + [pltpu.VMEM] * (len(outs) - smem_outs)
    return pl.pallas_call(
        kernel,
        out_shape=outs,
        in_specs=[pl.BlockSpec(memory_space=space) for space in spaces],
        out_specs=[pl.BlockSpec(memory_space=space) for space in out_spaces],
        scratch_shapes=scratch,
        compiler_params=pltpu.CompilerParams(vmem_limit_bytes=VMEM_LIMIT),
        cost_estimate=pl.CostEstimate(flops=cost, bytes_accessed=cost, transcendentals=0),
    )(*vmem, *[in_smem(value) for value in smem], *[pltpu.with_memory_space_constraint(value, pltpu.HBM) for value in hbm])


def fetched(sources, targets, sems):
    copies = [
        pltpu.make_async_copy(source, target, sems.at[index])
        for index, (source, target) in enumerate(zip(sources, targets))
    ]
    for copy in copies:
        copy.start()
    return copies


def picked(features, wanted, owner):
    tile = features.shape[1]
    source = lax.broadcasted_iota(jnp.int32, (tile, tile), 0) + owner * tile
    return nn(features[...], jnp.where(source == wanted, 1.0, 0.0).astype(BF16))


def prepare(live, order, features, tiles, live_out, part, wanted_out, tiles_out, *rest):
    live_out[0] = live[0]
    order_in, features_in, sems = rest
    copies = fetched((order, features, tiles), (order_in, features_in, tiles_out), sems)
    for copy in copies[:2]:
        copy.wait()
    tile = features.shape[1]
    member = lax.axis_index("rep")
    wanted = order_in[:, pl.ds(pl.multiple_of(member * tile, tile), tile)]
    wanted_out[...] = wanted
    part[...] = picked(features_in, wanted, member)
    copies[2].wait()


def arrange(part, wanted, *rest):
    *features, out = rest
    reps = len(features) + 1
    member = lax.axis_index("rep")
    total = part[...]
    for step in range(1, reps):
        owner = lax.rem(member + step, reps)
        total = total + picked(features[step - 1], wanted[...], owner)
    out[...] = total.astype(BF16)


def stage(reps, _, live, *refs):
    sources, (plan, bias_1, bias_2, weight_1, weight_2), scratch = refs[:6], refs[6:11], refs[11:]
    rows_in, columns_in, row_1, row_2, weight_in, sems = scratch
    slots = rows_in.shape[1]
    blocks = lax.axis_size("blk")
    for copy in fetched(sources, (rows_in, columns_in, row_1, row_2, weight_in, weight_2), sems):
        copy.wait()
    bias_1[...] = jnp.broadcast_to(row_1[...], (8, row_1.shape[1])).T[:, :1]
    bias_2[...] = jnp.broadcast_to(row_2[...], (8, row_2.shape[1])).T[:, :1]
    weight_1[...] = weight_in[...].astype(F32).T.astype(BF16)
    block, member = lax.axis_index("blk"), lax.axis_index("rep")
    for slot in range(slots):
        plan[slot] = lax.clamp(0, columns_in[0, slot] // reps, blocks - 1) ^ block
        local = rows_in[0, slot] - block * reps
        step = lax.rem(local - member + reps, reps)
        plan[slots + slot] = jnp.where((slot < live[0]) & (local >= 0) & (local < reps), step, -1)


def project(weight_t, stack, out):
    for index in range(stack.shape[0]):
        out[index] = nn(weight_t[...], stack[index]).astype(BF16)


def turn(tiles, arrived, plan, arrived_out, tiles_t, degrees):
    arrived_out[...] = arrived[...]
    slots, tile = tiles.shape[0], tiles.shape[1]
    count = degrees.shape[0]
    total = jnp.zeros((count * ONES_ROWS, tile), F32)
    for slot in range(slots):
        values = tiles[slot]
        tiles_t[slot] = values.T
        ones = [
            jnp.full((ONES_ROWS, tile), (plan[slots + slot] == step).astype(F32), F32).astype(BF16)
            for step in range(count)
        ]
        total = total + nt(jnp.concatenate(ones, axis=0), values)
    for step in range(count):
        degrees[step] = total[step * ONES_ROWS : step * ONES_ROWS + 8]


def summed(panels, plan, tiles_t, count):
    slots, tile = tiles_t.shape[0], tiles_t.shape[1]
    height = panels.shape[1]
    total = jnp.zeros((count * height, tile), F32)
    for slot in range(slots):
        values = panels[plan[slot]]
        pieces = [
            values * (plan[slots + slot] == step).astype(F32).astype(BF16) for step in range(count)
        ]
        total = total + nn(jnp.concatenate(pieces, axis=0), tiles_t[slot])
    return [total[step * height : (step + 1) * height] for step in range(count)]


def coded(values):
    top = jnp.max(jnp.abs(values), axis=0, keepdims=True)
    power = jnp.ceil(jnp.log2(jnp.maximum(top, 1e-30)))
    return jnp.round(values * jnp.exp2(14.0 - power)).astype(jnp.int32), power.astype(jnp.int32)


def decoded(codes, power):
    return codes.astype(F32) * jnp.exp2(power.astype(F32) - 14.0)


def in_thirds(row):
    first = jnp.floor(row)
    second = jnp.floor((row - first) * 16384.0)
    third = jnp.round(((row - first) * 16384.0 - second) * 16384.0)
    return [part.astype(jnp.int32) for part in (first, second, third)]


def aggregate_hidden(projected, far, weight_t, tiles_t, degrees, plan, own, *rest):
    others, panels = rest[:-1], rest[-1]
    mine, opposite = panel_order(panels.shape[0] // 4, lax.axis_index("blk") % 2)
    for index, place in enumerate(mine):
        panels[place] = projected[index]
    for index, place in enumerate(opposite):
        panels[place] = nn(weight_t[...], far[index]).astype(BF16)
    sums = summed(panels, plan, tiles_t, 1 + len(others))
    own[...] = sums[0]
    row = lax.broadcasted_iota(jnp.int32, (ONES_ROWS, own.shape[1]), 0)
    for step, (part, out) in enumerate(zip(sums[1:], others), 1):
        codes, power = coded(part)
        terms = jnp.zeros(row.shape, jnp.int32)
        for index, term in enumerate([power, *in_thirds(degrees[step, :1])]):
            terms = jnp.where(row == index, term, terms)
        out[...] = jnp.concatenate([codes, terms], axis=0).astype(jnp.int16)


def aggregate_classes(near, far, tiles_t, plan, own, *rest):
    others, panels = rest[:-1], rest[-1]
    chip = lax.axis_index("blk") // 2
    for index in range(near.shape[0]):
        panels[2 * (index ^ chip)] = near[index]
        panels[2 * (index ^ chip) + 1] = far[index]
    sums = summed(panels, plan, tiles_t, 1 + len(others))
    own[...] = sums[0]
    row = lax.broadcasted_iota(jnp.int32, own.shape, 0)
    for part, out in zip(sums[1:], others):
        codes, power = coded(part)
        out[...] = jnp.where(row == own.shape[0] - 1, power, codes).astype(jnp.int16)


def combine(hidden_in, bias, weight_t, degrees, own, *rest):
    *arrived, out, scale_out = rest
    height = hidden_in.shape[1]
    total, degree = own[...], degrees[0, :1]
    for part in arrived:
        codes = part[...].astype(jnp.int32)
        total = total + decoded(codes[:height], codes[height : height + 1])
        terms = [codes[height + 1 + index : height + 2 + index].astype(F32) for index in range(3)]
        degree = degree + (terms[0] + (terms[1] + terms[2] * 2.0**-14) * 2.0**-14)
    scaling = lax.rsqrt(1.0 + degree)
    hidden = scaling * (total + hidden_in[0].astype(F32)) + bias[...]
    hidden = jnp.maximum(hidden, 0.0).astype(BF16)
    classes = nn(weight_t[...], hidden)
    blank = jnp.zeros((out.shape[0] - classes.shape[0], classes.shape[1]), F32)
    out[...] = jnp.concatenate([classes, blank], axis=0).astype(BF16)
    scale_out[...] = scaling


def finish(classes_in, scaling, bias, own, *rest):
    *arrived, out = rest
    classes = out.shape[0]
    total = own[...]
    for part in arrived:
        codes = part[...].astype(jnp.int32)
        total = total + decoded(codes, codes[-1:])
    whole = total + classes_in[...].astype(F32)
    out[...] = scaling[...] * whole[:classes] + bias[...]


def shifted(value, axis, step):
    size = lax.axis_size(axis)
    return lax.ppermute(value, axis, [((d + step) % size, d) for d in range(size)])


def swapped(value, masks):
    return lax.ppermute(value, "blk", [(d ^ masks[d % 2], d) for d in range(lax.axis_size("blk"))])


def outer_order(outer):
    rest = list(range(2, outer))
    return 1, list(zip(rest[0::2], rest[1::2]))


def two_ways(pairs):
    return pairs, [(pair[1], pair[0]) for pair in pairs]


def panel_order(outer, core):
    first, pairs = outer_order(outer)
    lists = []
    for here in (core, 1 - core):
        early, late = ([4 * jnp.where(here == 0, *sides) for sides in way] for way in two_ways(pairs))
        mine = [0, 4 * first, *early, *late]
        lists.append(mine + [apart + 2 for apart in mine])
    return lists[0], [apart ^ 1 for apart in lists[1]]


def packed(*parts):
    def pack(*refs):
        for index in range(len(parts)):
            refs[-1][index] = refs[index][...]

    out = jax.ShapeDtypeStruct((len(parts), *parts[0].shape), BF16)
    return call(pack, [out], vmem=parts)[0]


def gather_features(value, aside, later):
    outer = lax.axis_size("blk") // 4
    first, pairs = outer_order(outer)
    ahead = swapped(value, (4 * first, 4 * first))
    early, late = ([swapped(value, (4 * a, 4 * b)) for a, b in way] for way in two_ways(pairs))
    crossed = [swapped(value, (4 * a + 2, 4 * b + 2)) for a, b in two_ways(pairs)[1]]
    here, early = packed(value, ahead), packed(*early)
    over = [swapped(here, (2, 2)), swapped(early, (2, 2))]
    beside = aside(here)
    over[0], *behind = later(over[0], beside)
    near = jnp.concatenate([here, early, packed(*late), *over, packed(*crossed)])
    return (near, swapped(near, (1, 1))), beside, behind


def gather_classes(value):
    size = lax.axis_size("blk")
    groups = [list(range(core, size, 2)) for core in range(2)]
    copies = jnp.broadcast_to(value[None], (size // 2, *value.shape))
    near = lax.all_to_all(copies, "blk", 0, 0, axis_index_groups=groups)
    return near, swapped(near, (1, 1))


def body(
    features,
    node_order,
    tile_values,
    tile_rows,
    tile_columns,
    tile_live,
    first_weight,
    first_bias,
    second_weight,
    second_bias,
):
    tile, width = features.shape
    slots = tile_values.shape[1]
    reps = lax.axis_size("rep")
    blocks = lax.axis_size("blk")
    hidden, classes = second_weight.shape
    padded = -(-(classes + 1) // 16) * 16
    shape = jax.ShapeDtypeStruct

    def exchanged(sums):
        return [shifted(sums[reps - 1 - step], "rep", step) for step in range(1, reps)]

    own_t = features.T
    others = [shifted(own_t, "rep", step) for step in range(1, reps)]
    live, part, wanted, tiles = call(
        prepare,
        [
            pltpu.SMEM((8,), jnp.int32),
            shape((width, tile), F32),
            shape((1, tile), jnp.int32),
            shape(tile_values.shape[1:], BF16),
        ],
        smem=(tile_live,),
        hbm=(node_order, own_t, tile_values[0]),
        scratch=[
            pltpu.VMEM(node_order.shape, jnp.int32),
            pltpu.VMEM(own_t.shape, BF16),
            pltpu.SemaphoreType.DMA((3,)),
        ],
        smem_outs=1,
    )
    (ordered,) = call(arrange, [shape((width, tile), BF16)], vmem=(part, wanted, *others))

    def staged(after):
        return call(
            functools.partial(stage, reps),
            [
                pltpu.SMEM((2 * slots,), jnp.int32),
                shape((hidden, 1), F32),
                shape((classes, 1), F32),
                shape((hidden, width), BF16),
                shape((classes, hidden), BF16),
            ],
            vmem=(after,),
            smem=(live,),
            hbm=(
                tile_rows,
                tile_columns,
                first_bias[None],
                second_bias[None],
                first_weight,
                second_weight.T,
            ),
            scratch=[
                pltpu.SMEM((1, slots), jnp.int32),
                pltpu.SMEM((1, slots), jnp.int32),
                pltpu.VMEM((1, hidden), F32),
                pltpu.VMEM((1, classes), F32),
                pltpu.VMEM(first_weight.shape, BF16),
                pltpu.SemaphoreType.DMA((6,)),
            ],
            smem_outs=1,
        )

    def turned(arrived, values):
        return call(
            turn,
            [
                shape(arrived.shape, BF16),
                shape(tiles.shape, BF16),
                shape((reps, 8, tile), F32),
            ],
            vmem=(tiles, arrived),
            smem=(values[0],),
        )

    (near, far), values, (tiles_t, degrees) = gather_features(ordered, staged, turned)
    plan, bias_1, bias_2, weight_1, weight_2 = values
    (projected,) = call(
        project,
        [shape((near.shape[0], hidden, tile), BF16)],
        vmem=(weight_1, near),
    )
    own, *sums = call(
        aggregate_hidden,
        [shape((hidden, tile), F32)] + [shape((hidden + ONES_ROWS, tile), jnp.int16)] * (reps - 1),
        vmem=(projected, far, weight_1, tiles_t, degrees),
        smem=(plan,),
        scratch=[pltpu.VMEM((blocks, hidden, tile), BF16)],
    )
    classes_in, scaling = call(
        combine,
        [shape((padded, tile), BF16), shape((1, tile), F32)],
        vmem=(projected, bias_1, weight_2, degrees, own, *exchanged(sums)),
    )
    own, *sums = call(
        aggregate_classes,
        [shape((padded, tile), F32)] + [shape((padded, tile), jnp.int16)] * (reps - 1),
        vmem=(*gather_classes(classes_in), tiles_t),
        smem=(plan,),
        scratch=[pltpu.VMEM((blocks, padded, tile), BF16)],
    )
    (logits,) = call(
        finish,
        [shape((classes, tile), F32)],
        vmem=(classes_in, scaling, bias_2, own, *exchanged(sums)),
    )
    return logits.T


def solution(mesh):
    placed = (
        P(("blk", "rep"), None),
        P("blk", None),
        P(("blk", "rep"), None, None, None),
        P(("blk", "rep"), None),
        P(("blk", "rep"), None),
        P(("blk", "rep")),
        P(),
        P(),
        P(),
        P(),
    )
    return jax.shard_map(
        body, mesh=mesh, in_specs=placed, out_specs=P(("blk", "rep"), None), check_vma=False
    )
```

```python
import functools

import jax
import jax.numpy as jnp
from jax import lax
from jax.experimental import pallas as pl
from jax.experimental.pallas import tpu as pltpu
from jax.sharding import PartitionSpec as P

BF16 = jnp.bfloat16
F32 = jnp.float32
ONES_ROWS = 16
VMEM_LIMIT = 32 * 1024 * 1024


def nn(a, b):
    return lax.dot_general(a, b, (((1,), (0,)), ((), ())), preferred_element_type=F32)


def nt(a, b):
    return lax.dot_general(a, b, (((1,), (1,)), ((), ())), preferred_element_type=F32)


def in_smem(value):
    return value if value.size == 1 else pltpu.with_memory_space_constraint(value, pltpu.SMEM)


def call(kernel, outs, smem=(), vmem=(), hbm=(), scratch=(), smem_outs=0, cost=1 << 20):
    spaces = [pltpu.VMEM] * len(vmem) + [pltpu.SMEM] * len(smem) + [pltpu.HBM] * len(hbm)
    out_spaces = [pltpu.SMEM] * smem_outs + [pltpu.VMEM] * (len(outs) - smem_outs)
    return pl.pallas_call(
        kernel,
        out_shape=outs,
        in_specs=[pl.BlockSpec(memory_space=space) for space in spaces],
        out_specs=[pl.BlockSpec(memory_space=space) for space in out_spaces],
        scratch_shapes=scratch,
        compiler_params=pltpu.CompilerParams(vmem_limit_bytes=VMEM_LIMIT),
        cost_estimate=pl.CostEstimate(flops=cost, bytes_accessed=cost, transcendentals=0),
    )(*vmem, *[in_smem(value) for value in smem], *[pltpu.with_memory_space_constraint(value, pltpu.HBM) for value in hbm])


def fetched(sources, targets, sems):
    copies = [
        pltpu.make_async_copy(source, target, sems.at[index])
        for index, (source, target) in enumerate(zip(sources, targets))
    ]
    for copy in copies:
        copy.start()
    return copies


def picked(features, wanted, owner):
    tile = features.shape[1]
    source = lax.broadcasted_iota(jnp.int32, (tile, tile), 0) + owner * tile
    return nn(features[...], jnp.where(source == wanted, 1.0, 0.0).astype(BF16))


def prepare(reps, live, *refs):
    order, features, tiles, rows, columns, *sources = refs[:9]
    plan, part, wanted_out, tiles_out, bias_1, bias_2, weight_1, weight_2 = refs[9:17]
    order_in, features_in, rows_in, columns_in, row_1, row_2, weight_in, sems = refs[17:]
    copies = fetched(
        (order, features, rows, columns, *sources, tiles),
        (order_in, features_in, rows_in, columns_in, row_1, row_2, weight_in, weight_2, tiles_out),
        sems,
    )
    for copy in copies[:7]:
        copy.wait()
    tile = features.shape[1]
    slots = rows_in.shape[1]
    blocks = lax.axis_size("blk")
    block, member = lax.axis_index("blk"), lax.axis_index("rep")
    wanted = order_in[:, pl.ds(pl.multiple_of(member * tile, tile), tile)]
    wanted_out[...] = wanted
    part[...] = picked(features_in, wanted, member)
    bias_1[...] = jnp.broadcast_to(row_1[...], (8, row_1.shape[1])).T[:, :1]
    bias_2[...] = jnp.broadcast_to(row_2[...], (8, row_2.shape[1])).T[:, :1]
    weight_1[...] = weight_in[...].astype(F32).T.astype(BF16)
    for slot in range(slots):
        plan[slot] = lax.clamp(0, columns_in[0, slot] // reps, blocks - 1) ^ block
        local = rows_in[0, slot] - block * reps
        step = lax.rem(local - member + reps, reps)
        plan[slots + slot] = jnp.where((slot < live[0]) & (local >= 0) & (local < reps), step, -1)
    for copy in copies[7:]:
        copy.wait()


def arrange(part, wanted, *rest):
    *features, out = rest
    reps = len(features) + 1
    member = lax.axis_index("rep")
    total = part[...]
    for step in range(1, reps):
        owner = lax.rem(member + step, reps)
        total = total + picked(features[step - 1], wanted[...], owner)
    out[...] = total.astype(BF16)


def project(weight_t, stack, out):
    for index in range(stack.shape[0]):
        out[index] = nn(weight_t[...], stack[index]).astype(BF16)


def turn(tiles, plan, tiles_t, degrees):
    slots, tile = tiles.shape[0], tiles.shape[1]
    count = degrees.shape[0]
    total = jnp.zeros((count * ONES_ROWS, tile), F32)
    for slot in range(slots):
        values = tiles[slot]
        tiles_t[slot] = values.T
        ones = [
            jnp.full((ONES_ROWS, tile), (plan[slots + slot] == step).astype(F32), F32).astype(BF16)
            for step in range(count)
        ]
        total = total + nt(jnp.concatenate(ones, axis=0), values)
    for step in range(count):
        degrees[step] = total[step * ONES_ROWS : step * ONES_ROWS + 8]


def summed(panels, plan, tiles_t, count):
    slots, tile = tiles_t.shape[0], tiles_t.shape[1]
    height = panels.shape[1]
    total = jnp.zeros((count * height, tile), F32)
    for slot in range(slots):
        values = panels[plan[slot]]
        pieces = [
            values * (plan[slots + slot] == step).astype(F32).astype(BF16) for step in range(count)
        ]
        total = total + nn(jnp.concatenate(pieces, axis=0), tiles_t[slot])
    return [total[step * height : (step + 1) * height] for step in range(count)]


def coded(values):
    top = jnp.max(jnp.abs(values), axis=0, keepdims=True)
    power = jnp.ceil(jnp.log2(jnp.maximum(top, 1e-30)))
    return jnp.round(values * jnp.exp2(14.0 - power)).astype(jnp.int32), power.astype(jnp.int32)


def decoded(codes, power):
    return codes.astype(F32) * jnp.exp2(power.astype(F32) - 14.0)


def in_thirds(row):
    first = jnp.floor(row)
    second = jnp.floor((row - first) * 16384.0)
    third = jnp.round(((row - first) * 16384.0 - second) * 16384.0)
    return [part.astype(jnp.int32) for part in (first, second, third)]


def aggregate_hidden(projected, far, weight_t, tiles_t, degrees, plan, own, *rest):
    others, panels = rest[:-1], rest[-1]
    mine, opposite = panel_order(panels.shape[0] // 4, lax.axis_index("blk") % 2)
    for index, place in enumerate(mine):
        panels[place] = projected[index]
    for index, place in enumerate(opposite):
        panels[place] = nn(weight_t[...], far[index]).astype(BF16)
    sums = summed(panels, plan, tiles_t, 1 + len(others))
    own[...] = sums[0]
    row = lax.broadcasted_iota(jnp.int32, (ONES_ROWS, own.shape[1]), 0)
    for step, (part, out) in enumerate(zip(sums[1:], others), 1):
        codes, power = coded(part)
        terms = jnp.zeros(row.shape, jnp.int32)
        for index, term in enumerate([power, *in_thirds(degrees[step, :1])]):
            terms = jnp.where(row == index, term, terms)
        out[...] = jnp.concatenate([codes, terms], axis=0).astype(jnp.int16)


def aggregate_classes(near, far, tiles_t, plan, own, *rest):
    others, panels = rest[:-1], rest[-1]
    chip = lax.axis_index("blk") // 2
    for index in range(near.shape[0]):
        panels[2 * (index ^ chip)] = near[index]
        panels[2 * (index ^ chip) + 1] = far[index]
    sums = summed(panels, plan, tiles_t, 1 + len(others))
    own[...] = sums[0]
    row = lax.broadcasted_iota(jnp.int32, own.shape, 0)
    for part, out in zip(sums[1:], others):
        codes, power = coded(part)
        out[...] = jnp.where(row == own.shape[0] - 1, power, codes).astype(jnp.int16)


def combine(hidden_in, bias, weight_t, degrees, own, *rest):
    *arrived, out, scale_out = rest
    height = hidden_in.shape[1]
    total, degree = own[...], degrees[0, :1]
    for part in arrived:
        codes = part[...].astype(jnp.int32)
        total = total + decoded(codes[:height], codes[height : height + 1])
        terms = [codes[height + 1 + index : height + 2 + index].astype(F32) for index in range(3)]
        degree = degree + (terms[0] + (terms[1] + terms[2] * 2.0**-14) * 2.0**-14)
    scaling = lax.rsqrt(1.0 + degree)
    hidden = scaling * (total + hidden_in[0].astype(F32)) + bias[...]
    hidden = jnp.maximum(hidden, 0.0).astype(BF16)
    classes = nn(weight_t[...], hidden)
    blank = jnp.zeros((out.shape[0] - classes.shape[0], classes.shape[1]), F32)
    out[...] = jnp.concatenate([classes, blank], axis=0).astype(BF16)
    scale_out[...] = scaling


def finish(classes_in, scaling, bias, own, *rest):
    *arrived, out = rest
    classes = out.shape[0]
    total = own[...]
    for part in arrived:
        codes = part[...].astype(jnp.int32)
        total = total + decoded(codes, codes[-1:])
    whole = total + classes_in[...].astype(F32)
    out[...] = scaling[...] * whole[:classes] + bias[...]


def shifted(value, axis, step):
    size = lax.axis_size(axis)
    return lax.ppermute(value, axis, [((d + step) % size, d) for d in range(size)])


def swapped(value, masks):
    return lax.ppermute(value, "blk", [(d ^ masks[d % 2], d) for d in range(lax.axis_size("blk"))])


def outer_order(outer):
    rest = list(range(2, outer))
    return 1, list(zip(rest[0::2], rest[1::2]))


def two_ways(pairs):
    return pairs, [(pair[1], pair[0]) for pair in pairs]


def panel_order(outer, core):
    first, pairs = outer_order(outer)
    lists = []
    for here in (core, 1 - core):
        early, late = ([4 * jnp.where(here == 0, *sides) for sides in way] for way in two_ways(pairs))
        crossed, over = [apart + 2 for apart in late], [apart + 2 for apart in early]
        lists.append([0, 4 * first, *crossed, *late, *early, 2, 4 * first + 2, *over])
    return lists[0], [apart ^ 1 for apart in lists[1]]


def packed(*parts):
    def pack(*refs):
        for index in range(len(parts)):
            refs[-1][index] = refs[index][...]

    out = jax.ShapeDtypeStruct((len(parts), *parts[0].shape), BF16)
    return call(pack, [out], vmem=parts)[0]


def gather_features(value):
    outer = lax.axis_size("blk") // 4
    first, pairs = outer_order(outer)
    ahead = swapped(value, (4 * first, 4 * first))
    early, late = ([swapped(value, (4 * a, 4 * b)) for a, b in way] for way in two_ways(pairs))
    crossed = [swapped(value, (4 * a + 2, 4 * b + 2)) for a, b in two_ways(pairs)[1]]
    here, early = packed(value, ahead), packed(*early)
    over = [swapped(here, (2, 2)), swapped(early, (2, 2))]
    near = jnp.concatenate([here, packed(*crossed), packed(*late), early, *over])
    return near, swapped(near, (1, 1))


def gather_classes(value):
    size = lax.axis_size("blk")
    groups = [list(range(core, size, 2)) for core in range(2)]
    copies = jnp.broadcast_to(value[None], (size // 2, *value.shape))
    near = lax.all_to_all(copies, "blk", 0, 0, axis_index_groups=groups)
    return near, swapped(near, (1, 1))


def body(
    features,
    node_order,
    tile_values,
    tile_rows,
    tile_columns,
    tile_live,
    first_weight,
    first_bias,
    second_weight,
    second_bias,
):
    tile, width = features.shape
    slots = tile_values.shape[1]
    reps = lax.axis_size("rep")
    blocks = lax.axis_size("blk")
    hidden, classes = second_weight.shape
    padded = -(-(classes + 1) // 16) * 16
    shape = jax.ShapeDtypeStruct

    def exchanged(sums):
        return [shifted(sums[reps - 1 - step], "rep", step) for step in range(1, reps)]

    own_t = features.T
    others = [shifted(own_t, "rep", step) for step in range(1, reps)]
    plan, part, wanted, tiles, bias_1, bias_2, weight_1, weight_2 = call(
        functools.partial(prepare, reps),
        [
            pltpu.SMEM((2 * slots,), jnp.int32),
            shape((width, tile), F32),
            shape((1, tile), jnp.int32),
            shape(tile_values.shape[1:], BF16),
            shape((hidden, 1), F32),
            shape((classes, 1), F32),
            shape((hidden, width), BF16),
            shape((classes, hidden), BF16),
        ],
        smem=(tile_live,),
        hbm=(
            node_order,
            own_t,
            tile_values[0],
            tile_rows,
            tile_columns,
            first_bias[None],
            second_bias[None],
            first_weight,
            second_weight.T,
        ),
        scratch=[
            pltpu.VMEM(node_order.shape, jnp.int32),
            pltpu.VMEM(own_t.shape, BF16),
            pltpu.SMEM((1, slots), jnp.int32),
            pltpu.SMEM((1, slots), jnp.int32),
            pltpu.VMEM((1, hidden), F32),
            pltpu.VMEM((1, classes), F32),
            pltpu.VMEM(first_weight.shape, BF16),
            pltpu.SemaphoreType.DMA((9,)),
        ],
        smem_outs=1,
    )
    (ordered,) = call(arrange, [shape((width, tile), BF16)], vmem=(part, wanted, *others))
    near, far = gather_features(ordered)
    tiles_t, degrees = call(
        turn,
        [shape(tiles.shape, BF16), shape((reps, 8, tile), F32)],
        vmem=(tiles,),
        smem=(plan,),
    )
    (projected,) = call(
        project,
        [shape((near.shape[0], hidden, tile), BF16)],
        vmem=(weight_1, near),
    )
    own, *sums = call(
        aggregate_hidden,
        [shape((hidden, tile), F32)] + [shape((hidden + ONES_ROWS, tile), jnp.int16)] * (reps - 1),
        vmem=(projected, far, weight_1, tiles_t, degrees),
        smem=(plan,),
        scratch=[pltpu.VMEM((blocks, hidden, tile), BF16)],
    )
    classes_in, scaling = call(
        combine,
        [shape((padded, tile), BF16), shape((1, tile), F32)],
        vmem=(projected, bias_1, weight_2, degrees, own, *exchanged(sums)),
    )
    own, *sums = call(
        aggregate_classes,
        [shape((padded, tile), F32)] + [shape((padded, tile), jnp.int16)] * (reps - 1),
        vmem=(*gather_classes(classes_in), tiles_t),
        smem=(plan,),
        scratch=[pltpu.VMEM((blocks, padded, tile), BF16)],
    )
    (logits,) = call(
        finish,
        [shape((classes, tile), F32)],
        vmem=(classes_in, scaling, bias_2, own, *exchanged(sums)),
    )
    return logits.T


def solution(mesh):
    placed = (
        P(("blk", "rep"), None),
        P("blk", None),
        P(("blk", "rep"), None, None, None),
        P(("blk", "rep"), None),
        P(("blk", "rep"), None),
        P(("blk", "rep")),
        P(),
        P(),
        P(),
        P(),
    )
    return jax.shard_map(
        body, mesh=mesh, in_specs=placed, out_specs=P(("blk", "rep"), None), check_vma=False
    )
```

```python
import functools

import jax
import jax.numpy as jnp
from jax import lax
from jax.experimental import pallas as pl
from jax.experimental.pallas import tpu as pltpu
from jax.sharding import PartitionSpec as P

BF16 = jnp.bfloat16
F32 = jnp.float32
ONES_ROWS = 16
VMEM_LIMIT = 32 * 1024 * 1024


def nn(a, b):
    return lax.dot_general(a, b, (((1,), (0,)), ((), ())), preferred_element_type=F32)


def nt(a, b):
    return lax.dot_general(a, b, (((1,), (1,)), ((), ())), preferred_element_type=F32)


def in_smem(value):
    return value if value.size == 1 else pltpu.with_memory_space_constraint(value, pltpu.SMEM)


def call(kernel, outs, smem=(), vmem=(), hbm=(), scratch=(), smem_outs=0, cost=1 << 20):
    spaces = [pltpu.VMEM] * len(vmem) + [pltpu.SMEM] * len(smem) + [pltpu.HBM] * len(hbm)
    out_spaces = [pltpu.SMEM] * smem_outs + [pltpu.VMEM] * (len(outs) - smem_outs)
    return pl.pallas_call(
        kernel,
        out_shape=outs,
        in_specs=[pl.BlockSpec(memory_space=space) for space in spaces],
        out_specs=[pl.BlockSpec(memory_space=space) for space in out_spaces],
        scratch_shapes=scratch,
        compiler_params=pltpu.CompilerParams(vmem_limit_bytes=VMEM_LIMIT),
        cost_estimate=pl.CostEstimate(flops=cost, bytes_accessed=cost, transcendentals=0),
    )(*vmem, *[in_smem(value) for value in smem], *[pltpu.with_memory_space_constraint(value, pltpu.HBM) for value in hbm])


def fetched(sources, targets, sems):
    copies = [
        pltpu.make_async_copy(source, target, sems.at[index])
        for index, (source, target) in enumerate(zip(sources, targets))
    ]
    for copy in copies:
        copy.start()
    return copies


def picked(features, wanted, owner):
    tile = features.shape[1]
    source = lax.broadcasted_iota(jnp.int32, (tile, tile), 0) + owner * tile
    return nn(features[...], jnp.where(source == wanted, 1.0, 0.0).astype(BF16))


def prepare(reps, live, *refs):
    order, features, tiles, rows, columns, *sources = refs[:9]
    plan, part, wanted_out, tiles_out, bias_1, bias_2, weight_1, weight_2 = refs[9:17]
    order_in, features_in, rows_in, columns_in, row_1, row_2, weight_in, sems = refs[17:]
    copies = fetched(
        (order, features, rows, columns, *sources, tiles),
        (order_in, features_in, rows_in, columns_in, row_1, row_2, weight_in, weight_2, tiles_out),
        sems,
    )
    for copy in copies[:7]:
        copy.wait()
    tile = features.shape[1]
    slots = rows_in.shape[1]
    blocks = lax.axis_size("blk")
    block, member = lax.axis_index("blk"), lax.axis_index("rep")
    wanted = order_in[:, pl.ds(pl.multiple_of(member * tile, tile), tile)]
    wanted_out[...] = wanted
    part[...] = picked(features_in, wanted, member)
    bias_1[...] = jnp.broadcast_to(row_1[...], (8, row_1.shape[1])).T[:, :1]
    bias_2[...] = jnp.broadcast_to(row_2[...], (8, row_2.shape[1])).T[:, :1]
    weight_1[...] = weight_in[...].astype(F32).T.astype(BF16)
    for slot in range(slots):
        plan[slot] = lax.clamp(0, columns_in[0, slot] // reps, blocks - 1) ^ block
        local = rows_in[0, slot] - block * reps
        step = lax.rem(local - member + reps, reps)
        plan[slots + slot] = jnp.where((slot < live[0]) & (local >= 0) & (local < reps), step, -1)
    for copy in copies[7:]:
        copy.wait()


def arrange(part, wanted, *rest):
    *features, out = rest
    reps = len(features) + 1
    member = lax.axis_index("rep")
    total = part[...]
    for step in range(1, reps):
        owner = lax.rem(member + step, reps)
        total = total + picked(features[step - 1], wanted[...], owner)
    out[...] = total.astype(BF16)


def project(weight_t, stack, out):
    for index in range(stack.shape[0]):
        out[index] = nn(weight_t[...], stack[index]).astype(BF16)


def turn(tiles, plan, tiles_t, degrees):
    slots, tile = tiles.shape[0], tiles.shape[1]
    count = degrees.shape[0]
    total = jnp.zeros((count * ONES_ROWS, tile), F32)
    for slot in range(slots):
        values = tiles[slot]
        tiles_t[slot] = values.T
        ones = [
            jnp.full((ONES_ROWS, tile), (plan[slots + slot] == step).astype(F32), F32).astype(BF16)
            for step in range(count)
        ]
        total = total + nt(jnp.concatenate(ones, axis=0), values)
    for step in range(count):
        degrees[step] = total[step * ONES_ROWS : step * ONES_ROWS + 8]


def summed(panels, plan, tiles_t, count):
    slots, tile = tiles_t.shape[0], tiles_t.shape[1]
    height = panels.shape[1]
    total = jnp.zeros((count * height, tile), F32)
    for slot in range(slots):
        values = panels[plan[slot]]
        pieces = [
            values * (plan[slots + slot] == step).astype(F32).astype(BF16) for step in range(count)
        ]
        total = total + nn(jnp.concatenate(pieces, axis=0), tiles_t[slot])
    return [total[step * height : (step + 1) * height] for step in range(count)]


def coded(values):
    top = jnp.max(jnp.abs(values), axis=0, keepdims=True)
    power = jnp.ceil(jnp.log2(jnp.maximum(top, 1e-30)))
    return jnp.round(values * jnp.exp2(14.0 - power)).astype(jnp.int32), power.astype(jnp.int32)


def decoded(codes, power):
    return codes.astype(F32) * jnp.exp2(power.astype(F32) - 14.0)


def in_thirds(row):
    first = jnp.floor(row)
    second = jnp.floor((row - first) * 16384.0)
    third = jnp.round(((row - first) * 16384.0 - second) * 16384.0)
    return [part.astype(jnp.int32) for part in (first, second, third)]


def aggregate_hidden(projected, far, weight_t, tiles_t, degrees, plan, own, *rest):
    others, panels = rest[:-1], rest[-1]
    mine, opposite = panel_order(panels.shape[0] // 4, lax.axis_index("blk") % 2)
    for index, place in enumerate(mine):
        panels[place] = projected[index]
    for index, place in enumerate(opposite):
        panels[place] = nn(weight_t[...], far[index]).astype(BF16)
    sums = summed(panels, plan, tiles_t, 1 + len(others))
    own[...] = sums[0]
    row = lax.broadcasted_iota(jnp.int32, (ONES_ROWS, own.shape[1]), 0)
    for step, (part, out) in enumerate(zip(sums[1:], others), 1):
        codes, power = coded(part)
        terms = jnp.zeros(row.shape, jnp.int32)
        for index, term in enumerate([power, *in_thirds(degrees[step, :1])]):
            terms = jnp.where(row == index, term, terms)
        out[...] = jnp.concatenate([codes, terms], axis=0).astype(jnp.int16)


def aggregate_classes(near, far, tiles_t, plan, own, *rest):
    others, panels = rest[:-1], rest[-1]
    mine, opposite = panel_order(panels.shape[0] // 4, lax.axis_index("blk") % 2)
    for index, (here, there) in enumerate(zip(mine, opposite)):
        panels[here] = near[index]
        panels[there] = far[index]
    sums = summed(panels, plan, tiles_t, 1 + len(others))
    own[...] = sums[0]
    row = lax.broadcasted_iota(jnp.int32, own.shape, 0)
    for part, out in zip(sums[1:], others):
        codes, power = coded(part)
        out[...] = jnp.where(row == own.shape[0] - 1, power, codes).astype(jnp.int16)


def combine(hidden_in, bias, weight_t, degrees, own, *rest):
    *arrived, out, scale_out = rest
    height = hidden_in.shape[1]
    total, degree = own[...], degrees[0, :1]
    for part in arrived:
        codes = part[...].astype(jnp.int32)
        total = total + decoded(codes[:height], codes[height : height + 1])
        terms = [codes[height + 1 + index : height + 2 + index].astype(F32) for index in range(3)]
        degree = degree + (terms[0] + (terms[1] + terms[2] * 2.0**-14) * 2.0**-14)
    scaling = lax.rsqrt(1.0 + degree)
    hidden = scaling * (total + hidden_in[0].astype(F32)) + bias[...]
    hidden = jnp.maximum(hidden, 0.0).astype(BF16)
    classes = nn(weight_t[...], hidden)
    blank = jnp.zeros((out.shape[0] - classes.shape[0], classes.shape[1]), F32)
    out[...] = jnp.concatenate([classes, blank], axis=0).astype(BF16)
    scale_out[...] = scaling


def finish(classes_in, scaling, bias, own, *rest):
    *arrived, out = rest
    classes = out.shape[0]
    total = own[...]
    for part in arrived:
        codes = part[...].astype(jnp.int32)
        total = total + decoded(codes, codes[-1:])
    whole = total + classes_in[...].astype(F32)
    out[...] = scaling[...] * whole[:classes] + bias[...]


def shifted(value, axis, step):
    size = lax.axis_size(axis)
    return lax.ppermute(value, axis, [((d + step) % size, d) for d in range(size)])


def swapped(value, masks):
    return lax.ppermute(value, "blk", [(d ^ masks[d % 2], d) for d in range(lax.axis_size("blk"))])


def outer_order(outer):
    rest = list(range(2, outer))
    return 1, list(zip(rest[0::2], rest[1::2]))


def two_ways(pairs):
    return pairs, [(pair[1], pair[0]) for pair in pairs]


def panel_order(outer, core):
    first, pairs = outer_order(outer)
    lists = []
    for here in (core, 1 - core):
        early, late = ([4 * jnp.where(here == 0, *sides) for sides in way] for way in two_ways(pairs))
        over = [apart + 2 for apart in [0, 4 * first, *early, *late]]
        lists.append([0, 4 * first, *late, *early, *over])
    return lists[0], [apart ^ 1 for apart in lists[1]]


def packed(*parts):
    def pack(*refs):
        for index in range(len(parts)):
            refs[-1][index] = refs[index][...]

    out = jax.ShapeDtypeStruct((len(parts), *parts[0].shape), BF16)
    return call(pack, [out], vmem=parts)[0]


def gather(value):
    outer = lax.axis_size("blk") // 4
    first, pairs = outer_order(outer)
    ahead = swapped(value, (4 * first, 4 * first))
    early, late = ([swapped(value, (4 * a, 4 * b)) for a, b in way] for way in two_ways(pairs))
    stacks = packed(value, ahead), packed(*early), packed(*late)
    over = [swapped(stack, (2, 2)) for stack in stacks]
    near = jnp.concatenate([stacks[0], stacks[2], stacks[1], *over])
    return near, swapped(near, (1, 1))


def body(
    features,
    node_order,
    tile_values,
    tile_rows,
    tile_columns,
    tile_live,
    first_weight,
    first_bias,
    second_weight,
    second_bias,
):
    tile, width = features.shape
    slots = tile_values.shape[1]
    reps = lax.axis_size("rep")
    blocks = lax.axis_size("blk")
    hidden, classes = second_weight.shape
    padded = -(-(classes + 1) // 16) * 16
    shape = jax.ShapeDtypeStruct

    def exchanged(sums):
        return [shifted(sums[reps - 1 - step], "rep", step) for step in range(1, reps)]

    own_t = features.T
    others = [shifted(own_t, "rep", step) for step in range(1, reps)]
    plan, part, wanted, tiles, bias_1, bias_2, weight_1, weight_2 = call(
        functools.partial(prepare, reps),
        [
            pltpu.SMEM((2 * slots,), jnp.int32),
            shape((width, tile), F32),
            shape((1, tile), jnp.int32),
            shape(tile_values.shape[1:], BF16),
            shape((hidden, 1), F32),
            shape((classes, 1), F32),
            shape((hidden, width), BF16),
            shape((classes, hidden), BF16),
        ],
        smem=(tile_live,),
        hbm=(
            node_order,
            own_t,
            tile_values[0],
            tile_rows,
            tile_columns,
            first_bias[None],
            second_bias[None],
            first_weight,
            second_weight.T,
        ),
        scratch=[
            pltpu.VMEM(node_order.shape, jnp.int32),
            pltpu.VMEM(own_t.shape, BF16),
            pltpu.SMEM((1, slots), jnp.int32),
            pltpu.SMEM((1, slots), jnp.int32),
            pltpu.VMEM((1, hidden), F32),
            pltpu.VMEM((1, classes), F32),
            pltpu.VMEM(first_weight.shape, BF16),
            pltpu.SemaphoreType.DMA((9,)),
        ],
        smem_outs=1,
    )
    (ordered,) = call(arrange, [shape((width, tile), BF16)], vmem=(part, wanted, *others))
    near, far = gather(ordered)
    tiles_t, degrees = call(
        turn,
        [shape(tiles.shape, BF16), shape((reps, 8, tile), F32)],
        vmem=(tiles,),
        smem=(plan,),
    )
    (projected,) = call(
        project,
        [shape((near.shape[0], hidden, tile), BF16)],
        vmem=(weight_1, near),
    )
    own, *sums = call(
        aggregate_hidden,
        [shape((hidden, tile), F32)] + [shape((hidden + ONES_ROWS, tile), jnp.int16)] * (reps - 1),
        vmem=(projected, far, weight_1, tiles_t, degrees),
        smem=(plan,),
        scratch=[pltpu.VMEM((blocks, hidden, tile), BF16)],
    )
    classes_in, scaling = call(
        combine,
        [shape((padded, tile), BF16), shape((1, tile), F32)],
        vmem=(projected, bias_1, weight_2, degrees, own, *exchanged(sums)),
    )
    own, *sums = call(
        aggregate_classes,
        [shape((padded, tile), F32)] + [shape((padded, tile), jnp.int16)] * (reps - 1),
        vmem=(*gather(classes_in), tiles_t),
        smem=(plan,),
        scratch=[pltpu.VMEM((blocks, padded, tile), BF16)],
    )
    (logits,) = call(
        finish,
        [shape((classes, tile), F32)],
        vmem=(classes_in, scaling, bias_2, own, *exchanged(sums)),
    )
    return logits.T


def solution(mesh):
    placed = (
        P(("blk", "rep"), None),
        P("blk", None),
        P(("blk", "rep"), None, None, None),
        P(("blk", "rep"), None),
        P(("blk", "rep"), None),
        P(("blk", "rep")),
        P(),
        P(),
        P(),
        P(),
    )
    return jax.shard_map(
        body, mesh=mesh, in_specs=placed, out_specs=P(("blk", "rep"), None), check_vma=False
    )
```

```python
import functools

import jax
import jax.numpy as jnp
from jax import lax
from jax.experimental import pallas as pl
from jax.experimental.pallas import tpu as pltpu
from jax.sharding import PartitionSpec as P

BF16 = jnp.bfloat16
F32 = jnp.float32
ONES_ROWS = 16
VMEM_LIMIT = 32 * 1024 * 1024


def nn(a, b):
    return lax.dot_general(a, b, (((1,), (0,)), ((), ())), preferred_element_type=F32)


def nt(a, b):
    return lax.dot_general(a, b, (((1,), (1,)), ((), ())), preferred_element_type=F32)


def in_smem(value):
    return value if value.size == 1 else pltpu.with_memory_space_constraint(value, pltpu.SMEM)


def call(kernel, outs, smem=(), vmem=(), hbm=(), scratch=(), smem_outs=0, cost=1 << 20):
    spaces = [pltpu.VMEM] * len(vmem) + [pltpu.SMEM] * len(smem) + [pltpu.HBM] * len(hbm)
    out_spaces = [pltpu.SMEM] * smem_outs + [pltpu.VMEM] * (len(outs) - smem_outs)
    return pl.pallas_call(
        kernel,
        out_shape=outs,
        in_specs=[pl.BlockSpec(memory_space=space) for space in spaces],
        out_specs=[pl.BlockSpec(memory_space=space) for space in out_spaces],
        scratch_shapes=scratch,
        compiler_params=pltpu.CompilerParams(vmem_limit_bytes=VMEM_LIMIT),
        cost_estimate=pl.CostEstimate(flops=cost, bytes_accessed=cost, transcendentals=0),
    )(*vmem, *[in_smem(value) for value in smem], *[pltpu.with_memory_space_constraint(value, pltpu.HBM) for value in hbm])


def fetched(sources, targets, sems):
    copies = [
        pltpu.make_async_copy(source, target, sems.at[index])
        for index, (source, target) in enumerate(zip(sources, targets))
    ]
    for copy in copies:
        copy.start()
    return copies


def picked(features, wanted, owner):
    tile = features.shape[1]
    source = lax.broadcasted_iota(jnp.int32, (tile, tile), 0) + owner * tile
    return nn(features[...], jnp.where(source == wanted, 1.0, 0.0).astype(BF16))


def prepare(reps, live, *refs):
    order, features, tiles, rows, columns, *sources = refs[:9]
    plan, part, wanted_out, tiles_out, bias_1, bias_2, weight_1, weight_2 = refs[9:17]
    order_in, features_in, rows_in, columns_in, row_1, row_2, weight_in, sems = refs[17:]
    copies = fetched(
        (order, features, rows, columns, *sources, tiles),
        (order_in, features_in, rows_in, columns_in, row_1, row_2, weight_in, weight_2, tiles_out),
        sems,
    )
    for copy in copies[:7]:
        copy.wait()
    tile = features.shape[1]
    slots = rows_in.shape[1]
    blocks = lax.axis_size("blk")
    block, member = lax.axis_index("blk"), lax.axis_index("rep")
    wanted = order_in[:, pl.ds(pl.multiple_of(member * tile, tile), tile)]
    wanted_out[...] = wanted
    part[...] = picked(features_in, wanted, member)
    bias_1[...] = jnp.broadcast_to(row_1[...], (8, row_1.shape[1])).T[:, :1]
    bias_2[...] = jnp.broadcast_to(row_2[...], (8, row_2.shape[1])).T[:, :1]
    weight_1[...] = weight_in[...].astype(F32).T.astype(BF16)
    for slot in range(slots):
        plan[slot] = lax.clamp(0, columns_in[0, slot] // reps, blocks - 1) ^ block
        local = rows_in[0, slot] - block * reps
        step = lax.rem(local - member + reps, reps)
        plan[slots + slot] = jnp.where((slot < live[0]) & (local >= 0) & (local < reps), step, -1)
    for copy in copies[7:]:
        copy.wait()


def arrange(part, wanted, *rest):
    *features, out = rest
    reps = len(features) + 1
    member = lax.axis_index("rep")
    total = part[...]
    for step in range(1, reps):
        owner = lax.rem(member + step, reps)
        total = total + picked(features[step - 1], wanted[...], owner)
    out[...] = total.astype(BF16)


def project(weight_t, stack, out):
    for index in range(stack.shape[0]):
        out[index] = nn(weight_t[...], stack[index]).astype(BF16)


def turn(tiles, plan, tiles_t, degrees):
    slots, tile = tiles.shape[0], tiles.shape[1]
    count = degrees.shape[0]
    total = jnp.zeros((count * ONES_ROWS, tile), F32)
    for slot in range(slots):
        values = tiles[slot]
        tiles_t[slot] = values.T
        ones = [
            jnp.full((ONES_ROWS, tile), (plan[slots + slot] == step).astype(F32), F32).astype(BF16)
            for step in range(count)
        ]
        total = total + nt(jnp.concatenate(ones, axis=0), values)
    for step in range(count):
        degrees[step] = total[step * ONES_ROWS : step * ONES_ROWS + 8]


def summed(panels, plan, tiles_t, count):
    slots, tile = tiles_t.shape[0], tiles_t.shape[1]
    height = panels.shape[1]
    total = jnp.zeros((count * height, tile), F32)
    for slot in range(slots):
        values = panels[plan[slot]]
        pieces = [
            values * (plan[slots + slot] == step).astype(F32).astype(BF16) for step in range(count)
        ]
        total = total + nn(jnp.concatenate(pieces, axis=0), tiles_t[slot])
    return [total[step * height : (step + 1) * height] for step in range(count)]


def coded(values):
    top = jnp.max(jnp.abs(values), axis=0, keepdims=True)
    power = jnp.ceil(jnp.log2(jnp.maximum(top, 1e-30)))
    return jnp.round(values * jnp.exp2(14.0 - power)).astype(jnp.int32), power.astype(jnp.int32)


def decoded(codes, power):
    return codes.astype(F32) * jnp.exp2(power.astype(F32) - 14.0)


def in_thirds(row):
    first = jnp.floor(row)
    second = jnp.floor((row - first) * 16384.0)
    third = jnp.round(((row - first) * 16384.0 - second) * 16384.0)
    return [part.astype(jnp.int32) for part in (first, second, third)]


def aggregate_hidden(projected, far, weight_t, tiles_t, degrees, plan, own, *rest):
    others, panels = rest[:-1], rest[-1]
    mine, opposite = panel_order(panels.shape[0] // 4, lax.axis_index("blk") % 2)
    for index, place in enumerate(mine):
        panels[place] = projected[index]
    for index, place in enumerate(opposite):
        panels[place] = nn(weight_t[...], far[index]).astype(BF16)
    sums = summed(panels, plan, tiles_t, 1 + len(others))
    own[...] = sums[0]
    row = lax.broadcasted_iota(jnp.int32, (ONES_ROWS, own.shape[1]), 0)
    for step, (part, out) in enumerate(zip(sums[1:], others), 1):
        codes, power = coded(part)
        terms = jnp.zeros(row.shape, jnp.int32)
        for index, term in enumerate([power, *in_thirds(degrees[step, :1])]):
            terms = jnp.where(row == index, term, terms)
        out[...] = jnp.concatenate([codes, terms], axis=0).astype(jnp.int16)


def aggregate_classes(near, far, tiles_t, plan, own, *rest):
    others, panels = rest[:-1], rest[-1]
    chip = lax.axis_index("blk") // 2
    for index in range(near.shape[0]):
        panels[2 * (index ^ chip)] = near[index]
        panels[2 * (index ^ chip) + 1] = far[index]
    sums = summed(panels, plan, tiles_t, 1 + len(others))
    own[...] = sums[0]
    row = lax.broadcasted_iota(jnp.int32, own.shape, 0)
    for part, out in zip(sums[1:], others):
        codes, power = coded(part)
        out[...] = jnp.where(row == own.shape[0] - 1, power, codes).astype(jnp.int16)


def combine(hidden_in, bias, weight_t, degrees, own, *rest):
    *arrived, out, scale_out = rest
    height = hidden_in.shape[1]
    total, degree = own[...], degrees[0, :1]
    for part in arrived:
        codes = part[...].astype(jnp.int32)
        total = total + decoded(codes[:height], codes[height : height + 1])
        terms = [codes[height + 1 + index : height + 2 + index].astype(F32) for index in range(3)]
        degree = degree + (terms[0] + (terms[1] + terms[2] * 2.0**-14) * 2.0**-14)
    scaling = lax.rsqrt(1.0 + degree)
    hidden = scaling * (total + hidden_in[0].astype(F32)) + bias[...]
    hidden = jnp.maximum(hidden, 0.0).astype(BF16)
    classes = nn(weight_t[...], hidden)
    blank = jnp.zeros((out.shape[0] - classes.shape[0], classes.shape[1]), F32)
    out[...] = jnp.concatenate([classes, blank], axis=0).astype(BF16)
    scale_out[...] = scaling


def finish(classes_in, scaling, bias, own, *rest):
    *arrived, out = rest
    classes = out.shape[0]
    total = own[...]
    for part in arrived:
        codes = part[...].astype(jnp.int32)
        total = total + decoded(codes, codes[-1:])
    whole = total + classes_in[...].astype(F32)
    out[...] = scaling[...] * whole[:classes] + bias[...]


def shifted(value, axis, step):
    size = lax.axis_size(axis)
    return lax.ppermute(value, axis, [((d + step) % size, d) for d in range(size)])


def swapped(value, masks):
    size = lax.axis_size("blk")
    pairs = [(d ^ masks[d % 2], d) for d in range(size) if masks[d % 2] is not None]
    return lax.ppermute(value, "blk", pairs)


def outer_order(outer):
    rest = list(range(2, outer))
    return 1, list(zip(rest[0::2], rest[1::2]))


def two_ways(pairs):
    return pairs, [(pair[1], pair[0]) for pair in pairs]


def panel_order(outer, core):
    first, pairs = outer_order(outer)
    lists = []
    for here in (core, 1 - core):
        early, late = ([4 * jnp.where(here == 0, *sides) for sides in way] for way in two_ways(pairs))
        crossed, over = [apart + 2 for apart in late], [apart + 2 for apart in early]
        lists.append([0, 4 * first, *late, *crossed, *early, 2, 4 * first + 2, *over])
    return lists[0], [apart ^ 1 for apart in lists[1]]


def packed(*parts):
    def pack(*refs):
        for index in range(len(parts)):
            refs[-1][index] = refs[index][...]

    out = jax.ShapeDtypeStruct((len(parts), *parts[0].shape), BF16)
    return call(pack, [out], vmem=parts)[0]


def gather_features(value):
    outer = lax.axis_size("blk") // 4
    first, pairs = outer_order(outer)
    ahead = swapped(value, (4 * first, 4 * first))
    early, late = ([swapped(value, (4 * a, 4 * b)) for a, b in way] for way in two_ways(pairs))
    crossed = [swapped(value, (4 * a + 2, None)) for a, b in two_ways(pairs)[1]]
    here, early, late = packed(value, ahead), packed(*early), packed(*late)
    over = [swapped(here, (2, 2)), swapped(early, (2, 2))]
    beyond = swapped(late, (None, 2)) + jnp.stack(crossed)
    near = jnp.concatenate([here, late, beyond, early, *over])
    return near, swapped(near, (1, 1))


def gather_classes(value):
    size = lax.axis_size("blk")
    groups = [list(range(core, size, 2)) for core in range(2)]
    copies = jnp.broadcast_to(value[None], (size // 2, *value.shape))
    near = lax.all_to_all(copies, "blk", 0, 0, axis_index_groups=groups)
    return near, swapped(near, (1, 1))


def body(
    features,
    node_order,
    tile_values,
    tile_rows,
    tile_columns,
    tile_live,
    first_weight,
    first_bias,
    second_weight,
    second_bias,
):
    tile, width = features.shape
    slots = tile_values.shape[1]
    reps = lax.axis_size("rep")
    blocks = lax.axis_size("blk")
    hidden, classes = second_weight.shape
    padded = -(-(classes + 1) // 16) * 16
    shape = jax.ShapeDtypeStruct

    def exchanged(sums):
        return [shifted(sums[reps - 1 - step], "rep", step) for step in range(1, reps)]

    own_t = features.T
    others = [shifted(own_t, "rep", step) for step in range(1, reps)]
    plan, part, wanted, tiles, bias_1, bias_2, weight_1, weight_2 = call(
        functools.partial(prepare, reps),
        [
            pltpu.SMEM((2 * slots,), jnp.int32),
            shape((width, tile), F32),
            shape((1, tile), jnp.int32),
            shape(tile_values.shape[1:], BF16),
            shape((hidden, 1), F32),
            shape((classes, 1), F32),
            shape((hidden, width), BF16),
            shape((classes, hidden), BF16),
        ],
        smem=(tile_live,),
        hbm=(
            node_order,
            own_t,
            tile_values[0],
            tile_rows,
            tile_columns,
            first_bias[None],
            second_bias[None],
            first_weight,
            second_weight.T,
        ),
        scratch=[
            pltpu.VMEM(node_order.shape, jnp.int32),
            pltpu.VMEM(own_t.shape, BF16),
            pltpu.SMEM((1, slots), jnp.int32),
            pltpu.SMEM((1, slots), jnp.int32),
            pltpu.VMEM((1, hidden), F32),
            pltpu.VMEM((1, classes), F32),
            pltpu.VMEM(first_weight.shape, BF16),
            pltpu.SemaphoreType.DMA((9,)),
        ],
        smem_outs=1,
    )
    (ordered,) = call(arrange, [shape((width, tile), BF16)], vmem=(part, wanted, *others))
    near, far = gather_features(ordered)
    tiles_t, degrees = call(
        turn,
        [shape(tiles.shape, BF16), shape((reps, 8, tile), F32)],
        vmem=(tiles,),
        smem=(plan,),
    )
    (projected,) = call(
        project,
        [shape((near.shape[0], hidden, tile), BF16)],
        vmem=(weight_1, near),
    )
    own, *sums = call(
        aggregate_hidden,
        [shape((hidden, tile), F32)] + [shape((hidden + ONES_ROWS, tile), jnp.int16)] * (reps - 1),
        vmem=(projected, far, weight_1, tiles_t, degrees),
        smem=(plan,),
        scratch=[pltpu.VMEM((blocks, hidden, tile), BF16)],
    )
    classes_in, scaling = call(
        combine,
        [shape((padded, tile), BF16), shape((1, tile), F32)],
        vmem=(projected, bias_1, weight_2, degrees, own, *exchanged(sums)),
    )
    own, *sums = call(
        aggregate_classes,
        [shape((padded, tile), F32)] + [shape((padded, tile), jnp.int16)] * (reps - 1),
        vmem=(*gather_classes(classes_in), tiles_t),
        smem=(plan,),
        scratch=[pltpu.VMEM((blocks, padded, tile), BF16)],
    )
    (logits,) = call(
        finish,
        [shape((classes, tile), F32)],
        vmem=(classes_in, scaling, bias_2, own, *exchanged(sums)),
    )
    return logits.T


def solution(mesh):
    placed = (
        P(("blk", "rep"), None),
        P("blk", None),
        P(("blk", "rep"), None, None, None),
        P(("blk", "rep"), None),
        P(("blk", "rep"), None),
        P(("blk", "rep")),
        P(),
        P(),
        P(),
        P(),
    )
    return jax.shard_map(
        body, mesh=mesh, in_specs=placed, out_specs=P(("blk", "rep"), None), check_vma=False
    )
```

```python
import functools

import jax
import jax.numpy as jnp
from jax import lax
from jax.experimental import pallas as pl
from jax.experimental.pallas import tpu as pltpu
from jax.sharding import PartitionSpec as P

BF16 = jnp.bfloat16
F32 = jnp.float32
ONES_ROWS = 16
VMEM_LIMIT = 32 * 1024 * 1024


def nn(a, b):
    return lax.dot_general(a, b, (((1,), (0,)), ((), ())), preferred_element_type=F32)


def nt(a, b):
    return lax.dot_general(a, b, (((1,), (1,)), ((), ())), preferred_element_type=F32)


def in_smem(value):
    return value if value.size == 1 else pltpu.with_memory_space_constraint(value, pltpu.SMEM)


def call(kernel, outs, smem=(), vmem=(), hbm=(), scratch=(), smem_outs=0, cost=1 << 20):
    spaces = [pltpu.VMEM] * len(vmem) + [pltpu.SMEM] * len(smem) + [pltpu.HBM] * len(hbm)
    out_spaces = [pltpu.SMEM] * smem_outs + [pltpu.VMEM] * (len(outs) - smem_outs)
    return pl.pallas_call(
        kernel,
        out_shape=outs,
        in_specs=[pl.BlockSpec(memory_space=space) for space in spaces],
        out_specs=[pl.BlockSpec(memory_space=space) for space in out_spaces],
        scratch_shapes=scratch,
        compiler_params=pltpu.CompilerParams(vmem_limit_bytes=VMEM_LIMIT),
        cost_estimate=pl.CostEstimate(flops=cost, bytes_accessed=cost, transcendentals=0),
    )(*vmem, *[in_smem(value) for value in smem], *[pltpu.with_memory_space_constraint(value, pltpu.HBM) for value in hbm])


def fetched(sources, targets, sems):
    copies = [
        pltpu.make_async_copy(source, target, sems.at[index])
        for index, (source, target) in enumerate(zip(sources, targets))
    ]
    for copy in copies:
        copy.start()
    return copies


def picked(features, wanted, owner):
    tile = features.shape[1]
    source = lax.broadcasted_iota(jnp.int32, (tile, tile), 0) + owner * tile
    return nn(features[...], jnp.where(source == wanted, 1.0, 0.0).astype(BF16))


def prepare(reps, live, *refs):
    order, features, tiles, rows, columns, *sources = refs[:9]
    plan, part, wanted_out, tiles_out, bias_1, bias_2, weight_1, weight_2 = refs[9:17]
    order_in, features_in, rows_in, columns_in, row_1, row_2, weight_in, sems = refs[17:]
    copies = fetched(
        (order, features, rows, columns, *sources, tiles),
        (order_in, features_in, rows_in, columns_in, row_1, row_2, weight_in, weight_2, tiles_out),
        sems,
    )
    for copy in copies[:7]:
        copy.wait()
    tile = features.shape[1]
    slots = rows_in.shape[1]
    blocks = lax.axis_size("blk")
    block, member = lax.axis_index("blk"), lax.axis_index("rep")
    wanted = order_in[:, pl.ds(pl.multiple_of(member * tile, tile), tile)]
    wanted_out[...] = wanted
    part[...] = picked(features_in, wanted, member)
    bias_1[...] = jnp.broadcast_to(row_1[...], (8, row_1.shape[1])).T[:, :1]
    bias_2[...] = jnp.broadcast_to(row_2[...], (8, row_2.shape[1])).T[:, :1]
    weight_1[...] = weight_in[...].astype(F32).T.astype(BF16)
    for slot in range(slots):
        plan[slot] = lax.clamp(0, columns_in[0, slot] // reps, blocks - 1) ^ block
        local = rows_in[0, slot] - block * reps
        step = lax.rem(local - member + reps, reps)
        plan[slots + slot] = jnp.where((slot < live[0]) & (local >= 0) & (local < reps), step, -1)
    for copy in copies[7:]:
        copy.wait()


def arrange(part, wanted, *rest):
    *features, out = rest
    reps = len(features) + 1
    member = lax.axis_index("rep")
    total = part[...]
    for step in range(1, reps):
        owner = lax.rem(member + step, reps)
        total = total + picked(features[step - 1], wanted[...], owner)
    out[...] = total.astype(BF16)


def project(weight_t, stack, out):
    for index in range(stack.shape[0]):
        out[index] = nn(weight_t[...], stack[index]).astype(BF16)


def turn(tiles, plan, tiles_t, degrees):
    slots, tile = tiles.shape[0], tiles.shape[1]
    count = degrees.shape[0]
    total = jnp.zeros((count * ONES_ROWS, tile), F32)
    for slot in range(slots):
        values = tiles[slot]
        tiles_t[slot] = values.T
        ones = [
            jnp.full((ONES_ROWS, tile), (plan[slots + slot] == step).astype(F32), F32).astype(BF16)
            for step in range(count)
        ]
        total = total + nt(jnp.concatenate(ones, axis=0), values)
    for step in range(count):
        degrees[step] = total[step * ONES_ROWS : step * ONES_ROWS + 8]


def summed(panels, plan, tiles_t, count):
    slots, tile = tiles_t.shape[0], tiles_t.shape[1]
    height = panels.shape[1]
    total = jnp.zeros((count * height, tile), F32)
    for slot in range(slots):
        values = panels[plan[slot]]
        pieces = [
            values * (plan[slots + slot] == step).astype(F32).astype(BF16) for step in range(count)
        ]
        total = total + nn(jnp.concatenate(pieces, axis=0), tiles_t[slot])
    return [total[step * height : (step + 1) * height] for step in range(count)]


def coded(values):
    top = jnp.max(jnp.abs(values), axis=0, keepdims=True)
    power = jnp.ceil(jnp.log2(jnp.maximum(top, 1e-30)))
    return jnp.round(values * jnp.exp2(14.0 - power)).astype(jnp.int32), power.astype(jnp.int32)


def decoded(codes, power):
    return codes.astype(F32) * jnp.exp2(power.astype(F32) - 14.0)


def in_thirds(row):
    first = jnp.floor(row)
    second = jnp.floor((row - first) * 16384.0)
    third = jnp.round(((row - first) * 16384.0 - second) * 16384.0)
    return [part.astype(jnp.int32) for part in (first, second, third)]


def aggregate_hidden(projected, far, weight_t, tiles_t, degrees, plan, own, *rest):
    others, panels = rest[:-1], rest[-1]
    mine, opposite = panel_order(panels.shape[0] // 4, lax.axis_index("blk") % 2)
    for index, place in enumerate(mine):
        panels[place] = projected[index]
    for index, place in enumerate(opposite):
        panels[place] = nn(weight_t[...], far[index]).astype(BF16)
    sums = summed(panels, plan, tiles_t, 1 + len(others))
    own[...] = sums[0]
    row = lax.broadcasted_iota(jnp.int32, (ONES_ROWS, own.shape[1]), 0)
    for step, (part, out) in enumerate(zip(sums[1:], others), 1):
        codes, power = coded(part)
        terms = jnp.zeros(row.shape, jnp.int32)
        for index, term in enumerate([power, *in_thirds(degrees[step, :1])]):
            terms = jnp.where(row == index, term, terms)
        out[...] = jnp.concatenate([codes, terms], axis=0).astype(jnp.int16)


def aggregate_classes(near, far, tiles_t, plan, own, *rest):
    others, panels = rest[:-1], rest[-1]
    chip = lax.axis_index("blk") // 2
    for index in range(near.shape[0]):
        panels[2 * (index ^ chip)] = near[index]
        panels[2 * (index ^ chip) + 1] = far[index]
    sums = summed(panels, plan, tiles_t, 1 + len(others))
    own[...] = sums[0]
    row = lax.broadcasted_iota(jnp.int32, own.shape, 0)
    for part, out in zip(sums[1:], others):
        codes, power = coded(part)
        out[...] = jnp.where(row == own.shape[0] - 1, power, codes).astype(jnp.int16)


def combine(hidden_in, bias, weight_t, degrees, own, *rest):
    *arrived, out, scale_out = rest
    height = hidden_in.shape[1]
    total, degree = own[...], degrees[0, :1]
    for part in arrived:
        codes = part[...].astype(jnp.int32)
        total = total + decoded(codes[:height], codes[height : height + 1])
        terms = [codes[height + 1 + index : height + 2 + index].astype(F32) for index in range(3)]
        degree = degree + (terms[0] + (terms[1] + terms[2] * 2.0**-14) * 2.0**-14)
    scaling = lax.rsqrt(1.0 + degree)
    hidden = scaling * (total + hidden_in[0].astype(F32)) + bias[...]
    hidden = jnp.maximum(hidden, 0.0).astype(BF16)
    classes = nn(weight_t[...], hidden)
    blank = jnp.zeros((out.shape[0] - classes.shape[0], classes.shape[1]), F32)
    out[...] = jnp.concatenate([classes, blank], axis=0).astype(BF16)
    scale_out[...] = scaling


def finish(classes_in, scaling, bias, own, *rest):
    *arrived, out = rest
    classes = out.shape[0]
    total = own[...]
    for part in arrived:
        codes = part[...].astype(jnp.int32)
        total = total + decoded(codes, codes[-1:])
    whole = total + classes_in[...].astype(F32)
    out[...] = scaling[...] * whole[:classes] + bias[...]


def shifted(value, axis, step):
    size = lax.axis_size(axis)
    return lax.ppermute(value, axis, [((d + step) % size, d) for d in range(size)])


def swapped(value, masks):
    return lax.ppermute(value, "blk", [(d ^ masks[d % 2], d) for d in range(lax.axis_size("blk"))])


def outer_steps(outer):
    steps = list(range(1, outer))
    return list(zip(steps[1:] + steps[:1], steps))


def panel_order(outer, core):
    lists = []
    for here in (core, 1 - core):
        first, *rest, last = [4 * jnp.where(here == 0, *sides) for sides in outer_steps(outer)]
        over = [apart + 2 for apart in [0, first, *rest, last]]
        lists.append([0, first, last, *rest, *over])
    return lists[0], [apart ^ 1 for apart in lists[1]]


def packed(*parts):
    def pack(*refs):
        for index in range(len(parts)):
            refs[-1][index] = refs[index][...]

    out = jax.ShapeDtypeStruct((len(parts), *parts[0].shape), BF16)
    return call(pack, [out], vmem=parts)[0]


def gather_features(value):
    outer = lax.axis_size("blk") // 4
    first, *rest, last = [swapped(value, (4 * a, 4 * b)) for a, b in outer_steps(outer)]
    stacks = packed(value, first), packed(*rest), packed(last)
    over = [swapped(stack, (2, 2)) for stack in stacks]
    near = jnp.concatenate([stacks[0], stacks[2], stacks[1], *over])
    return near, swapped(near, (1, 1))


def gather_classes(value):
    size = lax.axis_size("blk")
    groups = [list(range(core, size, 2)) for core in range(2)]
    copies = jnp.broadcast_to(value[None], (size // 2, *value.shape))
    near = lax.all_to_all(copies, "blk", 0, 0, axis_index_groups=groups)
    return near, swapped(near, (1, 1))


def body(
    features,
    node_order,
    tile_values,
    tile_rows,
    tile_columns,
    tile_live,
    first_weight,
    first_bias,
    second_weight,
    second_bias,
):
    tile, width = features.shape
    slots = tile_values.shape[1]
    reps = lax.axis_size("rep")
    blocks = lax.axis_size("blk")
    hidden, classes = second_weight.shape
    padded = -(-(classes + 1) // 16) * 16
    shape = jax.ShapeDtypeStruct

    def exchanged(sums):
        return [shifted(sums[reps - 1 - step], "rep", step) for step in range(1, reps)]

    own_t = features.T
    others = [shifted(own_t, "rep", step) for step in range(1, reps)]
    plan, part, wanted, tiles, bias_1, bias_2, weight_1, weight_2 = call(
        functools.partial(prepare, reps),
        [
            pltpu.SMEM((2 * slots,), jnp.int32),
            shape((width, tile), F32),
            shape((1, tile), jnp.int32),
            shape(tile_values.shape[1:], BF16),
            shape((hidden, 1), F32),
            shape((classes, 1), F32),
            shape((hidden, width), BF16),
            shape((classes, hidden), BF16),
        ],
        smem=(tile_live,),
        hbm=(
            node_order,
            own_t,
            tile_values[0],
            tile_rows,
            tile_columns,
            first_bias[None],
            second_bias[None],
            first_weight,
            second_weight.T,
        ),
        scratch=[
            pltpu.VMEM(node_order.shape, jnp.int32),
            pltpu.VMEM(own_t.shape, BF16),
            pltpu.SMEM((1, slots), jnp.int32),
            pltpu.SMEM((1, slots), jnp.int32),
            pltpu.VMEM((1, hidden), F32),
            pltpu.VMEM((1, classes), F32),
            pltpu.VMEM(first_weight.shape, BF16),
            pltpu.SemaphoreType.DMA((9,)),
        ],
        smem_outs=1,
    )
    (ordered,) = call(arrange, [shape((width, tile), BF16)], vmem=(part, wanted, *others))
    near, far = gather_features(ordered)
    tiles_t, degrees = call(
        turn,
        [shape(tiles.shape, BF16), shape((reps, 8, tile), F32)],
        vmem=(tiles,),
        smem=(plan,),
    )
    (projected,) = call(
        project,
        [shape((near.shape[0], hidden, tile), BF16)],
        vmem=(weight_1, near),
    )
    own, *sums = call(
        aggregate_hidden,
        [shape((hidden, tile), F32)] + [shape((hidden + ONES_ROWS, tile), jnp.int16)] * (reps - 1),
        vmem=(projected, far, weight_1, tiles_t, degrees),
        smem=(plan,),
        scratch=[pltpu.VMEM((blocks, hidden, tile), BF16)],
    )
    classes_in, scaling = call(
        combine,
        [shape((padded, tile), BF16), shape((1, tile), F32)],
        vmem=(projected, bias_1, weight_2, degrees, own, *exchanged(sums)),
    )
    own, *sums = call(
        aggregate_classes,
        [shape((padded, tile), F32)] + [shape((padded, tile), jnp.int16)] * (reps - 1),
        vmem=(*gather_classes(classes_in), tiles_t),
        smem=(plan,),
        scratch=[pltpu.VMEM((blocks, padded, tile), BF16)],
    )
    (logits,) = call(
        finish,
        [shape((classes, tile), F32)],
        vmem=(classes_in, scaling, bias_2, own, *exchanged(sums)),
    )
    return logits.T


def solution(mesh):
    placed = (
        P(("blk", "rep"), None),
        P("blk", None),
        P(("blk", "rep"), None, None, None),
        P(("blk", "rep"), None),
        P(("blk", "rep"), None),
        P(("blk", "rep")),
        P(),
        P(),
        P(),
        P(),
    )
    return jax.shard_map(
        body, mesh=mesh, in_specs=placed, out_specs=P(("blk", "rep"), None), check_vma=False
    )
```

```python
import functools

import jax
import jax.numpy as jnp
from jax import lax
from jax.experimental import pallas as pl
from jax.experimental.pallas import tpu as pltpu
from jax.sharding import PartitionSpec as P

BF16 = jnp.bfloat16
F32 = jnp.float32
ONES_ROWS = 16
VMEM_LIMIT = 32 * 1024 * 1024


def nn(a, b):
    return lax.dot_general(a, b, (((1,), (0,)), ((), ())), preferred_element_type=F32)


def nt(a, b):
    return lax.dot_general(a, b, (((1,), (1,)), ((), ())), preferred_element_type=F32)


def in_smem(value):
    return value if value.size == 1 else pltpu.with_memory_space_constraint(value, pltpu.SMEM)


def call(kernel, outs, smem=(), vmem=(), hbm=(), scratch=(), smem_outs=0, cost=1 << 20):
    spaces = [pltpu.VMEM] * len(vmem) + [pltpu.SMEM] * len(smem) + [pltpu.HBM] * len(hbm)
    out_spaces = [pltpu.SMEM] * smem_outs + [pltpu.VMEM] * (len(outs) - smem_outs)
    return pl.pallas_call(
        kernel,
        out_shape=outs,
        in_specs=[pl.BlockSpec(memory_space=space) for space in spaces],
        out_specs=[pl.BlockSpec(memory_space=space) for space in out_spaces],
        scratch_shapes=scratch,
        compiler_params=pltpu.CompilerParams(vmem_limit_bytes=VMEM_LIMIT),
        cost_estimate=pl.CostEstimate(flops=cost, bytes_accessed=cost, transcendentals=0),
    )(*vmem, *[in_smem(value) for value in smem], *[pltpu.with_memory_space_constraint(value, pltpu.HBM) for value in hbm])


def fetched(sources, targets, sems):
    copies = [
        pltpu.make_async_copy(source, target, sems.at[index])
        for index, (source, target) in enumerate(zip(sources, targets))
    ]
    for copy in copies:
        copy.start()
    return copies


def picked(features, wanted, owner):
    tile = features.shape[1]
    source = lax.broadcasted_iota(jnp.int32, (tile, tile), 0) + owner * tile
    return nn(features[...], jnp.where(source == wanted, 1.0, 0.0).astype(BF16))


def prepare(reps, live, *refs):
    order, features, tiles, rows, columns, *sources = refs[:9]
    plan, part, wanted_out, tiles_out, bias_1, bias_2, weight_1, weight_2 = refs[9:17]
    order_in, features_in, rows_in, columns_in, row_1, row_2, weight_in, sems = refs[17:]
    copies = fetched(
        (order, features, rows, columns, *sources, tiles),
        (order_in, features_in, rows_in, columns_in, row_1, row_2, weight_in, weight_2, tiles_out),
        sems,
    )
    for copy in copies[:7]:
        copy.wait()
    tile = features.shape[1]
    slots = rows_in.shape[1]
    blocks = lax.axis_size("blk")
    block, member = lax.axis_index("blk"), lax.axis_index("rep")
    wanted = order_in[:, pl.ds(pl.multiple_of(member * tile, tile), tile)]
    wanted_out[...] = wanted
    part[...] = picked(features_in, wanted, member)
    bias_1[...] = jnp.broadcast_to(row_1[...], (8, row_1.shape[1])).T[:, :1]
    bias_2[...] = jnp.broadcast_to(row_2[...], (8, row_2.shape[1])).T[:, :1]
    weight_1[...] = weight_in[...].astype(F32).T.astype(BF16)
    for slot in range(slots):
        plan[slot] = lax.clamp(0, columns_in[0, slot] // reps, blocks - 1) ^ block
        local = rows_in[0, slot] - block * reps
        step = lax.rem(local - member + reps, reps)
        plan[slots + slot] = jnp.where((slot < live[0]) & (local >= 0) & (local < reps), step, -1)
    for copy in copies[7:]:
        copy.wait()


def arrange(part, wanted, *rest):
    *features, out = rest
    reps = len(features) + 1
    member = lax.axis_index("rep")
    total = part[...]
    for step in range(1, reps):
        owner = lax.rem(member + step, reps)
        total = total + picked(features[step - 1], wanted[...], owner)
    out[...] = total.astype(BF16)


def project(weight_t, stack, out):
    for index in range(stack.shape[0]):
        out[index] = nn(weight_t[...], stack[index]).astype(BF16)


def turn(tiles, plan, tiles_t, degrees):
    slots, tile = tiles.shape[0], tiles.shape[1]
    count = degrees.shape[0]
    total = jnp.zeros((count * ONES_ROWS, tile), F32)
    for slot in range(slots):
        values = tiles[slot]
        tiles_t[slot] = values.T
        ones = [
            jnp.full((ONES_ROWS, tile), (plan[slots + slot] == step).astype(F32), F32).astype(BF16)
            for step in range(count)
        ]
        total = total + nt(jnp.concatenate(ones, axis=0), values)
    for step in range(count):
        degrees[step] = total[step * ONES_ROWS : step * ONES_ROWS + 8]


def summed(panels, plan, tiles_t, count):
    slots, tile = tiles_t.shape[0], tiles_t.shape[1]
    height = panels.shape[1]
    total = jnp.zeros((count * height, tile), F32)
    for slot in range(slots):
        values = panels[plan[slot]]
        pieces = [
            values * (plan[slots + slot] == step).astype(F32).astype(BF16) for step in range(count)
        ]
        total = total + nn(jnp.concatenate(pieces, axis=0), tiles_t[slot])
    return [total[step * height : (step + 1) * height] for step in range(count)]


def coded(values):
    top = jnp.max(jnp.abs(values), axis=0, keepdims=True)
    power = jnp.ceil(jnp.log2(jnp.maximum(top, 1e-30)))
    return jnp.round(values * jnp.exp2(14.0 - power)).astype(jnp.int32), power.astype(jnp.int32)


def decoded(codes, power):
    return codes.astype(F32) * jnp.exp2(power.astype(F32) - 14.0)


def in_thirds(row):
    first = jnp.floor(row)
    second = jnp.floor((row - first) * 16384.0)
    third = jnp.round(((row - first) * 16384.0 - second) * 16384.0)
    return [part.astype(jnp.int32) for part in (first, second, third)]


def aggregate_hidden(projected, far, weight_t, tiles_t, degrees, plan, own, *rest):
    others, panels = rest[:-1], rest[-1]
    mine, opposite = panel_order(panels.shape[0] // 4, lax.axis_index("blk") % 2)
    for index, place in enumerate(mine):
        panels[place] = projected[index]
    for index, place in enumerate(opposite):
        panels[place] = nn(weight_t[...], far[index]).astype(BF16)
    sums = summed(panels, plan, tiles_t, 1 + len(others))
    own[...] = sums[0]
    row = lax.broadcasted_iota(jnp.int32, (ONES_ROWS, own.shape[1]), 0)
    for step, (part, out) in enumerate(zip(sums[1:], others), 1):
        codes, power = coded(part)
        terms = jnp.zeros(row.shape, jnp.int32)
        for index, term in enumerate([power, *in_thirds(degrees[step, :1])]):
            terms = jnp.where(row == index, term, terms)
        out[...] = jnp.concatenate([codes, terms], axis=0).astype(jnp.int16)


def aggregate_classes(near, far, tiles_t, plan, own, *rest):
    others, panels = rest[:-1], rest[-1]
    chip = lax.axis_index("blk") // 2
    for index in range(near.shape[0]):
        panels[2 * (index ^ chip)] = near[index]
        panels[2 * (index ^ chip) + 1] = far[index]
    sums = summed(panels, plan, tiles_t, 1 + len(others))
    own[...] = sums[0]
    row = lax.broadcasted_iota(jnp.int32, own.shape, 0)
    for part, out in zip(sums[1:], others):
        codes, power = coded(part)
        out[...] = jnp.where(row == own.shape[0] - 1, power, codes).astype(jnp.int16)


def combine(hidden_in, bias, weight_t, degrees, own, *rest):
    *arrived, out, scale_out = rest
    height = hidden_in.shape[1]
    total, degree = own[...], degrees[0, :1]
    for part in arrived:
        codes = part[...].astype(jnp.int32)
        total = total + decoded(codes[:height], codes[height : height + 1])
        terms = [codes[height + 1 + index : height + 2 + index].astype(F32) for index in range(3)]
        degree = degree + (terms[0] + (terms[1] + terms[2] * 2.0**-14) * 2.0**-14)
    scaling = lax.rsqrt(1.0 + degree)
    hidden = scaling * (total + hidden_in[0].astype(F32)) + bias[...]
    hidden = jnp.maximum(hidden, 0.0).astype(BF16)
    classes = nn(weight_t[...], hidden)
    blank = jnp.zeros((out.shape[0] - classes.shape[0], classes.shape[1]), F32)
    out[...] = jnp.concatenate([classes, blank], axis=0).astype(BF16)
    scale_out[...] = scaling


def finish(classes_in, scaling, bias, own, *rest):
    *arrived, out = rest
    classes = out.shape[0]
    total = own[...]
    for part in arrived:
        codes = part[...].astype(jnp.int32)
        total = total + decoded(codes, codes[-1:])
    whole = total + classes_in[...].astype(F32)
    out[...] = scaling[...] * whole[:classes] + bias[...]


def shifted(value, axis, step):
    size = lax.axis_size(axis)
    return lax.ppermute(value, axis, [((d + step) % size, d) for d in range(size)])


def swapped(value, masks):
    return lax.ppermute(value, "blk", [(d ^ masks[d % 2], d) for d in range(lax.axis_size("blk"))])


def outer_order(outer):
    rest = list(range(2, outer))
    return 1, list(zip(rest[0::2], rest[1::2]))


def two_ways(pairs):
    return pairs, [(pair[1], pair[0]) for pair in pairs]


def panel_order(outer, core):
    first, pairs = outer_order(outer)
    lists = []
    for here in (core, 1 - core):
        early, late = ([4 * jnp.where(here == 0, *sides) for sides in way] for way in two_ways(pairs))
        crossed, over = [apart + 2 for apart in late], [apart + 2 for apart in early]
        lists.append([0, 4 * first, 2, 4 * first + 2, *early, *over, *late, *crossed])
    return lists[0], [apart ^ 1 for apart in lists[1]]


def packed(*parts):
    def pack(*refs):
        for index in range(len(parts)):
            refs[-1][index] = refs[index][...]

    out = jax.ShapeDtypeStruct((len(parts), *parts[0].shape), BF16)
    return call(pack, [out], vmem=parts)[0]


def gather_features(value):
    outer = lax.axis_size("blk") // 4
    first, pairs = outer_order(outer)
    ahead = swapped(value, (4 * first, 4 * first))
    early, late = ([swapped(value, (4 * a, 4 * b)) for a, b in way] for way in two_ways(pairs))
    crossed = [swapped(value, (4 * a + 2, 4 * b + 2)) for a, b in two_ways(pairs)[1]]
    here, early = packed(value, ahead), packed(*early)
    over = [swapped(here, (2, 2)), swapped(early, (2, 2))]
    near = jnp.concatenate([here, over[0], early, over[1], packed(*late), packed(*crossed)])
    return near, swapped(near, (1, 1))


def gather_classes(value):
    size = lax.axis_size("blk")
    groups = [list(range(core, size, 2)) for core in range(2)]
    copies = jnp.broadcast_to(value[None], (size // 2, *value.shape))
    near = lax.all_to_all(copies, "blk", 0, 0, axis_index_groups=groups)
    return near, swapped(near, (1, 1))


def body(
    features,
    node_order,
    tile_values,
    tile_rows,
    tile_columns,
    tile_live,
    first_weight,
    first_bias,
    second_weight,
    second_bias,
):
    tile, width = features.shape
    slots = tile_values.shape[1]
    reps = lax.axis_size("rep")
    blocks = lax.axis_size("blk")
    hidden, classes = second_weight.shape
    padded = -(-(classes + 1) // 16) * 16
    shape = jax.ShapeDtypeStruct

    def exchanged(sums):
        return [shifted(sums[reps - 1 - step], "rep", step) for step in range(1, reps)]

    own_t = features.T
    others = [shifted(own_t, "rep", step) for step in range(1, reps)]
    plan, part, wanted, tiles, bias_1, bias_2, weight_1, weight_2 = call(
        functools.partial(prepare, reps),
        [
            pltpu.SMEM((2 * slots,), jnp.int32),
            shape((width, tile), F32),
            shape((1, tile), jnp.int32),
            shape(tile_values.shape[1:], BF16),
            shape((hidden, 1), F32),
            shape((classes, 1), F32),
            shape((hidden, width), BF16),
            shape((classes, hidden), BF16),
        ],
        smem=(tile_live,),
        hbm=(
            node_order,
            own_t,
            tile_values[0],
            tile_rows,
            tile_columns,
            first_bias[None],
            second_bias[None],
            first_weight,
            second_weight.T,
        ),
        scratch=[
            pltpu.VMEM(node_order.shape, jnp.int32),
            pltpu.VMEM(own_t.shape, BF16),
            pltpu.SMEM((1, slots), jnp.int32),
            pltpu.SMEM((1, slots), jnp.int32),
            pltpu.VMEM((1, hidden), F32),
            pltpu.VMEM((1, classes), F32),
            pltpu.VMEM(first_weight.shape, BF16),
            pltpu.SemaphoreType.DMA((9,)),
        ],
        smem_outs=1,
    )
    (ordered,) = call(arrange, [shape((width, tile), BF16)], vmem=(part, wanted, *others))
    near, far = gather_features(ordered)
    tiles_t, degrees = call(
        turn,
        [shape(tiles.shape, BF16), shape((reps, 8, tile), F32)],
        vmem=(tiles,),
        smem=(plan,),
    )
    (projected,) = call(
        project,
        [shape((near.shape[0], hidden, tile), BF16)],
        vmem=(weight_1, near),
    )
    own, *sums = call(
        aggregate_hidden,
        [shape((hidden, tile), F32)] + [shape((hidden + ONES_ROWS, tile), jnp.int16)] * (reps - 1),
        vmem=(projected, far, weight_1, tiles_t, degrees),
        smem=(plan,),
        scratch=[pltpu.VMEM((blocks, hidden, tile), BF16)],
    )
    classes_in, scaling = call(
        combine,
        [shape((padded, tile), BF16), shape((1, tile), F32)],
        vmem=(projected, bias_1, weight_2, degrees, own, *exchanged(sums)),
    )
    own, *sums = call(
        aggregate_classes,
        [shape((padded, tile), F32)] + [shape((padded, tile), jnp.int16)] * (reps - 1),
        vmem=(*gather_classes(classes_in), tiles_t),
        smem=(plan,),
        scratch=[pltpu.VMEM((blocks, padded, tile), BF16)],
    )
    (logits,) = call(
        finish,
        [shape((classes, tile), F32)],
        vmem=(classes_in, scaling, bias_2, own, *exchanged(sums)),
    )
    return logits.T


def solution(mesh):
    placed = (
        P(("blk", "rep"), None),
        P("blk", None),
        P(("blk", "rep"), None, None, None),
        P(("blk", "rep"), None),
        P(("blk", "rep"), None),
        P(("blk", "rep")),
        P(),
        P(),
        P(),
        P(),
    )
    return jax.shard_map(
        body, mesh=mesh, in_specs=placed, out_specs=P(("blk", "rep"), None), check_vma=False
    )
```

```python
import functools

import jax
import jax.numpy as jnp
from jax import lax
from jax.experimental import pallas as pl
from jax.experimental.pallas import tpu as pltpu
from jax.sharding import PartitionSpec as P

BF16 = jnp.bfloat16
F32 = jnp.float32
ONES_ROWS = 16
VMEM_LIMIT = 32 * 1024 * 1024


def nn(a, b):
    return lax.dot_general(a, b, (((1,), (0,)), ((), ())), preferred_element_type=F32)


def nt(a, b):
    return lax.dot_general(a, b, (((1,), (1,)), ((), ())), preferred_element_type=F32)


def in_smem(value):
    return value if value.size == 1 else pltpu.with_memory_space_constraint(value, pltpu.SMEM)


def call(kernel, outs, smem=(), vmem=(), hbm=(), scratch=(), smem_outs=0, cost=1 << 20):
    spaces = [pltpu.VMEM] * len(vmem) + [pltpu.SMEM] * len(smem) + [pltpu.HBM] * len(hbm)
    out_spaces = [pltpu.SMEM] * smem_outs + [pltpu.VMEM] * (len(outs) - smem_outs)
    return pl.pallas_call(
        kernel,
        out_shape=outs,
        in_specs=[pl.BlockSpec(memory_space=space) for space in spaces],
        out_specs=[pl.BlockSpec(memory_space=space) for space in out_spaces],
        scratch_shapes=scratch,
        compiler_params=pltpu.CompilerParams(vmem_limit_bytes=VMEM_LIMIT),
        cost_estimate=pl.CostEstimate(flops=cost, bytes_accessed=cost, transcendentals=0),
    )(*vmem, *[in_smem(value) for value in smem], *[pltpu.with_memory_space_constraint(value, pltpu.HBM) for value in hbm])


def fetched(sources, targets, sems):
    copies = [
        pltpu.make_async_copy(source, target, sems.at[index])
        for index, (source, target) in enumerate(zip(sources, targets))
    ]
    for copy in copies:
        copy.start()
    return copies


def picked(features, wanted, owner):
    tile = features.shape[1]
    source = lax.broadcasted_iota(jnp.int32, (tile, tile), 0) + owner * tile
    return nn(features[...], jnp.where(source == wanted, 1.0, 0.0).astype(BF16))


def prepare(reps, live, *refs):
    order, features, tiles, rows, columns, *sources = refs[:9]
    plan, part, wanted_out, tiles_out, bias_1, bias_2, weight_1, weight_2 = refs[9:17]
    order_in, features_in, rows_in, columns_in, row_1, row_2, weight_in, sems = refs[17:]
    copies = fetched(
        (order, features, rows, columns, *sources, tiles),
        (order_in, features_in, rows_in, columns_in, row_1, row_2, weight_in, weight_2, tiles_out),
        sems,
    )
    for copy in copies[:7]:
        copy.wait()
    tile = features.shape[1]
    slots = rows_in.shape[1]
    blocks = lax.axis_size("blk")
    block, member = lax.axis_index("blk"), lax.axis_index("rep")
    wanted = order_in[:, pl.ds(pl.multiple_of(member * tile, tile), tile)]
    wanted_out[...] = wanted
    part[...] = picked(features_in, wanted, member)
    bias_1[...] = jnp.broadcast_to(row_1[...], (8, row_1.shape[1])).T[:, :1]
    bias_2[...] = jnp.broadcast_to(row_2[...], (8, row_2.shape[1])).T[:, :1]
    weight_1[...] = weight_in[...].astype(F32).T.astype(BF16)
    for slot in range(slots):
        plan[slot] = lax.clamp(0, columns_in[0, slot] // reps, blocks - 1) ^ block
        local = rows_in[0, slot] - block * reps
        step = lax.rem(local - member + reps, reps)
        plan[slots + slot] = jnp.where((slot < live[0]) & (local >= 0) & (local < reps), step, -1)
    for copy in copies[7:]:
        copy.wait()


def arrange(part, wanted, *rest):
    *features, out = rest
    reps = len(features) + 1
    member = lax.axis_index("rep")
    total = part[...]
    for step in range(1, reps):
        owner = lax.rem(member + step, reps)
        total = total + picked(features[step - 1], wanted[...], owner)
    out[...] = total.astype(BF16)


def project(weight_t, stack, out):
    for index in range(stack.shape[0]):
        out[index] = nn(weight_t[...], stack[index]).astype(BF16)


def turn(tiles, plan, tiles_t, degrees):
    slots, tile = tiles.shape[0], tiles.shape[1]
    count = degrees.shape[0]
    total = jnp.zeros((count * ONES_ROWS, tile), F32)
    for slot in range(slots):
        values = tiles[slot]
        tiles_t[slot] = values.T
        ones = [
            jnp.full((ONES_ROWS, tile), (plan[slots + slot] == step).astype(F32), F32).astype(BF16)
            for step in range(count)
        ]
        total = total + nt(jnp.concatenate(ones, axis=0), values)
    for step in range(count):
        degrees[step] = total[step * ONES_ROWS : step * ONES_ROWS + 8]


def summed(panels, plan, tiles_t, count):
    slots, tile = tiles_t.shape[0], tiles_t.shape[1]
    height = panels.shape[1]
    total = jnp.zeros((count * height, tile), F32)
    for slot in range(slots):
        values = panels[plan[slot]]
        pieces = [
            values * (plan[slots + slot] == step).astype(F32).astype(BF16) for step in range(count)
        ]
        total = total + nn(jnp.concatenate(pieces, axis=0), tiles_t[slot])
    return [total[step * height : (step + 1) * height] for step in range(count)]


def coded(values):
    top = jnp.max(jnp.abs(values), axis=0, keepdims=True)
    power = jnp.ceil(jnp.log2(jnp.maximum(top, 1e-30)))
    return jnp.round(values * jnp.exp2(14.0 - power)).astype(jnp.int32), power.astype(jnp.int32)


def decoded(codes, power):
    return codes.astype(F32) * jnp.exp2(power.astype(F32) - 14.0)


def in_thirds(row):
    first = jnp.floor(row)
    second = jnp.floor((row - first) * 16384.0)
    third = jnp.round(((row - first) * 16384.0 - second) * 16384.0)
    return [part.astype(jnp.int32) for part in (first, second, third)]


def aggregate_hidden(projected, far, weight_t, tiles_t, degrees, plan, own, *rest):
    others, panels = rest[:-1], rest[-1]
    mine, opposite = panel_order(panels.shape[0] // 4, lax.axis_index("blk") % 2)
    for index, place in enumerate(mine):
        panels[place] = projected[index]
    for index, place in enumerate(opposite):
        panels[place] = nn(weight_t[...], far[index]).astype(BF16)
    sums = summed(panels, plan, tiles_t, 1 + len(others))
    own[...] = sums[0]
    row = lax.broadcasted_iota(jnp.int32, (ONES_ROWS, own.shape[1]), 0)
    for step, (part, out) in enumerate(zip(sums[1:], others), 1):
        codes, power = coded(part)
        terms = jnp.zeros(row.shape, jnp.int32)
        for index, term in enumerate([power, *in_thirds(degrees[step, :1])]):
            terms = jnp.where(row == index, term, terms)
        out[...] = jnp.concatenate([codes, terms], axis=0).astype(jnp.int16)


def aggregate_classes(near, far, tiles_t, plan, own, *rest):
    others, panels = rest[:-1], rest[-1]
    chip = lax.axis_index("blk") // 2
    for index in range(near.shape[0]):
        panels[2 * (index ^ chip)] = near[index]
        panels[2 * (index ^ chip) + 1] = far[index]
    sums = summed(panels, plan, tiles_t, 1 + len(others))
    own[...] = sums[0]
    row = lax.broadcasted_iota(jnp.int32, own.shape, 0)
    for part, out in zip(sums[1:], others):
        codes, power = coded(part)
        out[...] = jnp.where(row == own.shape[0] - 1, power, codes).astype(jnp.int16)


def combine(hidden_in, bias, weight_t, degrees, own, *rest):
    *arrived, out, scale_out = rest
    height = hidden_in.shape[1]
    total, degree = own[...], degrees[0, :1]
    for part in arrived:
        codes = part[...].astype(jnp.int32)
        total = total + decoded(codes[:height], codes[height : height + 1])
        terms = [codes[height + 1 + index : height + 2 + index].astype(F32) for index in range(3)]
        degree = degree + (terms[0] + (terms[1] + terms[2] * 2.0**-14) * 2.0**-14)
    scaling = lax.rsqrt(1.0 + degree)
    hidden = scaling * (total + hidden_in[0].astype(F32)) + bias[...]
    hidden = jnp.maximum(hidden, 0.0).astype(BF16)
    classes = nn(weight_t[...], hidden)
    blank = jnp.zeros((out.shape[0] - classes.shape[0], classes.shape[1]), F32)
    out[...] = jnp.concatenate([classes, blank], axis=0).astype(BF16)
    scale_out[...] = scaling


def finish(classes_in, scaling, bias, own, *rest):
    *arrived, out = rest
    classes = out.shape[0]
    total = own[...]
    for part in arrived:
        codes = part[...].astype(jnp.int32)
        total = total + decoded(codes, codes[-1:])
    whole = total + classes_in[...].astype(F32)
    out[...] = scaling[...] * whole[:classes] + bias[...]


def shifted(value, axis, step):
    size = lax.axis_size(axis)
    return lax.ppermute(value, axis, [((d + step) % size, d) for d in range(size)])


def swapped(value, masks):
    return lax.ppermute(value, "blk", [(d ^ masks[d % 2], d) for d in range(lax.axis_size("blk"))])


def outer_order(outer):
    rest = list(range(2, outer))
    return 1, list(zip(rest[0::2], rest[1::2]))


def two_ways(pairs):
    return pairs, [(pair[1], pair[0]) for pair in pairs]


def panel_order(outer, core):
    first, pairs = outer_order(outer)
    lists = []
    for here in (core, 1 - core):
        early, late = ([4 * jnp.where(here == 0, *sides) for sides in way] for way in two_ways(pairs))
        over = [apart + 2 for apart in [0, 4 * first, *early, *late]]
        lists.append([0, 4 * first, *late, *early, *over])
    return lists[0], [apart ^ 1 for apart in lists[1]]


def packed(*parts):
    def pack(*refs):
        for index in range(len(parts)):
            refs[-1][index] = refs[index][...]

    out = jax.ShapeDtypeStruct((len(parts), *parts[0].shape), BF16)
    return call(pack, [out], vmem=parts)[0]


def gather_features(value):
    outer = lax.axis_size("blk") // 4
    first, pairs = outer_order(outer)
    ahead = swapped(value, (4 * first, 4 * first))
    early, late = ([swapped(value, (4 * a, 4 * b)) for a, b in way] for way in two_ways(pairs))
    stacks = packed(value, ahead), packed(*early), packed(*late)
    over = [swapped(stack, (2, 2)) for stack in stacks]
    near = jnp.concatenate([stacks[0], stacks[2], stacks[1], *over])
    return near, swapped(near, (1, 1))


def gather_classes(value):
    size = lax.axis_size("blk")
    groups = [list(range(core, size, 2)) for core in range(2)]
    copies = jnp.broadcast_to(value[None], (size // 2, *value.shape))
    near = lax.all_to_all(copies, "blk", 0, 0, axis_index_groups=groups)
    return near, swapped(near, (1, 1))


def body(
    features,
    node_order,
    tile_values,
    tile_rows,
    tile_columns,
    tile_live,
    first_weight,
    first_bias,
    second_weight,
    second_bias,
):
    tile, width = features.shape
    slots = tile_values.shape[1]
    reps = lax.axis_size("rep")
    blocks = lax.axis_size("blk")
    hidden, classes = second_weight.shape
    padded = -(-(classes + 1) // 16) * 16
    shape = jax.ShapeDtypeStruct

    def exchanged(sums):
        return [shifted(sums[reps - 1 - step], "rep", step) for step in range(1, reps)]

    own_t = features.T
    others = [shifted(own_t, "rep", step) for step in range(1, reps)]
    plan, part, wanted, tiles, bias_1, bias_2, weight_1, weight_2 = call(
        functools.partial(prepare, reps),
        [
            pltpu.SMEM((2 * slots,), jnp.int32),
            shape((width, tile), F32),
            shape((1, tile), jnp.int32),
            shape(tile_values.shape[1:], BF16),
            shape((hidden, 1), F32),
            shape((classes, 1), F32),
            shape((hidden, width), BF16),
            shape((classes, hidden), BF16),
        ],
        smem=(tile_live,),
        hbm=(
            node_order,
            own_t,
            tile_values[0],
            tile_rows,
            tile_columns,
            first_bias[None],
            second_bias[None],
            first_weight,
            second_weight.T,
        ),
        scratch=[
            pltpu.VMEM(node_order.shape, jnp.int32),
            pltpu.VMEM(own_t.shape, BF16),
            pltpu.SMEM((1, slots), jnp.int32),
            pltpu.SMEM((1, slots), jnp.int32),
            pltpu.VMEM((1, hidden), F32),
            pltpu.VMEM((1, classes), F32),
            pltpu.VMEM(first_weight.shape, BF16),
            pltpu.SemaphoreType.DMA((9,)),
        ],
        smem_outs=1,
    )
    (ordered,) = call(arrange, [shape((width, tile), BF16)], vmem=(part, wanted, *others))
    near, far = gather_features(ordered)
    tiles_t, degrees = call(
        turn,
        [shape(tiles.shape, BF16), shape((reps, 8, tile), F32)],
        vmem=(tiles,),
        smem=(plan,),
    )
    (projected,) = call(
        project,
        [shape((near.shape[0], hidden, tile), BF16)],
        vmem=(weight_1, near),
    )
    own, *sums = call(
        aggregate_hidden,
        [shape((hidden, tile), F32)] + [shape((hidden + ONES_ROWS, tile), jnp.int16)] * (reps - 1),
        vmem=(projected, far, weight_1, tiles_t, degrees),
        smem=(plan,),
        scratch=[pltpu.VMEM((blocks, hidden, tile), BF16)],
    )
    classes_in, scaling = call(
        combine,
        [shape((padded, tile), BF16), shape((1, tile), F32)],
        vmem=(projected, bias_1, weight_2, degrees, own, *exchanged(sums)),
    )
    own, *sums = call(
        aggregate_classes,
        [shape((padded, tile), F32)] + [shape((padded, tile), jnp.int16)] * (reps - 1),
        vmem=(*gather_classes(classes_in), tiles_t),
        smem=(plan,),
        scratch=[pltpu.VMEM((blocks, padded, tile), BF16)],
    )
    (logits,) = call(
        finish,
        [shape((classes, tile), F32)],
        vmem=(classes_in, scaling, bias_2, own, *exchanged(sums)),
    )
    return logits.T


def solution(mesh):
    placed = (
        P(("blk", "rep"), None),
        P("blk", None),
        P(("blk", "rep"), None, None, None),
        P(("blk", "rep"), None),
        P(("blk", "rep"), None),
        P(("blk", "rep")),
        P(),
        P(),
        P(),
        P(),
    )
    return jax.shard_map(
        body, mesh=mesh, in_specs=placed, out_specs=P(("blk", "rep"), None), check_vma=False
    )
```

```python
import functools

import jax
import jax.numpy as jnp
from jax import lax
from jax.experimental import pallas as pl
from jax.experimental.pallas import tpu as pltpu
from jax.sharding import PartitionSpec as P

BF16 = jnp.bfloat16
F32 = jnp.float32
ONES_ROWS = 16
VMEM_LIMIT = 32 * 1024 * 1024


def nn(a, b):
    return lax.dot_general(a, b, (((1,), (0,)), ((), ())), preferred_element_type=F32)


def nt(a, b):
    return lax.dot_general(a, b, (((1,), (1,)), ((), ())), preferred_element_type=F32)


def in_smem(value):
    return value if value.size == 1 else pltpu.with_memory_space_constraint(value, pltpu.SMEM)


def call(kernel, outs, smem=(), vmem=(), hbm=(), scratch=(), smem_outs=0, cost=1 << 20):
    spaces = [pltpu.VMEM] * len(vmem) + [pltpu.SMEM] * len(smem) + [pltpu.HBM] * len(hbm)
    out_spaces = [pltpu.SMEM] * smem_outs + [pltpu.VMEM] * (len(outs) - smem_outs)
    return pl.pallas_call(
        kernel,
        out_shape=outs,
        in_specs=[pl.BlockSpec(memory_space=space) for space in spaces],
        out_specs=[pl.BlockSpec(memory_space=space) for space in out_spaces],
        scratch_shapes=scratch,
        compiler_params=pltpu.CompilerParams(vmem_limit_bytes=VMEM_LIMIT),
        cost_estimate=pl.CostEstimate(flops=cost, bytes_accessed=cost, transcendentals=0),
    )(*vmem, *[in_smem(value) for value in smem], *[pltpu.with_memory_space_constraint(value, pltpu.HBM) for value in hbm])


def fetched(sources, targets, sems):
    copies = [
        pltpu.make_async_copy(source, target, sems.at[index])
        for index, (source, target) in enumerate(zip(sources, targets))
    ]
    for copy in copies:
        copy.start()
    return copies


def picked(features, wanted, owner):
    tile = features.shape[1]
    source = lax.broadcasted_iota(jnp.int32, (tile, tile), 0) + owner * tile
    return nn(features[...], jnp.where(source == wanted, 1.0, 0.0).astype(BF16))


def prepare(reps, features, live, *refs):
    order, tiles, rows, columns, *sources = refs[:6]
    plan, part, wanted_out, tiles_out, bias_1, bias_2 = refs[6:12]
    order_in, rows_in, columns_in, row_1, row_2, sems = refs[12:]
    copies = fetched(
        (order, rows, columns, *sources, tiles),
        (order_in, rows_in, columns_in, row_1, row_2, tiles_out),
        sems,
    )
    for copy in copies[:5]:
        copy.wait()
    tile = features.shape[1]
    slots = rows_in.shape[1]
    blocks = lax.axis_size("blk")
    block, member = lax.axis_index("blk"), lax.axis_index("rep")
    wanted = order_in[:, pl.ds(pl.multiple_of(member * tile, tile), tile)]
    wanted_out[...] = wanted
    part[...] = picked(features, wanted, member)
    bias_1[...] = jnp.broadcast_to(row_1[...], (8, row_1.shape[1])).T[:, :1]
    bias_2[...] = jnp.broadcast_to(row_2[...], (8, row_2.shape[1])).T[:, :1]
    for slot in range(slots):
        plan[slot] = lax.clamp(0, columns_in[0, slot] // reps, blocks - 1) ^ block
        local = rows_in[0, slot] - block * reps
        step = lax.rem(local - member + reps, reps)
        plan[slots + slot] = jnp.where((slot < live[0]) & (local >= 0) & (local < reps), step, -1)
    copies[5].wait()


def arrange(part, wanted, *rest):
    *features, out = rest
    reps = len(features) + 1
    member = lax.axis_index("rep")
    total = part[...]
    for step in range(1, reps):
        owner = lax.rem(member + step, reps)
        total = total + picked(features[step - 1], wanted[...], owner)
    out[...] = total.astype(BF16)


def project(weight_t, stack, out):
    for index in range(stack.shape[0]):
        out[index] = nn(weight_t[...], stack[index]).astype(BF16)


def turn(tiles, weight, plan, tiles_t, degrees, weight_t):
    weight_t[...] = weight[...].astype(F32).T.astype(BF16)
    slots, tile = tiles.shape[0], tiles.shape[1]
    count = degrees.shape[0]
    total = jnp.zeros((count * ONES_ROWS, tile), F32)
    for slot in range(slots):
        values = tiles[slot]
        tiles_t[slot] = values.T
        ones = [
            jnp.full((ONES_ROWS, tile), (plan[slots + slot] == step).astype(F32), F32).astype(BF16)
            for step in range(count)
        ]
        total = total + nt(jnp.concatenate(ones, axis=0), values)
    for step in range(count):
        degrees[step] = total[step * ONES_ROWS : step * ONES_ROWS + 8]


def summed(panels, plan, tiles_t, count):
    slots, tile = tiles_t.shape[0], tiles_t.shape[1]
    height = panels.shape[1]
    total = jnp.zeros((count * height, tile), F32)
    for slot in range(slots):
        values = panels[plan[slot]]
        pieces = [
            values * (plan[slots + slot] == step).astype(F32).astype(BF16) for step in range(count)
        ]
        total = total + nn(jnp.concatenate(pieces, axis=0), tiles_t[slot])
    return [total[step * height : (step + 1) * height] for step in range(count)]


def coded(values):
    top = jnp.max(jnp.abs(values), axis=0, keepdims=True)
    power = jnp.ceil(jnp.log2(jnp.maximum(top, 1e-30)))
    return jnp.round(values * jnp.exp2(14.0 - power)).astype(jnp.int32), power.astype(jnp.int32)


def decoded(codes, power):
    return codes.astype(F32) * jnp.exp2(power.astype(F32) - 14.0)


def in_thirds(row):
    first = jnp.floor(row)
    second = jnp.floor((row - first) * 16384.0)
    third = jnp.round(((row - first) * 16384.0 - second) * 16384.0)
    return [part.astype(jnp.int32) for part in (first, second, third)]


def aggregate_hidden(projected, far, weight_t, tiles_t, degrees, plan, own, *rest):
    others, panels = rest[:-1], rest[-1]
    mine, opposite = panel_order(panels.shape[0] // 4, lax.axis_index("blk") % 2)
    for index, place in enumerate(mine):
        panels[place] = projected[index]
    for index, place in enumerate(opposite):
        panels[place] = nn(weight_t[...], far[index]).astype(BF16)
    sums = summed(panels, plan, tiles_t, 1 + len(others))
    own[...] = sums[0]
    row = lax.broadcasted_iota(jnp.int32, (ONES_ROWS, own.shape[1]), 0)
    for step, (part, out) in enumerate(zip(sums[1:], others), 1):
        codes, power = coded(part)
        terms = jnp.zeros(row.shape, jnp.int32)
        for index, term in enumerate([power, *in_thirds(degrees[step, :1])]):
            terms = jnp.where(row == index, term, terms)
        out[...] = jnp.concatenate([codes, terms], axis=0).astype(jnp.int16)


def aggregate_classes(near, far, tiles_t, plan, own, *rest):
    others, panels = rest[:-1], rest[-1]
    chip = lax.axis_index("blk") // 2
    for index in range(near.shape[0]):
        panels[2 * (index ^ chip)] = near[index]
        panels[2 * (index ^ chip) + 1] = far[index]
    sums = summed(panels, plan, tiles_t, 1 + len(others))
    own[...] = sums[0]
    row = lax.broadcasted_iota(jnp.int32, own.shape, 0)
    for part, out in zip(sums[1:], others):
        codes, power = coded(part)
        out[...] = jnp.where(row == own.shape[0] - 1, power, codes).astype(jnp.int16)


def combine(hidden_in, bias, weight_t, degrees, own, *rest):
    *arrived, out, scale_out = rest
    height = hidden_in.shape[1]
    total, degree = own[...], degrees[0, :1]
    for part in arrived:
        codes = part[...].astype(jnp.int32)
        total = total + decoded(codes[:height], codes[height : height + 1])
        terms = [codes[height + 1 + index : height + 2 + index].astype(F32) for index in range(3)]
        degree = degree + (terms[0] + (terms[1] + terms[2] * 2.0**-14) * 2.0**-14)
    scaling = lax.rsqrt(1.0 + degree)
    hidden = scaling * (total + hidden_in[0].astype(F32)) + bias[...]
    hidden = jnp.maximum(hidden, 0.0).astype(BF16)
    classes = nn(weight_t[...], hidden)
    blank = jnp.zeros((out.shape[0] - classes.shape[0], classes.shape[1]), F32)
    out[...] = jnp.concatenate([classes, blank], axis=0).astype(BF16)
    scale_out[...] = scaling


def finish(classes_in, scaling, bias, own, *rest):
    *arrived, out = rest
    classes = out.shape[0]
    total = own[...]
    for part in arrived:
        codes = part[...].astype(jnp.int32)
        total = total + decoded(codes, codes[-1:])
    whole = total + classes_in[...].astype(F32)
    out[...] = scaling[...] * whole[:classes] + bias[...]


def shifted(value, axis, step):
    size = lax.axis_size(axis)
    return lax.ppermute(value, axis, [((d + step) % size, d) for d in range(size)])


def swapped(value, masks):
    return lax.ppermute(value, "blk", [(d ^ masks[d % 2], d) for d in range(lax.axis_size("blk"))])


def outer_order(outer):
    rest = list(range(2, outer))
    return 1, list(zip(rest[0::2], rest[1::2]))


def two_ways(pairs):
    return pairs, [(pair[1], pair[0]) for pair in pairs]


def panel_order(outer, core):
    first, pairs = outer_order(outer)
    lists = []
    for here in (core, 1 - core):
        early, late = ([4 * jnp.where(here == 0, *sides) for sides in way] for way in two_ways(pairs))
        over = [apart + 2 for apart in [0, 4 * first, *early, *late]]
        lists.append([0, 4 * first, *late, *early, *over])
    return lists[0], [apart ^ 1 for apart in lists[1]]


def packed(*parts):
    def pack(*refs):
        for index in range(len(parts)):
            refs[-1][index] = refs[index][...]

    out = jax.ShapeDtypeStruct((len(parts), *parts[0].shape), BF16)
    return call(pack, [out], vmem=parts)[0]


def gather_features(value):
    outer = lax.axis_size("blk") // 4
    first, pairs = outer_order(outer)
    ahead = swapped(value, (4 * first, 4 * first))
    early, late = ([swapped(value, (4 * a, 4 * b)) for a, b in way] for way in two_ways(pairs))
    stacks = packed(value, ahead), packed(*early), packed(*late)
    over = [swapped(stack, (2, 2)) for stack in stacks]
    near = jnp.concatenate([stacks[0], stacks[2], stacks[1], *over])
    return near, swapped(near, (1, 1))


def gather_classes(value):
    size = lax.axis_size("blk")
    groups = [list(range(core, size, 2)) for core in range(2)]
    copies = jnp.broadcast_to(value[None], (size // 2, *value.shape))
    near = lax.all_to_all(copies, "blk", 0, 0, axis_index_groups=groups)
    return near, swapped(near, (1, 1))


def body(
    features,
    node_order,
    tile_values,
    tile_rows,
    tile_columns,
    tile_live,
    first_weight,
    first_bias,
    second_weight,
    second_bias,
):
    tile, width = features.shape
    slots = tile_values.shape[1]
    reps = lax.axis_size("rep")
    blocks = lax.axis_size("blk")
    hidden, classes = second_weight.shape
    padded = -(-(classes + 1) // 16) * 16
    shape = jax.ShapeDtypeStruct

    def exchanged(sums):
        return [shifted(sums[reps - 1 - step], "rep", step) for step in range(1, reps)]

    own_t = features.T
    others = [shifted(own_t, "rep", step) for step in range(1, reps)]
    plan, part, wanted, tiles, bias_1, bias_2 = call(
        functools.partial(prepare, reps),
        [
            pltpu.SMEM((2 * slots,), jnp.int32),
            shape((width, tile), F32),
            shape((1, tile), jnp.int32),
            shape(tile_values.shape[1:], BF16),
            shape((hidden, 1), F32),
            shape((classes, 1), F32),
        ],
        vmem=(own_t,),
        smem=(tile_live,),
        hbm=(
            node_order,
            tile_values[0],
            tile_rows,
            tile_columns,
            first_bias[None],
            second_bias[None],
        ),
        scratch=[
            pltpu.VMEM(node_order.shape, jnp.int32),
            pltpu.SMEM((1, slots), jnp.int32),
            pltpu.SMEM((1, slots), jnp.int32),
            pltpu.VMEM((1, hidden), F32),
            pltpu.VMEM((1, classes), F32),
            pltpu.SemaphoreType.DMA((6,)),
        ],
        smem_outs=1,
    )
    (ordered,) = call(arrange, [shape((width, tile), BF16)], vmem=(part, wanted, *others))
    near, far = gather_features(ordered)
    tiles_t, degrees, weight_1 = call(
        turn,
        [shape(tiles.shape, BF16), shape((reps, 8, tile), F32), shape((hidden, width), BF16)],
        vmem=(tiles, first_weight),
        smem=(plan,),
    )
    (projected,) = call(
        project,
        [shape((near.shape[0], hidden, tile), BF16)],
        vmem=(weight_1, near),
    )
    own, *sums = call(
        aggregate_hidden,
        [shape((hidden, tile), F32)] + [shape((hidden + ONES_ROWS, tile), jnp.int16)] * (reps - 1),
        vmem=(projected, far, weight_1, tiles_t, degrees),
        smem=(plan,),
        scratch=[pltpu.VMEM((blocks, hidden, tile), BF16)],
    )
    classes_in, scaling = call(
        combine,
        [shape((padded, tile), BF16), shape((1, tile), F32)],
        vmem=(projected, bias_1, second_weight.T, degrees, own, *exchanged(sums)),
    )
    own, *sums = call(
        aggregate_classes,
        [shape((padded, tile), F32)] + [shape((padded, tile), jnp.int16)] * (reps - 1),
        vmem=(*gather_classes(classes_in), tiles_t),
        smem=(plan,),
        scratch=[pltpu.VMEM((blocks, padded, tile), BF16)],
    )
    (logits,) = call(
        finish,
        [shape((classes, tile), F32)],
        vmem=(classes_in, scaling, bias_2, own, *exchanged(sums)),
    )
    return logits.T


def solution(mesh):
    placed = (
        P(("blk", "rep"), None),
        P("blk", None),
        P(("blk", "rep"), None, None, None),
        P(("blk", "rep"), None),
        P(("blk", "rep"), None),
        P(("blk", "rep")),
        P(),
        P(),
        P(),
        P(),
    )
    return jax.shard_map(
        body, mesh=mesh, in_specs=placed, out_specs=P(("blk", "rep"), None), check_vma=False
    )
```

```python
import functools

import jax
import jax.numpy as jnp
from jax import lax
from jax.experimental import pallas as pl
from jax.experimental.pallas import tpu as pltpu
from jax.sharding import PartitionSpec as P

BF16 = jnp.bfloat16
F32 = jnp.float32
ONES_ROWS = 16
VMEM_LIMIT = 32 * 1024 * 1024


def nn(a, b):
    return lax.dot_general(a, b, (((1,), (0,)), ((), ())), preferred_element_type=F32)


def nt(a, b):
    return lax.dot_general(a, b, (((1,), (1,)), ((), ())), preferred_element_type=F32)


def in_smem(value):
    return value if value.size == 1 else pltpu.with_memory_space_constraint(value, pltpu.SMEM)


def call(kernel, outs, smem=(), vmem=(), hbm=(), scratch=(), smem_outs=0, cost=1 << 20):
    spaces = [pltpu.VMEM] * len(vmem) + [pltpu.SMEM] * len(smem) + [pltpu.HBM] * len(hbm)
    out_spaces = [pltpu.SMEM] * smem_outs + [pltpu.VMEM] * (len(outs) - smem_outs)
    return pl.pallas_call(
        kernel,
        out_shape=outs,
        in_specs=[pl.BlockSpec(memory_space=space) for space in spaces],
        out_specs=[pl.BlockSpec(memory_space=space) for space in out_spaces],
        scratch_shapes=scratch,
        compiler_params=pltpu.CompilerParams(vmem_limit_bytes=VMEM_LIMIT),
        cost_estimate=pl.CostEstimate(flops=cost, bytes_accessed=cost, transcendentals=0),
    )(*vmem, *[in_smem(value) for value in smem], *[pltpu.with_memory_space_constraint(value, pltpu.HBM) for value in hbm])


def fetched(sources, targets, sems):
    copies = [
        pltpu.make_async_copy(source, target, sems.at[index])
        for index, (source, target) in enumerate(zip(sources, targets))
    ]
    for copy in copies:
        copy.start()
    return copies


def picked(features, wanted, owner):
    tile = features.shape[1]
    source = lax.broadcasted_iota(jnp.int32, (tile, tile), 0) + owner * tile
    return nn(features[...], jnp.where(source == wanted, 1.0, 0.0).astype(BF16))


def prepare(reps, live, *refs):
    order, features, tiles, rows, columns, *sources = refs[:9]
    plan, part, wanted_out, tiles_out, bias_1, bias_2, weight_1, weight_2 = refs[9:17]
    order_in, features_in, rows_in, columns_in, row_1, row_2, weight_in, sems = refs[17:]
    copies = fetched(
        (order, features, rows, columns, *sources, tiles),
        (order_in, features_in, rows_in, columns_in, row_1, row_2, weight_in, weight_2, tiles_out),
        sems,
    )
    for copy in copies[:7]:
        copy.wait()
    tile = features.shape[1]
    slots = rows_in.shape[1]
    blocks = lax.axis_size("blk")
    block, member = lax.axis_index("blk"), lax.axis_index("rep")
    wanted = order_in[:, pl.ds(pl.multiple_of(member * tile, tile), tile)]
    wanted_out[...] = wanted
    part[...] = picked(features_in, wanted, member)
    bias_1[...] = jnp.broadcast_to(row_1[...], (8, row_1.shape[1])).T[:, :1]
    bias_2[...] = jnp.broadcast_to(row_2[...], (8, row_2.shape[1])).T[:, :1]
    weight_1[...] = weight_in[...].astype(F32).T.astype(BF16)
    for slot in range(slots):
        plan[slot] = lax.clamp(0, columns_in[0, slot] // reps, blocks - 1) ^ block
        local = rows_in[0, slot] - block * reps
        step = lax.rem(local - member + reps, reps)
        plan[slots + slot] = jnp.where((slot < live[0]) & (local >= 0) & (local < reps), step, -1)
    for copy in copies[7:]:
        copy.wait()


def arrange(part, wanted, *rest):
    *features, out = rest
    reps = len(features) + 1
    member = lax.axis_index("rep")
    total = part[...]
    for step in range(1, reps):
        owner = lax.rem(member + step, reps)
        total = total + picked(features[step - 1], wanted[...], owner)
    out[...] = total.astype(BF16)


def project(weight_t, stack, out):
    for index in range(stack.shape[0]):
        out[index] = nn(weight_t[...], stack[index]).astype(BF16)


def turn(tiles, plan, tiles_t, degrees):
    slots, tile = tiles.shape[0], tiles.shape[1]
    count = degrees.shape[0]
    total = jnp.zeros((count * ONES_ROWS, tile), F32)
    for slot in range(slots):
        values = tiles[slot]
        tiles_t[slot] = values.T
        ones = [
            jnp.full((ONES_ROWS, tile), (plan[slots + slot] == step).astype(F32), F32).astype(BF16)
            for step in range(count)
        ]
        total = total + nt(jnp.concatenate(ones, axis=0), values)
    for step in range(count):
        degrees[step] = total[step * ONES_ROWS : step * ONES_ROWS + 8]


def summed(panels, plan, tiles_t, count):
    slots, tile = tiles_t.shape[0], tiles_t.shape[1]
    height = panels.shape[1]
    total = jnp.zeros((count * height, tile), F32)
    for slot in range(slots):
        values = panels[plan[slot]]
        pieces = [
            values * (plan[slots + slot] == step).astype(F32).astype(BF16) for step in range(count)
        ]
        total = total + nn(jnp.concatenate(pieces, axis=0), tiles_t[slot])
    return [total[step * height : (step + 1) * height] for step in range(count)]


def coded(values):
    top = jnp.max(jnp.abs(values), axis=0, keepdims=True)
    power = jnp.ceil(jnp.log2(jnp.maximum(top, 1e-30)))
    return jnp.round(values * jnp.exp2(14.0 - power)).astype(jnp.int32), power.astype(jnp.int32)


def decoded(codes, power):
    return codes.astype(F32) * jnp.exp2(power.astype(F32) - 14.0)


def in_thirds(row):
    first = jnp.floor(row)
    second = jnp.floor((row - first) * 16384.0)
    third = jnp.round(((row - first) * 16384.0 - second) * 16384.0)
    return [part.astype(jnp.int32) for part in (first, second, third)]


def aggregate_hidden(projected, far, weight_t, tiles_t, degrees, plan, own, *rest):
    others, panels = rest[:-1], rest[-1]
    mine, opposite = panel_order(panels.shape[0] // 4, lax.axis_index("blk") % 2)
    for index, place in enumerate(mine):
        panels[place] = projected[index]
    for index, place in enumerate(opposite):
        panels[place] = nn(weight_t[...], far[index]).astype(BF16)
    sums = summed(panels, plan, tiles_t, 1 + len(others))
    own[...] = sums[0]
    row = lax.broadcasted_iota(jnp.int32, (ONES_ROWS, own.shape[1]), 0)
    for step, (part, out) in enumerate(zip(sums[1:], others), 1):
        codes, power = coded(part)
        terms = jnp.zeros(row.shape, jnp.int32)
        for index, term in enumerate([power, *in_thirds(degrees[step, :1])]):
            terms = jnp.where(row == index, term, terms)
        out[...] = jnp.concatenate([codes, terms], axis=0).astype(jnp.int16)


def aggregate_classes(near, far, tiles_t, plan, own, *rest):
    others, panels = rest[:-1], rest[-1]
    chip = lax.axis_index("blk") // 2
    for index in range(near.shape[0]):
        panels[2 * (index ^ chip)] = near[index]
        panels[2 * (index ^ chip) + 1] = far[index]
    sums = summed(panels, plan, tiles_t, 1 + len(others))
    own[...] = sums[0]
    row = lax.broadcasted_iota(jnp.int32, own.shape, 0)
    for part, out in zip(sums[1:], others):
        codes, power = coded(part)
        out[...] = jnp.where(row == own.shape[0] - 1, power, codes).astype(jnp.int16)


def combine(hidden_in, bias, weight_t, degrees, own, *rest):
    *arrived, out, scale_out = rest
    height = hidden_in.shape[1]
    total, degree = own[...], degrees[0, :1]
    for part in arrived:
        codes = part[...].astype(jnp.int32)
        total = total + decoded(codes[:height], codes[height : height + 1])
        terms = [codes[height + 1 + index : height + 2 + index].astype(F32) for index in range(3)]
        degree = degree + (terms[0] + (terms[1] + terms[2] * 2.0**-14) * 2.0**-14)
    scaling = lax.rsqrt(1.0 + degree)
    hidden = scaling * (total + hidden_in[0].astype(F32)) + bias[...]
    hidden = jnp.maximum(hidden, 0.0).astype(BF16)
    classes = nn(weight_t[...], hidden)
    blank = jnp.zeros((out.shape[0] - classes.shape[0], classes.shape[1]), F32)
    out[...] = jnp.concatenate([classes, blank], axis=0).astype(BF16)
    scale_out[...] = scaling


def finish(classes_in, scaling, bias, own, *rest):
    *arrived, out = rest
    classes = out.shape[0]
    total = own[...]
    for part in arrived:
        codes = part[...].astype(jnp.int32)
        total = total + decoded(codes, codes[-1:])
    whole = total + classes_in[...].astype(F32)
    out[...] = scaling[...] * whole[:classes] + bias[...]


def shifted(value, axis, step):
    size = lax.axis_size(axis)
    return lax.ppermute(value, axis, [((d + step) % size, d) for d in range(size)])


def swapped(value, masks):
    return lax.ppermute(value, "blk", [(d ^ masks[d % 2], d) for d in range(lax.axis_size("blk"))])


def outer_order(outer):
    rest = list(range(2, outer))
    return 1, list(zip(rest[0::2], rest[1::2]))


def two_ways(pairs):
    return pairs, [(pair[1], pair[0]) for pair in pairs]


def panel_order(outer, core):
    first, pairs = outer_order(outer)
    lists = []
    for here in (core, 1 - core):
        early, late = ([4 * jnp.where(here == 0, *sides) for sides in way] for way in two_ways(pairs))
        over = [apart + 2 for apart in [0, 4 * first, *early, *late]]
        lists.append([0, 4 * first, *early, *late, *over])
    return lists[0], [apart ^ 1 for apart in lists[1]]


def packed(*parts):
    def pack(*refs):
        for index in range(len(parts)):
            refs[-1][index] = refs[index][...]

    out = jax.ShapeDtypeStruct((len(parts), *parts[0].shape), BF16)
    return call(pack, [out], vmem=parts)[0]


def gather_features(value):
    outer = lax.axis_size("blk") // 4
    first, pairs = outer_order(outer)
    ahead = swapped(value, (4 * first, 4 * first))
    early, late = ([swapped(value, (4 * a, 4 * b)) for a, b in way] for way in two_ways(pairs))
    stacks = packed(value, ahead), packed(*early), packed(*late)
    over = [swapped(stack, (2, 2)) for stack in stacks]
    near = jnp.concatenate([*stacks, *over])
    return near, swapped(near, (1, 1))


def gather_classes(value):
    size = lax.axis_size("blk")
    groups = [list(range(core, size, 2)) for core in range(2)]
    copies = jnp.broadcast_to(value[None], (size // 2, *value.shape))
    near = lax.all_to_all(copies, "blk", 0, 0, axis_index_groups=groups)
    return near, swapped(near, (1, 1))


def body(
    features,
    node_order,
    tile_values,
    tile_rows,
    tile_columns,
    tile_live,
    first_weight,
    first_bias,
    second_weight,
    second_bias,
):
    tile, width = features.shape
    slots = tile_values.shape[1]
    reps = lax.axis_size("rep")
    blocks = lax.axis_size("blk")
    hidden, classes = second_weight.shape
    padded = -(-(classes + 1) // 16) * 16
    shape = jax.ShapeDtypeStruct

    def exchanged(sums):
        return [shifted(sums[reps - 1 - step], "rep", step) for step in range(1, reps)]

    own_t = features.T
    others = [shifted(own_t, "rep", step) for step in range(1, reps)]
    plan, part, wanted, tiles, bias_1, bias_2, weight_1, weight_2 = call(
        functools.partial(prepare, reps),
        [
            pltpu.SMEM((2 * slots,), jnp.int32),
            shape((width, tile), F32),
            shape((1, tile), jnp.int32),
            shape(tile_values.shape[1:], BF16),
            shape((hidden, 1), F32),
            shape((classes, 1), F32),
            shape((hidden, width), BF16),
            shape((classes, hidden), BF16),
        ],
        smem=(tile_live,),
        hbm=(
            node_order,
            own_t,
            tile_values[0],
            tile_rows,
            tile_columns,
            first_bias[None],
            second_bias[None],
            first_weight,
            second_weight.T,
        ),
        scratch=[
            pltpu.VMEM(node_order.shape, jnp.int32),
            pltpu.VMEM(own_t.shape, BF16),
            pltpu.SMEM((1, slots), jnp.int32),
            pltpu.SMEM((1, slots), jnp.int32),
            pltpu.VMEM((1, hidden), F32),
            pltpu.VMEM((1, classes), F32),
            pltpu.VMEM(first_weight.shape, BF16),
            pltpu.SemaphoreType.DMA((9,)),
        ],
        smem_outs=1,
    )
    (ordered,) = call(arrange, [shape((width, tile), BF16)], vmem=(part, wanted, *others))
    near, far = gather_features(ordered)
    tiles_t, degrees = call(
        turn,
        [shape(tiles.shape, BF16), shape((reps, 8, tile), F32)],
        vmem=(tiles,),
        smem=(plan,),
    )
    (projected,) = call(
        project,
        [shape((near.shape[0], hidden, tile), BF16)],
        vmem=(weight_1, near),
    )
    own, *sums = call(
        aggregate_hidden,
        [shape((hidden, tile), F32)] + [shape((hidden + ONES_ROWS, tile), jnp.int16)] * (reps - 1),
        vmem=(projected, far, weight_1, tiles_t, degrees),
        smem=(plan,),
        scratch=[pltpu.VMEM((blocks, hidden, tile), BF16)],
    )
    classes_in, scaling = call(
        combine,
        [shape((padded, tile), BF16), shape((1, tile), F32)],
        vmem=(projected, bias_1, weight_2, degrees, own, *exchanged(sums)),
    )
    own, *sums = call(
        aggregate_classes,
        [shape((padded, tile), F32)] + [shape((padded, tile), jnp.int16)] * (reps - 1),
        vmem=(*gather_classes(classes_in), tiles_t),
        smem=(plan,),
        scratch=[pltpu.VMEM((blocks, padded, tile), BF16)],
    )
    (logits,) = call(
        finish,
        [shape((classes, tile), F32)],
        vmem=(classes_in, scaling, bias_2, own, *exchanged(sums)),
    )
    return logits.T


def solution(mesh):
    placed = (
        P(("blk", "rep"), None),
        P("blk", None),
        P(("blk", "rep"), None, None, None),
        P(("blk", "rep"), None),
        P(("blk", "rep"), None),
        P(("blk", "rep")),
        P(),
        P(),
        P(),
        P(),
    )
    return jax.shard_map(
        body, mesh=mesh, in_specs=placed, out_specs=P(("blk", "rep"), None), check_vma=False
    )
```
